32 devices in a mesh: dp: 8 (over z, y), mp: 4 (over x, core).
Axes of the slice: x: 2, y: 2, z: 4, core: 2. Of those that a mesh axis runs over, the one named last changes fastest.
Arguments:
- hidden_rows: bfloat16 [16384, 768], P(('dp', 'mp')), may hold values from -6 to 6
- token_table: bfloat16 [4096, 768], replicated, may hold values from -6 to 6
- masked_positions: int32 [128, 32], P(('dp', 'mp')), may hold values from 0 to 127, as said below
- masked_counts: int32 [128], P(('dp', 'mp')), may hold values from 6 to 32, as said below
- replace_rows: int32 [128, 32], P(('dp', 'mp')), may hold values from 0 to 4095
- masked_cotangent: bfloat16 [128, 32, 768], P(('dp', 'mp')), may hold values from -6 to 6
- step_number: int32 [1], replicated, may hold values from 2 to 20
- attend_master: float32 [768, 2304], P('dp', 'mp'), may hold values from -0.21875 to 0.21875
- merge_master: float32 [768, 768], P('dp', 'mp'), may hold values from -0.625 to 0.625
- norms_master: float32 [4, 768], P('mp', 'dp'), may hold values from 0.5 to 1.5
- gate_master: float32 [768, 3072], P('dp', 'mp'), may hold values from -0.21875 to 0.21875
- value_master: float32 [768, 3072], P('dp', 'mp'), may hold values from -0.21875 to 0.21875
- down_master: float32 [3072, 768], P('mp', 'dp'), may hold values from -0.109375 to 0.109375
- first_attend: float32 [768, 2304], P('dp', 'mp'), may hold values from -24 to 24
- first_merge: float32 [768, 768], P('dp', 'mp'), may hold values from -14 to 14
- first_norms: float32 [4, 768], P('mp', 'dp'), may hold values from -32 to 32
- first_gate: float32 [768, 3072], P('dp', 'mp'), may hold values from -20 to 20
- first_value: float32 [768, 3072], P('dp', 'mp'), may hold values from -14 to 14
- first_down: float32 [3072, 768], P('mp', 'dp'), may hold values from -28 to 28
- second_attend: float32 [768, 2304], P('dp', 'mp'), may hold values from 1.032192 to 8.84736
- second_merge: float32 [768, 768], P('dp', 'mp'), may hold values from 0.262144 to 2.21184
- second_norms: float32 [4, 768], P('mp', 'dp'), may hold values from 1.572864 to 13.43488
- second_gate: float32 [768, 3072], P('dp', 'mp'), may hold values from 0.606208 to 5.24288
- second_value: float32 [768, 3072], P('dp', 'mp'), may hold values from 0.278528 to 2.359296
- second_down: float32 [3072, 768], P('mp', 'dp'), may hold values from 1.097728 to 9.50272
Outputs:
- layer_output: bfloat16 [16384, 768], P(('dp', 'mp'))
- input_gradient: float32 [16384, 768], P(('dp', 'mp'))
- gradient_attend: float32 [768, 2304], P('dp', 'mp')
- gradient_merge: float32 [768, 768], P('dp', 'mp')
- gradient_norms: float32 [4, 768], P('mp', 'dp')
- gradient_gate: float32 [768, 3072], P('dp', 'mp')
- gradient_value: float32 [768, 3072], P('dp', 'mp')
- gradient_down: float32 [3072, 768], P('mp', 'dp')
- moment_attend: float32 [768, 2304], P('dp', 'mp')
- moment_merge: float32 [768, 768], P('dp', 'mp')
- moment_norms: float32 [4, 768], P('mp', 'dp')
- moment_gate: float32 [768, 3072], P('dp', 'mp')
- moment_value: float32 [768, 3072], P('dp', 'mp')
- moment_down: float32 [3072, 768], P('mp', 'dp')
- squares_attend: float32 [768, 2304], P('dp', 'mp')
- squares_merge: float32 [768, 768], P('dp', 'mp')
- squares_norms: float32 [4, 768], P('mp', 'dp')
- squares_gate: float32 [768, 3072], P('dp', 'mp')
- squares_value: float32 [768, 3072], P('dp', 'mp')
- squares_down: float32 [3072, 768], P('mp', 'dp')
- updated_attend: float32 [768, 2304], P('dp', 'mp')
- updated_merge: float32 [768, 768], P('dp', 'mp')
- updated_norms: float32 [4, 768], P('mp', 'dp')
- updated_gate: float32 [768, 3072], P('dp', 'mp')
- updated_value: float32 [768, 3072], P('dp', 'mp')
- updated_down: float32 [3072, 768], P('mp', 'dp')
The draws below stay inside these ranges and needn't reach their ends.
Inputs may be any that keep to these rules, and one draw needn't show every extreme that they name: `masked_positions`: each row holds 32 different positions. Slots masked_counts[n] and later of sequence n are not live and are ignored, together with their replace_rows and masked_cotangent entries. Some sequence has exactly 32 live slots and some exactly the least value.
All inputs are finite; a program needn't handle non-finite values.
Results may differ from the reference program's by a relative error of at most 0.013.
The reference program's roundings to bfloat16 on the way count: a program that leaves them out, or rounds other values in their place, can miss the bound.
Values may be sent and summed in bfloat16 or wider, within the bound.
No kernel may reach another device: no remote copies, remote signals or barrier semaphores. Data moves between devices by JAX's collectives and lax.ppermute only.
A program may use at most 192 MiB of HBM per device.

```python
import math
import jax
import jax.numpy as jnp
from jax import lax

D = 768
HEADS = 12
HEAD_DIM = 64
FF = 3072
VOCAB = 4096
SEQ_LEN = 128
SEQ_DEV = 4
MASK_SLOTS = 32
SEQS = 128
TOKENS = 16384
N_DP = 8
N_MP = 4


def draw_masked_positions(key, part):
    subkeys = jax.random.split(key, SEQS)
    return jax.vmap(lambda subkey: jax.random.permutation(subkey, SEQ_LEN)[:MASK_SLOTS])(subkeys).astype(jnp.int32)


def draw_masked_counts(key, part):
    lowest = max(1, MASK_SLOTS // 5)
    counts = jax.random.randint(jax.random.fold_in(key, 11), (SEQS,), lowest, MASK_SLOTS + 1)
    fullest = jax.random.randint(jax.random.fold_in(key, 12), (), 0, SEQS)
    position = jnp.arange(SEQS)
    counts = jnp.where(position == fullest, MASK_SLOTS, counts)
    counts = jnp.where(position == (fullest + 1) % SEQS, lowest, counts)
    return counts.astype(jnp.int32)


def place_ends(values, key, least, largest):
    dims = values.shape
    spot = [jax.random.randint(jax.random.fold_in(key, axis), (), 0, dims[axis]) for axis in range(len(dims))]
    values = values.at[tuple(spot)].set(least)
    longest = dims.index(max(dims))
    spot[longest] = (spot[longest] + 1) % dims[longest]
    return values.at[tuple(spot)].set(largest)


def steps_of(own_key, dims, cuts, low, high):
    gain = 1.0
    for axis_at, blocks in cuts:
        steps = jax.random.uniform(jax.random.fold_in(jax.random.fold_in(own_key, 6), axis_at), (blocks,), jnp.float32, low / len(cuts), high / len(cuts))
        gain = gain * jnp.repeat(jnp.exp(steps), dims[axis_at] // blocks).reshape((-1,) + (1,) * (len(dims) - 1 - axis_at))
    return gain


def noise(own_key, extent, scale, limit, cuts=(), held_as=jnp.bfloat16):
    array = jax.random.normal(own_key, extent, jnp.float32) * scale
    if len(cuts) > 0:
        array = steps_of(own_key, extent, cuts, -0.22, 0.18) * array
    return jnp.clip(array, min=-limit, max=limit).astype(held_as)


def setup_inputs(seed: int = 0) -> dict:
    seeds = jax.random.split(jax.random.key(seed), 26)
    hidden_rows = noise(seeds[0], (TOKENS, D), 1.0, 6.0, ((0, 32),))
    token_table = noise(seeds[1], (VOCAB, D), 1.0, 6.0)
    masked_positions = draw_masked_positions(jax.random.fold_in(seeds[25], 71), 0)
    masked_counts = draw_masked_counts(jax.random.fold_in(seeds[25], 71), 0)
    replace_rows = place_ends(jax.random.randint(seeds[4], (SEQS, MASK_SLOTS), 0, VOCAB), jax.random.fold_in(seeds[4], 1), 0, VOCAB - 1).astype(jnp.int32)
    masked_cotangent = noise(seeds[5], (SEQS, MASK_SLOTS, D), 1.0, 6.0, ((0, 32),))
    step_number = jax.random.randint(seeds[6], (1,), 2, 21).astype(jnp.int32)
    attend_master = noise(seeds[7], (D, 3 * D), D ** -0.5, 0.21875, ((0, 8), (1, 4)), jnp.float32)
    merge_master = noise(seeds[8], (D, D), (D // 8) ** -0.5, 0.625, ((0, 8), (1, 4)), jnp.float32)
    norms_master = jnp.clip(1.0 + 0.1 * jax.random.normal(seeds[9], (4, D), jnp.float32), 0.5, 1.5)
    gate_master = noise(seeds[10], (D, FF), D ** -0.5, 0.21875, ((0, 8), (1, 4)), jnp.float32)
    value_master = noise(seeds[11], (D, FF), D ** -0.5, 0.21875, ((0, 8), (1, 4)), jnp.float32)
    down_master = noise(seeds[12], (FF, D), FF ** -0.5, 0.109375, ((0, 4), (1, 8)), jnp.float32)
    first_attend = noise(seeds[13], (D, 3 * D), (0.033 * TOKENS ** 0.5), 24.0, ((0, 8), (1, 4)), jnp.float32)
    first_merge = noise(seeds[14], (D, D), (0.017 * TOKENS ** 0.5), 14.0, ((0, 8), (1, 4)), jnp.float32)
    first_norms = noise(seeds[15], (4, D), (0.041 * TOKENS ** 0.5), 32.0, ((0, 4), (1, 8)), jnp.float32)
    first_gate = noise(seeds[16], (D, FF), (0.026 * TOKENS ** 0.5), 20.0, ((0, 8), (1, 4)), jnp.float32)
    first_value = noise(seeds[17], (D, FF), (0.017 * TOKENS ** 0.5), 14.0, ((0, 8), (1, 4)), jnp.float32)
    first_down = noise(seeds[18], (FF, D), (0.034 * TOKENS ** 0.5), 28.0, ((0, 4), (1, 8)), jnp.float32)
    second_attend = jnp.clip(jnp.exp(math.log(8.84736) - 2.1484344 * jax.random.uniform(seeds[19], (D, 3 * D), jnp.float32) ** steps_of(seeds[19], (D, 3 * D), ((0, 8), (1, 4)), -0.2, 0.2)), 1.032192, 8.84736)
    second_merge = jnp.clip(jnp.exp(math.log(2.21184) - 2.13268602 * jax.random.uniform(seeds[20], (D, D), jnp.float32) ** steps_of(seeds[20], (D, D), ((0, 8), (1, 4)), -0.2, 0.2)), 0.262144, 2.21184)
    second_norms = jnp.clip(jnp.exp(math.log(13.43488) - 2.144956 * jax.random.uniform(seeds[21], (4, D), jnp.float32) ** steps_of(seeds[21], (4, D), ((0, 4), (1, 8)), -0.2, 0.2)), 1.572864, 13.43488)
    second_gate = jnp.clip(jnp.exp(math.log(5.24288) - 2.157403 * jax.random.uniform(seeds[22], (D, FF), jnp.float32) ** steps_of(seeds[22], (D, FF), ((0, 8), (1, 4)), -0.2, 0.2)), 0.606208, 5.24288)
    second_value = jnp.clip(jnp.exp(math.log(2.359296) - 2.1366 * jax.random.uniform(seeds[23], (D, FF), jnp.float32) ** steps_of(seeds[23], (D, FF), ((0, 8), (1, 4)), -0.2, 0.2)), 0.278528, 2.359296)
    second_down = jnp.clip(jnp.exp(math.log(9.50272) - 2.1583355 * jax.random.uniform(seeds[24], (FF, D), jnp.float32) ** steps_of(seeds[24], (FF, D), ((0, 4), (1, 8)), -0.2, 0.2)), 1.097728, 9.50272)
    return {"hidden_rows": hidden_rows, "token_table": token_table, "masked_positions": masked_positions, "masked_counts": masked_counts, "replace_rows": replace_rows, "masked_cotangent": masked_cotangent, "step_number": step_number, "attend_master": attend_master, "merge_master": merge_master, "norms_master": norms_master, "gate_master": gate_master, "value_master": value_master, "down_master": down_master, "first_attend": first_attend, "first_merge": first_merge, "first_norms": first_norms, "first_gate": first_gate, "first_value": first_value, "first_down": first_down, "second_attend": second_attend, "second_merge": second_merge, "second_norms": second_norms, "second_gate": second_gate, "second_value": second_value, "second_down": second_down}


@jax.custom_vjp
def low(v):
    return lax.optimization_barrier(v.astype(jnp.bfloat16)).astype(jnp.float32)

@jax.custom_vjp
def low_back(v):
    return v

def low_keep(v):
    return (low(v), None)

def low_pass(kept, grad):
    return (grad,)

def back_keep(v):
    return (v, None)

def back_low(kept, grad):
    return (low(grad),)
low.defvjp(low_keep, low_pass)
low_back.defvjp(back_keep, back_low)
highest = lax.Precision.HIGHEST
beta_one = 0.9
beta_two = 0.999
peak_rate = 1.0
warm_steps = 4.0
total_steps = 100.0
decay_rate = 0.01
adam_eps = 1e-08
norm_eps = 1e-05

def layer_norm(row_data, gain_row, shift_row):
    centered = row_data - lax.optimization_barrier(jnp.mean(row_data, axis=-1, keepdims=True))
    spread = lax.optimization_barrier(jnp.mean(centered * centered, axis=-1, keepdims=True))
    return centered * lax.rsqrt(spread + norm_eps) * gain_row + shift_row

def alibi_table(head_count, seq_len):
    slopes = jnp.exp2(-8.0 * jnp.arange(1, head_count + 1, dtype=jnp.float32) / head_count)
    places = jnp.arange(seq_len, dtype=jnp.float32)
    return slopes[:, None, None] * jnp.abs(places[:, None] - places[None, :])

def forward(start_rows, attend, merge, norms, gate, value, down):
    groups = start_rows.shape[0]
    mixed = jnp.einsum('gsd,de->gse', start_rows, low(attend), precision=highest)
    mixed = low_back(low(mixed)).reshape(groups, SEQ_LEN, 3, HEADS, HEAD_DIM)
    queries = mixed[:, :, 0]
    key_rows = mixed[:, :, 1]
    value_rows = mixed[:, :, 2]
    scores = jnp.einsum('gshe,gthe->ghst', queries, key_rows, precision=highest) * HEAD_DIM ** (-0.5)
    scores = low_back(scores - alibi_table(HEADS, SEQ_LEN))
    row_max = lax.optimization_barrier(jnp.max(scores, axis=-1, keepdims=True))
    exp_scores = jnp.exp(scores - row_max)
    probs = low(exp_scores / lax.optimization_barrier(jnp.sum(exp_scores, axis=-1, keepdims=True)))
    attended = jnp.einsum('ghst,gthe->gshe', probs, value_rows, precision=highest).reshape(groups, SEQ_LEN, D)
    attended = low_back(low(attended))
    branch = low_back(jnp.einsum('gsd,de->gse', attended, low(merge), precision=highest))
    normed = layer_norm(start_rows + branch, norms[0], norms[1])
    narrow = low(normed)
    gated = low_back(jnp.einsum('gsd,df->gsf', narrow, low(gate), precision=highest))
    valued = low_back(jnp.einsum('gsd,df->gsf', narrow, low(value), precision=highest))
    hidden = low(jax.nn.gelu(gated, approximate=False) * valued)
    ffn_out = low_back(jnp.einsum('gsf,fd->gsd', hidden, low(down), precision=highest))
    return layer_norm(normed + ffn_out, norms[2], norms[3])

def adamw_step(master, first, second, gradient, step_value, decay):
    step_rate = peak_rate * jnp.minimum(step_value / warm_steps, (total_steps - step_value) / (total_steps - warm_steps))
    fix_one = 1.0 - jnp.power(jnp.float32(beta_one), step_value)
    fix_two = 1.0 - jnp.power(jnp.float32(beta_two), step_value)
    moment = beta_one * first + (1.0 - beta_one) * gradient
    squares = beta_two * second + (1.0 - beta_two) * gradient * gradient
    updated = master - step_rate * (moment / fix_one / (jnp.sqrt(squares / fix_two) + adam_eps) + decay * master)
    return (moment, squares, updated)

def reference(hidden_rows, token_table, masked_positions, masked_counts, replace_rows, masked_cotangent, step_number, attend_master, merge_master, norms_master, gate_master, value_master, down_master, first_attend, first_merge, first_norms, first_gate, first_value, first_down, second_attend, second_merge, second_norms, second_gate, second_value, second_down):
    group = SEQ_DEV * N_MP
    masters = (attend_master, merge_master, norms_master, gate_master, value_master, down_master)
    token_rows = hidden_rows.reshape(N_DP, group, SEQ_LEN, D)
    positions = masked_positions.reshape(N_DP, group, MASK_SLOTS)
    counts = masked_counts.reshape(N_DP, group)
    row_ids = replace_rows.reshape(N_DP, group, MASK_SLOTS)
    cotangents = masked_cotangent.reshape(N_DP, group, MASK_SLOTS, D)
    slot_ids = jnp.arange(MASK_SLOTS, dtype=jnp.int32)
    places = jnp.arange(SEQ_LEN, dtype=jnp.int32)

    def one_group(totals, pieces):
        block_rows, block_pos, block_count, block_ids, block_cot = pieces
        live_slots = slot_ids[None, :] < block_count[:, None]
        place_bool = (block_pos[:, :, None] == places[None, None, :]) & live_slots[:, :, None]
        place_map = place_bool.astype(jnp.float32)
        chosen = jnp.take(token_table, block_ids.reshape(-1), axis=0).astype(jnp.float32).reshape(group, MASK_SLOTS, D)
        swapped = jnp.einsum('gjs,gjd->gsd', place_map, chosen, precision=highest)
        replaced = jnp.any(place_bool, axis=1)[:, :, None]
        start_rows = jnp.where(replaced, swapped, block_rows.astype(jnp.float32))
        cotangent_rows = jnp.einsum('gjs,gjd->gsd', place_map, block_cot.astype(jnp.float32), precision=highest)
        result, pullback = jax.vjp(forward, start_rows, attend_master, merge_master, norms_master, gate_master, value_master, down_master)
        gradients = pullback(cotangent_rows)
        totals = tuple((summed + addend for summed, addend in zip(totals, gradients[1:])))
        return (totals, (result.astype(jnp.bfloat16), gradients[0]))
    initial = tuple((jnp.zeros_like(master) for master in masters))
    totals, stacked = lax.scan(one_group, initial, (token_rows, positions, counts, row_ids, cotangents))
    layer_output = stacked[0].reshape(TOKENS, D)
    input_gradient = stacked[1].reshape(TOKENS, D)
    step_value = step_number[0].astype(jnp.float32)
    firsts = (first_attend, first_merge, first_norms, first_gate, first_value, first_down)
    seconds = (second_attend, second_merge, second_norms, second_gate, second_value, second_down)
    decays = (decay_rate, decay_rate, 0.0, decay_rate, decay_rate, decay_rate)
    updates = [adamw_step(masters[k], firsts[k], seconds[k], totals[k], step_value, decays[k]) for k in range(6)]
    return (layer_output, input_gradient, totals[0], totals[1], totals[2], totals[3], totals[4], totals[5], updates[0][0], updates[1][0], updates[2][0], updates[3][0], updates[4][0], updates[5][0], updates[0][1], updates[1][1], updates[2][1], updates[3][1], updates[4][1], updates[5][1], updates[0][2], updates[1][2], updates[2][2], updates[3][2], updates[4][2], updates[5][2])
```

```python
from functools import partial

import jax
import jax.numpy as jnp
from jax import lax
from jax.sharding import PartitionSpec as P

HEADS = 12
HEAD_DIM = 64


beta_one = 0.9
beta_two = 0.999
peak_rate = 1.0
warm_steps = 4.0
total_steps = 100.0
decay_rate = 0.01
adam_eps = 1e-08
norm_eps = 1e-05


def layer_norm(row_data, gain_row, shift_row):
    centered = row_data - jnp.mean(row_data, axis=-1, keepdims=True)
    spread = jnp.mean(centered * centered, axis=-1, keepdims=True)
    return centered * lax.rsqrt(spread + norm_eps) * gain_row + shift_row


def alibi_table(head_count, seq_len):
    slopes = jnp.exp2(-8.0 * jnp.arange(1, head_count + 1, dtype=jnp.float32) / head_count)
    places = jnp.arange(seq_len, dtype=jnp.float32)
    return slopes[:, None, None] * jnp.abs(places[:, None] - places[None, :])


def dot_nn(left_op, right_op):
    return lax.dot_general(
        left_op, right_op, (((1,), (0,)), ((), ())), preferred_element_type=jnp.float32
    )


def dot_nt(left_op, right_op):
    return lax.dot_general(
        left_op, right_op, (((1,), (1,)), ((), ())), preferred_element_type=jnp.float32
    )


def dot_tn(left_op, right_op):
    return lax.dot_general(
        left_op, right_op, (((0,), (0,)), ((), ())), preferred_element_type=jnp.float32
    )


def flip(block, axis, bits):
    size = lax.axis_size(axis)
    return lax.ppermute(block, axis, [(i, i ^ bits) for i in range(size)])


def flip_core(block):
    return flip(block, "mp", 1)


def flip_x(block):
    return flip(block, "mp", 2)


def flip_y(block):
    return flip(block, "dp", 1)


def z_groups():
    size = lax.axis_size("dp")
    return [list(range(low, size, 2)) for low in range(2)]


def place(total, block, at):
    return lax.dynamic_update_slice(total, block[None], (at,) + (0,) * block.ndim)


def gather_z(block):
    z_size = lax.axis_size("dp") // 2
    if z_size != 4:
        return lax.all_gather(block, "dp", axis=0, axis_index_groups=z_groups())
    z_at = lax.axis_index("dp") // 2
    parts = [block] + [flip(block, "dp", 2 * k) for k in range(1, 4)]
    total = jnp.zeros((4,) + block.shape, block.dtype)
    for k, part in enumerate(parts):
        total = place(total, part, z_at ^ k)
    return total


def join_y(mine, other):
    y_at = lax.axis_index("dp") % 2
    z_size, rows, columns = mine.shape
    total = jnp.zeros((z_size, 2, rows, columns), mine.dtype)
    total = lax.dynamic_update_slice(total, mine[:, None], (0, y_at, 0, 0))
    total = lax.dynamic_update_slice(total, other[:, None], (0, 1 - y_at, 0, 0))
    return total.reshape(z_size * 2 * rows, columns)


def gather_zyx(block):
    along_z = gather_z(block)
    whole = join_y(along_z, flip_y(along_z))
    return whole, flip_x(whole)


def gather_zxy(block):
    along_z = gather_z(block)
    along_x = jnp.stack([along_z, flip_x(along_z)])
    other = flip_y(along_x)
    return join_y(along_x[0], other[0]), join_y(along_x[1], other[1])


def sum_z(parts):
    z_size = lax.axis_size("dp") // 2
    if z_size != 4:
        return lax.psum_scatter(
            parts.astype(jnp.float32), "dp", scatter_dimension=0, axis_index_groups=z_groups()
        )
    z_at = lax.axis_index("dp") // 2
    total = lax.dynamic_index_in_dim(parts, z_at, 0, keepdims=False).astype(jnp.float32)
    for k in range(1, 4):
        sent = lax.dynamic_index_in_dim(parts, z_at ^ k, 0, keepdims=False)
        total = total + flip(sent, "dp", 2 * k).astype(jnp.float32)
    return total


def add_low(left_op, right_op):
    return (left_op.astype(jnp.float32) + right_op.astype(jnp.float32)).astype(jnp.bfloat16)


def by_feature(partial_sum):
    size = lax.axis_size("dp")
    features, columns = partial_sum.shape
    return partial_sum.astype(jnp.bfloat16).reshape(size // 2, 2, features // size, columns)


def pick_y(parts, y_at):
    axis = parts.ndim - 3
    return lax.dynamic_index_in_dim(parts, y_at, axis, keepdims=False)


def scatter_xyz(mine, other):
    y_at = lax.axis_index("dp") % 2
    along_x = add_low(by_feature(mine), flip_x(by_feature(other)))
    along_y = add_low(pick_y(along_x, y_at), flip_y(pick_y(along_x, 1 - y_at)))
    return sum_z(along_y)


def scatter_yxz(mine, other):
    y_at = lax.axis_index("dp") % 2
    both = jnp.stack([by_feature(mine), by_feature(other)])
    along_y = add_low(pick_y(both, y_at), flip_y(pick_y(both, 1 - y_at)))
    along_x = add_low(along_y[0], flip_x(along_y[1]))
    return sum_z(along_x)


def gelu_parts(gated):
    below = 0.5 * (1.0 + lax.erf(gated * 0.7071067811865476))
    density = 0.3989422804014327 * jnp.exp(-0.5 * gated * gated)
    return gated * below, below + gated * density


def norm_stats(row_data):
    centered = row_data - jnp.mean(row_data, axis=-1, keepdims=True)
    spread = jnp.mean(centered * centered, axis=-1, keepdims=True)
    inverse = lax.rsqrt(spread + norm_eps)
    return centered * inverse, inverse


def norm_back(xhat, inverse, gain_row, incoming):
    scaled = incoming * gain_row
    inner = jnp.mean(scaled * xhat, axis=-1, keepdims=True)
    back = inverse * (scaled - jnp.mean(scaled, axis=-1, keepdims=True) - xhat * inner)
    return back, jnp.sum(incoming * xhat, axis=0), jnp.sum(incoming, axis=0)


def adamw_step(master, first, second, gradient, step_value, decay):
    step_rate = peak_rate * jnp.minimum(
        step_value / warm_steps, (total_steps - step_value) / (total_steps - warm_steps)
    )
    fix_one = 1.0 - jnp.power(jnp.float32(beta_one), step_value)
    fix_two = 1.0 - jnp.power(jnp.float32(beta_two), step_value)
    moment = beta_one * first + (1.0 - beta_one) * gradient
    squares = beta_two * second + (1.0 - beta_two) * gradient * gradient
    updated = master - step_rate * (
        moment / fix_one / (jnp.sqrt(squares / fix_two) + adam_eps) + decay * master
    )
    return (moment, squares, updated)


def shards(
    hidden_rows,
    token_table,
    masked_positions,
    masked_counts,
    replace_rows,
    masked_cotangent,
    step_number,
    attend_master,
    merge_master,
    norms_master,
    gate_master,
    value_master,
    down_master,
    first_attend,
    first_merge,
    first_norms,
    first_gate,
    first_value,
    first_down,
    second_attend,
    second_merge,
    second_norms,
    second_gate,
    second_value,
    second_down,
):
    local_seqs, slot_count = masked_positions.shape
    local_rows, model_width = hidden_rows.shape
    length = local_rows // local_seqs
    slot_rows = local_seqs * slot_count
    dp_size = lax.axis_size("dp")
    mp_size = lax.axis_size("mp")
    core_at = lax.axis_index("mp") % 2
    low = jnp.bfloat16

    half_width = model_width // 2
    attend_low = attend_master.astype(low)
    attend_cut = attend_low.shape[1]
    packet = jnp.concatenate([attend_low, merge_master.astype(low)], axis=1)
    norms_z = gather_z(norms_master)
    first_packs = gather_zyx(packet[:, :half_width])
    second_packs = gather_zxy(packet[:, half_width:])
    norms_y = flip_y(norms_z)
    norms_own = join_y(norms_z.reshape(dp_size // 2, -1, 1), norms_y.reshape(dp_size // 2, -1, 1))
    norms_own = norms_own.reshape(1, model_width)
    norms_pair = jnp.concatenate([norms_own, flip_core(norms_own)], axis=0)
    norms_far = flip_x(norms_pair)
    x_at = lax.axis_index("mp") // 2
    norms = jnp.zeros((mp_size, model_width), jnp.float32)
    for far, pair in enumerate((norms_pair, norms_far)):
        for core in range(2):
            norms = place(norms, pair[core], 2 * (x_at ^ far) + (core_at ^ core))
    gate_full = gather_zyx(gate_master.astype(low))
    value_full = gather_zxy(value_master.astype(low))
    down_low = down_master.astype(low).T
    down_first = gather_zyx(down_low[:, :half_width])
    down_second = gather_zxy(down_low[:, half_width:])
    down_full = [jnp.concatenate([down_first[k], down_second[k]], axis=1) for k in range(2)]

    near = [jnp.concatenate([first_packs[k], second_packs[k]], axis=1) for k in range(2)]
    near = jnp.stack(near)
    far = flip_core(near)
    attend_parts = jnp.zeros((mp_size, model_width, model_width), low)
    for core, packs in enumerate((near, far)):
        for k in range(2):
            attend_parts = place(attend_parts, packs[k], 2 * (x_at ^ k) + (core_at ^ core))
    attend_full = (
        attend_parts[:, :, :attend_cut].transpose(1, 0, 2).reshape(model_width, 3 * model_width)
    )
    merge_full = (
        attend_parts[:, :, attend_cut:].transpose(1, 0, 2).reshape(model_width, model_width)
    )

    live_slots = jnp.arange(slot_count, dtype=jnp.int32)[None, :] < masked_counts[:, None]
    at_slot = masked_positions[:, :, None] == jnp.arange(length, dtype=jnp.int32)[None, None, :]
    place_bool = at_slot & live_slots[:, :, None]
    place_low = place_bool.astype(low)
    select_low = at_slot.astype(low)
    chosen = jnp.take(token_table, replace_rows.reshape(-1), axis=0).reshape(
        local_seqs, slot_count, model_width
    )
    swapped = jnp.einsum(
        "sjt,sjd->std", place_low, chosen, preferred_element_type=jnp.float32
    ).astype(low)
    replaced = jnp.any(place_bool, axis=1)[:, :, None]
    start_rows = jnp.where(
        replaced, swapped, hidden_rows.reshape(local_seqs, length, model_width)
    ).reshape(local_rows, model_width)

    def slot_low(rows):
        picked = jnp.einsum(
            "sjt,std->sjd",
            select_low,
            rows.reshape(local_seqs, length, -1),
            preferred_element_type=jnp.float32,
        )
        return picked.astype(low).reshape(slot_rows, -1)

    def slot_wide(rows):
        picked = jnp.einsum(
            "sjt,std->sjd",
            at_slot.astype(jnp.float32),
            rows.reshape(local_seqs, length, -1),
            precision=lax.Precision.HIGHEST,
        )
        return picked.reshape(slot_rows, -1)

    alibi = alibi_table(HEADS, length)
    scale = HEAD_DIM ** (-0.5)
    mixed = dot_nn(start_rows, attend_full).astype(low)
    heads_shape = (local_seqs, length, 3, HEADS, HEAD_DIM)
    queries, key_rows, value_rows = (
        mixed.reshape(heads_shape)[:, :, part].transpose(0, 2, 1, 3) for part in range(3)
    )
    scores = (
        jnp.einsum("bhse,bhte->bhst", queries, key_rows, preferred_element_type=jnp.float32) * scale
        - alibi
    )
    row_max = jnp.max(scores, axis=-1, keepdims=True)
    exp_scores = jnp.exp(scores - row_max)
    row_total = jnp.sum(exp_scores, axis=-1, keepdims=True)
    probs = (exp_scores / row_total).astype(low)
    attended = jnp.einsum("bhst,bhte->bhse", probs, value_rows, preferred_element_type=jnp.float32)
    attended_rows = attended.astype(low).transpose(0, 2, 1, 3).reshape(local_rows, model_width)
    first_sum = start_rows.astype(jnp.float32) + dot_nn(attended_rows, merge_full)
    first_hat, first_inverse = norm_stats(first_sum)
    normed = first_hat * norms[0] + norms[1]
    narrow = normed.astype(low)

    chip_rows = jnp.concatenate([narrow, flip_core(narrow)], axis=0)
    ffn_part = 0.0
    for k in range(2):
        gated = dot_nn(chip_rows, gate_full[k])
        valued = dot_nn(chip_rows, value_full[k])
        hidden = (gelu_parts(gated)[0] * valued).astype(low)
        ffn_part = ffn_part + dot_nt(hidden, down_full[k])
    ffn_out = ffn_part[:local_rows] + flip_core(ffn_part[local_rows:])
    second_sum = normed + ffn_out
    second_hat, second_inverse = norm_stats(second_sum)
    layer_output = (second_hat * norms[2] + norms[3]).astype(low)

    slot_cotangent = jnp.where(
        live_slots[:, :, None], masked_cotangent.astype(jnp.float32), 0.0
    ).reshape(slot_rows, model_width)
    slot_hat, slot_inverse = norm_stats(slot_wide(second_sum))
    second_back, gain_two_back, shift_two_back = norm_back(
        slot_hat, slot_inverse, norms[2], slot_cotangent
    )
    pulled = second_back.astype(low)
    slot_narrow = slot_low(narrow)
    sent = jnp.stack([pulled, slot_narrow])
    got = flip_core(sent)
    work_pull = jnp.concatenate([pulled, got[0]], axis=0)
    work_rows = jnp.concatenate([slot_narrow, got[1]], axis=0)
    gate_grads, value_grads, down_grads = [], [], []
    normed_part = 0.0
    for k in range(2):
        gated = dot_nn(work_rows, gate_full[k])
        valued = dot_nn(work_rows, value_full[k])
        gelu, slope = gelu_parts(gated)
        hidden = (gelu * valued).astype(low)
        hidden_back = dot_nn(work_pull, down_full[k])
        gate_back = (hidden_back * valued * slope).astype(low)
        value_back = (hidden_back * gelu).astype(low)
        down_grads.append(dot_tn(work_pull, hidden))
        gate_grads.append(dot_tn(work_rows, gate_back))
        value_grads.append(dot_tn(work_rows, value_back))
        normed_part = (
            normed_part + dot_nt(gate_back, gate_full[k]) + dot_nt(value_back, value_full[k])
        )
    gradient_gate = scatter_xyz(gate_grads[0], gate_grads[1])
    gradient_value = scatter_yxz(value_grads[0], value_grads[1])
    gradient_down = jnp.concatenate(
        [
            scatter_xyz(down_grads[0][:, :half_width], down_grads[1][:, :half_width]),
            scatter_yxz(down_grads[0][:, half_width:], down_grads[1][:, half_width:]),
        ],
        axis=1,
    ).T
    normed_back = normed_part[:slot_rows] + flip_core(normed_part[slot_rows:])
    slot_hat, slot_inverse = norm_stats(slot_wide(first_sum))
    first_back, gain_one_back, shift_one_back = norm_back(
        slot_hat, slot_inverse, norms[0], normed_back + second_back
    )
    branch_pull = first_back.astype(low)
    attended_back = dot_nt(branch_pull, merge_full).astype(low)
    slot_attended = slot_low(attended_rows)
    slot_start = slot_low(start_rows)

    slot_queries = jnp.einsum(
        "sjt,shte->shje", select_low, queries, preferred_element_type=jnp.float32
    ).astype(low)
    slot_alibi = alibi_table(HEADS, length)
    slopes = jnp.exp2(-8.0 * jnp.arange(1, HEADS + 1, dtype=jnp.float32) / HEADS)
    apart = jnp.abs(
        masked_positions[:, :, None] - jnp.arange(length, dtype=jnp.int32)[None, None, :]
    ).astype(jnp.float32)
    slot_alibi = slopes[None, :, None, None] * apart[:, None]
    scores = (
        jnp.einsum("bhse,bhte->bhst", slot_queries, key_rows, preferred_element_type=jnp.float32)
        * scale
        - slot_alibi
    )
    row_max = jnp.max(scores, axis=-1, keepdims=True)
    exp_scores = jnp.exp(scores - row_max)
    probs = exp_scores / jnp.sum(exp_scores, axis=-1, keepdims=True)
    heads_back = attended_back.reshape(local_seqs, slot_count, HEADS, HEAD_DIM).transpose(
        0, 2, 1, 3
    )
    probs_back = jnp.einsum(
        "bhse,bhte->bhst", heads_back, value_rows, preferred_element_type=jnp.float32
    )
    inner = jnp.sum(probs * probs_back, axis=-1, keepdims=True)
    scores_back = (probs * (probs_back - inner)).astype(low)
    queries_back = (
        jnp.einsum("bhst,bhte->bhse", scores_back, key_rows, preferred_element_type=jnp.float32)
        * scale
    ).astype(low)
    keys_back = (
        jnp.einsum("bhst,bhse->bhte", scores_back, slot_queries, preferred_element_type=jnp.float32)
        * scale
    ).astype(low)
    values_back = jnp.einsum(
        "bhst,bhse->bhte", probs.astype(low), heads_back, preferred_element_type=jnp.float32
    ).astype(low)
    queries_back = jnp.einsum(
        "sjt,shje->shte", select_low, queries_back, preferred_element_type=jnp.float32
    ).astype(low)
    mixed_back = jnp.stack(
        [part.transpose(0, 2, 1, 3) for part in (queries_back, keys_back, values_back)], axis=2
    ).reshape(local_rows, 3 * model_width)
    placed_back = jnp.einsum(
        "sjt,sjd->std",
        at_slot.astype(jnp.float32),
        first_back.reshape(local_seqs, slot_count, model_width),
        precision=lax.Precision.HIGHEST,
    ).reshape(local_rows, model_width)
    input_gradient = placed_back + dot_nt(mixed_back, attend_full)

    merge_cut = merge_master.shape[1]
    grads = []
    for core in range(2):
        for k in range(2):
            block = 2 * (x_at ^ k) + (core_at ^ core)
            attend_cols = lax.dynamic_slice_in_dim(mixed_back, block * attend_cut, attend_cut, 1)
            merge_cols = lax.dynamic_slice_in_dim(branch_pull, block * merge_cut, merge_cut, 1)
            grads.append(
                jnp.concatenate(
                    [dot_tn(start_rows, attend_cols), dot_tn(slot_attended, merge_cols)], axis=1
                )
            )
    got = flip_core(jnp.stack(grads[2:]).astype(low))
    grads = [grads[k] + got[k].astype(jnp.float32) for k in range(2)]
    packed = jnp.concatenate(
        [
            scatter_xyz(grads[0][:, :half_width], grads[1][:, :half_width]),
            scatter_yxz(grads[0][:, half_width:], grads[1][:, half_width:]),
        ],
        axis=1,
    )
    gradient_attend, gradient_merge = packed[:, :attend_cut], packed[:, attend_cut:]

    norm_parts = jnp.stack([gain_one_back, shift_one_back, gain_two_back, shift_two_back], axis=0)
    norm_parts = norm_parts.reshape(2, 2, model_width)

    def mine_of(parts, at, axis):
        return lax.dynamic_index_in_dim(parts, at, axis, keepdims=False)

    norm_parts = mine_of(norm_parts, core_at, 1) + flip_core(mine_of(norm_parts, 1 - core_at, 1))
    norm_parts = mine_of(norm_parts, x_at, 0) + flip_x(mine_of(norm_parts, 1 - x_at, 0))
    norm_parts = norm_parts.reshape(dp_size // 2, 2, 1, -1)
    y_at = lax.axis_index("dp") % 2
    norm_parts = mine_of(norm_parts, y_at, 1) + flip_y(mine_of(norm_parts, 1 - y_at, 1))
    gradient_norms = sum_z(norm_parts)

    step_value = step_number[0].astype(jnp.float32)
    moment_attend, squares_attend, updated_attend = adamw_step(
        attend_master, first_attend, second_attend, gradient_attend, step_value, decay_rate
    )
    moment_merge, squares_merge, updated_merge = adamw_step(
        merge_master, first_merge, second_merge, gradient_merge, step_value, decay_rate
    )
    moment_norms, squares_norms, updated_norms = adamw_step(
        norms_master, first_norms, second_norms, gradient_norms, step_value, 0.0
    )
    moment_gate, squares_gate, updated_gate = adamw_step(
        gate_master, first_gate, second_gate, gradient_gate, step_value, decay_rate
    )
    moment_value, squares_value, updated_value = adamw_step(
        value_master, first_value, second_value, gradient_value, step_value, decay_rate
    )
    moment_down, squares_down, updated_down = adamw_step(
        down_master, first_down, second_down, gradient_down, step_value, decay_rate
    )
    return (
        layer_output,
        input_gradient,
        gradient_attend,
        gradient_merge,
        gradient_norms,
        gradient_gate,
        gradient_value,
        gradient_down,
        moment_attend,
        moment_merge,
        moment_norms,
        moment_gate,
        moment_value,
        moment_down,
        squares_attend,
        squares_merge,
        squares_norms,
        squares_gate,
        squares_value,
        squares_down,
        updated_attend,
        updated_merge,
        updated_norms,
        updated_gate,
        updated_value,
        updated_down,
    )


def solution(mesh):
    return jax.shard_map(
        shards,
        mesh=mesh,
        in_specs=(
            P(("dp", "mp"), None),
            P(),
            P(("dp", "mp"), None),
            P(("dp", "mp")),
            P(("dp", "mp"), None),
            P(("dp", "mp"), None, None),
            P(),
            P("dp", "mp"),
            P("dp", "mp"),
            P("mp", "dp"),
            P("dp", "mp"),
            P("dp", "mp"),
            P("mp", "dp"),
            P("dp", "mp"),
            P("dp", "mp"),
            P("mp", "dp"),
            P("dp", "mp"),
            P("dp", "mp"),
            P("mp", "dp"),
            P("dp", "mp"),
            P("dp", "mp"),
            P("mp", "dp"),
            P("dp", "mp"),
            P("dp", "mp"),
            P("mp", "dp"),
        ),
        out_specs=(
            P(("dp", "mp"), None),
            P(("dp", "mp"), None),
            P("dp", "mp"),
            P("dp", "mp"),
            P("mp", "dp"),
            P("dp", "mp"),
            P("dp", "mp"),
            P("mp", "dp"),
            P("dp", "mp"),
            P("dp", "mp"),
            P("mp", "dp"),
            P("dp", "mp"),
            P("dp", "mp"),
            P("mp", "dp"),
            P("dp", "mp"),
            P("dp", "mp"),
            P("mp", "dp"),
            P("dp", "mp"),
            P("dp", "mp"),
            P("mp", "dp"),
            P("dp", "mp"),
            P("dp", "mp"),
            P("mp", "dp"),
            P("dp", "mp"),
            P("dp", "mp"),
            P("mp", "dp"),
        ),
        check_vma=False,
    )
```

```python
from functools import partial

import jax
import jax.numpy as jnp
from jax import lax
from jax.experimental import pallas as pl
from jax.experimental.pallas import tpu as pltpu
from jax.sharding import PartitionSpec as P

HEADS = 12
HEAD_DIM = 64


beta_one = 0.9
beta_two = 0.999
peak_rate = 1.0
warm_steps = 4.0
total_steps = 100.0
decay_rate = 0.01
adam_eps = 1e-08
norm_eps = 1e-05


def layer_norm(row_data, gain_row, shift_row):
    centered = row_data - jnp.mean(row_data, axis=-1, keepdims=True)
    spread = jnp.mean(centered * centered, axis=-1, keepdims=True)
    return centered * lax.rsqrt(spread + norm_eps) * gain_row + shift_row


def alibi_table(head_count, seq_len):
    slopes = jnp.exp2(-8.0 * jnp.arange(1, head_count + 1, dtype=jnp.float32) / head_count)
    places = jnp.arange(seq_len, dtype=jnp.float32)
    return slopes[:, None, None] * jnp.abs(places[:, None] - places[None, :])


def dot_nn(left_op, right_op):
    return lax.dot_general(
        left_op, right_op, (((1,), (0,)), ((), ())), preferred_element_type=jnp.float32
    )


def dot_nt(left_op, right_op):
    return lax.dot_general(
        left_op, right_op, (((1,), (1,)), ((), ())), preferred_element_type=jnp.float32
    )


def dot_tn(left_op, right_op):
    return lax.dot_general(
        left_op, right_op, (((0,), (0,)), ((), ())), preferred_element_type=jnp.float32
    )


def flip(block, axis, bits):
    size = lax.axis_size(axis)
    return lax.ppermute(block, axis, [(i, i ^ bits) for i in range(size)])


def flip_core(block):
    return flip(block, "mp", 1)


def flip_x(block):
    return flip(block, "mp", 2)


def flip_y(block):
    return flip(block, "dp", 1)


def norm_stats(row_data):
    centered = row_data - jnp.mean(row_data, axis=-1, keepdims=True)
    spread = jnp.mean(centered * centered, axis=-1, keepdims=True)
    inverse = lax.rsqrt(spread + norm_eps)
    return centered * inverse, inverse


def z_groups():
    size = lax.axis_size("dp")
    return [list(range(low, size, 2)) for low in range(2)]


def pass_on(*refs):
    pass


def after(block, *others):
    return pl.pallas_call(
        pass_on,
        out_shape=jax.ShapeDtypeStruct(block.shape, block.dtype),
        in_specs=[pl.BlockSpec(memory_space=pl.ANY)] * (1 + len(others)),
        out_specs=pl.BlockSpec(memory_space=pl.ANY),
        input_output_aliases={0: 0},
        cost_estimate=pl.CostEstimate(flops=0, bytes_accessed=0, transcendentals=0),
    )(block, *others)


def is_small():
    return lax.axis_size("dp") == 8


def gather_z(block):
    far = flip(block, "dp", 4)
    return [block, far, flip(block, "dp", 2), flip(far, "dp", 2)]


def piece_rows(features):
    at = jnp.arange(8, dtype=jnp.int32)
    if is_small():
        along_z = ((at & 1) << 1) + ((at >> 1) & 1)
        at = (2 * along_z + (at >> 2)) ^ lax.axis_index("dp")
    return at * (features // 8)


def gather_whole(block):
    whole = lax.all_gather(block, "dp", axis=1, tiled=True)
    lots, features, columns = whole.shape
    whole = whole.reshape(lots, 8, features // 8, columns).transpose(1, 0, 2, 3)
    return [whole], [flip_x(whole)]


def add_low(*parts):
    return sum(part.astype(jnp.float32) for part in parts).astype(jnp.bfloat16)


def sum_dp(whole):
    return lax.psum_scatter(whole.astype(jnp.float32), "dp", scatter_dimension=0, tiled=True)


def from_pieces(*parts):
    whole = jnp.concatenate(parts, axis=0)
    return sum_dp(whole.reshape(-1, whole.shape[-1]))


COST = 0.0
VMEM_LIMIT = 56 * 1024 * 1024
ANYWHERE = pl.BlockSpec(memory_space=pl.ANY)
IN_VMEM = pl.BlockSpec(memory_space=pltpu.VMEM)
IN_SMEM = pl.BlockSpec(memory_space=pltpu.SMEM)


def kernel_call(body, outs, specs, scratch, flops, moved):
    return pl.pallas_call(
        body,
        out_shape=outs,
        in_specs=specs,
        out_specs=[IN_VMEM] * len(outs),
        scratch_shapes=scratch,
        compiler_params=pltpu.CompilerParams(vmem_limit_bytes=VMEM_LIMIT),
        cost_estimate=pl.CostEstimate(
            flops=int(flops * COST), bytes_accessed=int(moved * COST), transcendentals=0
        ),
    )


def like(shape, dtype):
    return jax.ShapeDtypeStruct(shape, dtype)


def with_lot(groups, lot):
    return [(group, (i, lot)) for group in groups for i in range(group.shape[0])]


def load_pieces(pieces, rows, total, sems):
    copies = []
    count = total.shape[0] // 8
    for k, (group, at) in enumerate(pieces):
        to = total.at[pl.ds(pl.multiple_of(rows[k], 32), count), :]
        copies.append(pltpu.make_async_copy(group.at[(*at, pl.ds(0, count))], to, sems.at[k]))
        copies[-1].start()
    return copies


EXTRA = 16


def load_extras(groups, spots, total, sems):
    copies = []
    for group in groups:
        for i in range(group.shape[0]):
            k = len(copies)
            source = group.at[i, 0, pl.ds(group.shape[2] - EXTRA, EXTRA), :]
            copies.append(pltpu.make_async_copy(source, total.at[spots[k]], sems.at[k]))
            copies[-1].start()
    return copies


def split_low(block):
    parts = []
    for _ in range(3):
        part = lax.reduce_precision(block, 8, 7)
        parts.append(jnp.pad(part.astype(jnp.bfloat16), ((0, EXTRA - 1), (0, 128 - block.shape[1]))))
        block = block - part
    return jnp.pad(jnp.concatenate(parts, axis=1), ((0, 0), (0, 384)))


def wait_all(copies):
    for copy in copies:
        copy.wait()


def gelu_parts(gated):
    below = 0.5 + 0.5 * lax.erf(gated * 0.7071067811865476)
    return gated * below, below


def lower_lanes(shape):
    return lax.broadcasted_iota(jnp.int32, shape, 1) < 64


def unpack_columns_of(blocks, attend, merge):
    for block, (column, merge_column) in enumerate(((0, 0), (640, 256), (1152, 384), (1792, 640))):
        attend[:, column : column + 512] = blocks[block, :, :512]
        merge[:, merge_column : merge_column + 128] = blocks[block, :, 512:640]
    for pair, (column, merge_column) in enumerate(((512, 128), (1664, 512))):
        even = blocks[2 * pair, :, 640:].astype(jnp.float32)
        odd = blocks[2 * pair + 1, :, 640:].astype(jnp.float32)
        lower = lower_lanes(even.shape)
        attend[:, column : column + 128] = jnp.where(lower, even, odd).astype(jnp.bfloat16)
        mixed_up = pltpu.roll(jnp.where(lower, odd, even), 64, 1)
        merge[:, merge_column : merge_column + 128] = mixed_up.astype(jnp.bfloat16)


def first_kernel(counts, extra, places, rows, spots, start, norms_given, positions, *refs):
    low = jnp.bfloat16
    groups = []
    for count in counts:
        groups.append(refs[:count])
        refs = refs[count:]
    attend, merge, mixed, normed, *narrow, slot_sum, slot_attended, slot_narrow, norms = refs[:10]
    blocks, attended, scores, extras, sems = refs[10:]
    copies = []
    for at, group in enumerate(groups):
        copies += load_pieces(with_lot(group, 0), rows, blocks.at[places[at]], sems.at[0, at])
        if extra:
            copies += load_extras(group, spots, extras.at[places[at]], sems.at[1, at])
    wait_all(copies)
    if extra:
        for block in range(4):
            whole = jnp.zeros((8, norms.shape[1]), jnp.float32)
            for spot in range(8):
                parts = extras[block, spot].astype(jnp.float32)[:8, :]
                value = parts[:, :128] + parts[:, 128:256] + parts[:, 256:384]
                value = jnp.concatenate([value, jnp.zeros((8, norms.shape[1] - 128), jnp.float32)], axis=1)
                whole = whole + (pltpu.roll(value, spot * (norms.shape[1] // 8), 1) if spot else value)
            norms[block : block + 1, :] = whole[:1, :]
    else:
        norms[...] = norms_given[...]
    unpack_columns_of(blocks, attend, merge)
    width = merge.shape[0]
    length = 128
    slots = 32
    scale = HEAD_DIM ** (-0.5)
    for column in range(0, 3 * width, 256):
        cut = slice(column, column + 256)
        mixed[:, cut] = dot_nn(start[...], attend[:, cut]).astype(low)
    shape = (length, length)
    apart = jnp.abs(
        lax.broadcasted_iota(jnp.int32, shape, 0) - lax.broadcasted_iota(jnp.int32, shape, 1)
    ).astype(jnp.float32)
    lower = lower_lanes(shape)

    def step(target, first, seq, carry):
        at = pl.ds(pl.multiple_of(seq * length, length), length)
        to = pl.ds(pl.multiple_of(seq * slots, slots), slots)
        for pair in range(HEADS // 2):
            column = 2 * HEAD_DIM * pair
            queries = mixed[at, column : column + 128]
            keys = mixed[at, width + column : width + column + 128]
            zero = jnp.zeros_like(queries)
            for half in range(2):
                own = jnp.where(lower, queries, zero) if half == 0 else jnp.where(lower, zero, queries)
                head = 2 * pair + half
                scores[head] = dot_nt(own, keys) * scale - apart * slopes_of(head)
        raised = scores[...]
        raised = jnp.exp(raised - jnp.max(raised, axis=-1, keepdims=True))
        scores[...] = raised / jnp.sum(raised, axis=-1, keepdims=True)
        for pair in range(HEADS // 2):
            column = 2 * HEAD_DIM * pair
            values = mixed[at, 2 * width + column : 2 * width + column + 128]
            heads = [dot_nn(scores[2 * pair + half].astype(low), values) for half in range(2)]
            attended[at, column : column + 128] = jnp.where(lower, heads[0], heads[1]).astype(low)
        total = start[at, :].astype(jnp.float32) + dot_nn(attended[at, :], merge[...])
        xhat, _ = norm_stats(total)
        rows = xhat * norms[0:1, :] + norms[1:2, :]
        normed[at, :] = rows
        target[pl.ds(pl.multiple_of((seq - first) * length, length), length), :] = rows.astype(low)
        selector = one_hot(positions[to, :], length)
        slot_sum[to, :] = select_exact(selector, total)
        slot_attended[to, :] = dot_nn(selector, attended[at, :]).astype(low)
        slot_narrow[to, :] = dot_nn(selector, rows.astype(low)).astype(low)
        return carry

    seqs = start.shape[0] // length // 2
    lax.fori_loop(0, seqs, partial(step, narrow[0], 0), 0, unroll=True)
    lax.fori_loop(seqs, 2 * seqs, partial(step, narrow[1], seqs), 0, unroll=True)


def first_part(extra, places, rows, spots, start, norms, positions, groups):
    count, width = start.shape
    slot_rows = positions.shape[0]
    low = jnp.bfloat16
    return kernel_call(
        partial(first_kernel, [len(group) for group in groups], extra),
        [
            like((width, 3 * width), low),
            like((width, width), low),
            like((count, 3 * width), low),
            like((count, width), jnp.float32),
            like((count // 2, width), low),
            like((count // 2, width), low),
            like((slot_rows, width), jnp.float32),
            like((slot_rows, width), low),
            like((slot_rows, width), low),
            like((4, width), jnp.float32),
        ],
        [IN_SMEM] * 3 + [IN_VMEM] * 3 + [ANYWHERE] * sum(map(len, groups)),
        [
            pltpu.VMEM((4, width, width), low),
            pltpu.VMEM((count, width), low),
            pltpu.VMEM((HEADS, 128, 128), jnp.float32),
            pltpu.VMEM((4, 8, EXTRA, width), low),
            pltpu.SemaphoreType.DMA((2, 4, 8)),
        ],
        2 * count * width * 4 * width,
        16 * width * width,
    )(places, rows, spots, start, norms, positions, *sum(groups, []))


def pack_columns(attend, merge, core_at):
    even = jnp.concatenate(
        [attend[:, :512], merge[:, :128], attend[:, 512:], merge[:, 128:]], axis=1
    )
    odd = jnp.concatenate([attend[:, 64:], merge[:, 64:], merge[:, :64], attend[:, :64]], axis=1)
    return jnp.where(core_at == 0, even, odd)


def unpack_columns(packed, core_at):
    even = jnp.concatenate([packed[:, :512], packed[:, 640:704]], axis=1)
    odd = jnp.concatenate([packed[:, 704:], packed[:, :512]], axis=1)
    even_merge = jnp.concatenate([packed[:, 512:640], packed[:, 704:]], axis=1)
    odd_merge = jnp.concatenate([packed[:, 640:704], packed[:, 512:640]], axis=1)
    return jnp.where(core_at == 0, even, odd), jnp.where(core_at == 0, even_merge, odd_merge)


def front_kernel(count, rows, *refs):
    sources, refs = refs[:4], refs[4:]
    near, far = refs[: count[0]], refs[count[0] : count[0] + count[1]]
    hidden, gates, values, sems = refs[count[0] + count[1] + 1 :]
    copies = []
    for k, groups in enumerate((near, far)):
        copies.append(
            load_pieces(with_lot(groups, 0), rows, gates.at[k], sems.at[k, 0])
            + load_pieces(with_lot(groups, 1), rows, values.at[k], sems.at[k, 1])
        )
    quarter = sources[0].shape[0]
    for k in range(2):
        wait_all(copies[k])
        for part, source in enumerate(sources):
            start = part * quarter

            def step(tile, carry, k=k, start=start, source=source):
                block = source[pl.ds(pl.multiple_of(tile * 256, 256), 256), :]
                to = pl.ds(pl.multiple_of(start + tile * 256, 256), 256)
                for column in range(0, gates.shape[2], 256):
                    cut = slice(column, column + 256)
                    gated = dot_nn(block, gates[k, :, cut])
                    valued = dot_nn(block, values[k, :, cut])
                    hidden[k, to, cut] = (gelu_parts(gated)[0] * valued).astype(jnp.bfloat16)
                return carry

            lax.fori_loop(0, source.shape[0] // 256, step, 0)


def ffn_front(rows, sources, near, far, earlier):
    quarter, width = sources[0].shape
    return kernel_call(
        partial(front_kernel, (len(near), len(far))),
        [like((2, 4 * quarter, width), jnp.bfloat16)],
        [IN_SMEM] + [IN_VMEM] * 4 + [ANYWHERE] * (len(near) + len(far) + 1),
        [
            pltpu.VMEM((2, width, width), jnp.bfloat16),
            pltpu.VMEM((2, width, width), jnp.bfloat16),
            pltpu.SemaphoreType.DMA((2, 2, 8)),
        ],
        2 * 4 * quarter * width * 4 * width,
        16 * width * width,
    )(rows, *sources, *near, *far, earlier)[0]


def down_kernel(lots, rows, hidden, *refs):
    split, end = len(lots[0]), len(lots[0]) + len(lots[1])
    mine, other, downs, sems = refs[end + 1 :]
    copies = load_pieces(zip(refs[:split], lots[0]), rows, downs.at[0], sems.at[0])
    copies += load_pieces(zip(refs[split:end], lots[1]), rows, downs.at[1], sems.at[1])
    wait_all(copies)
    half = mine.shape[0]
    width = downs.shape[1]
    for part, target in ((1, other), (0, mine)):
        at = slice(part * half, (part + 1) * half)
        for column in range(0, width, 256):
            cut = slice(column, column + 256)
            target[:, cut] = dot_nt(hidden[0, at, :], downs[0, cut, :]) + dot_nt(
                hidden[1, at, :], downs[1, cut, :]
            )


def ffn_down(rows, hidden, near, far, earlier):
    both, width = hidden.shape[1:]
    return kernel_call(
        partial(down_kernel, [[lot for _, lot in group] for group in (near, far)]),
        [like((both // 2, width), jnp.float32)] * 2,
        [IN_SMEM, IN_VMEM] + [ANYWHERE] * (len(near) + len(far) + 1),
        [pltpu.VMEM((2, width, width), jnp.bfloat16), pltpu.SemaphoreType.DMA((2, 8))],
        2 * both * width * 2 * width,
        12 * width * width,
    )(rows, hidden, *[group for group, _ in near + far], earlier)


def select_exact(selector, block):
    first = block.astype(jnp.bfloat16)
    rest = block - first.astype(jnp.float32)
    second = rest.astype(jnp.bfloat16)
    third = (rest - second.astype(jnp.float32)).astype(jnp.bfloat16)
    return dot_nn(selector, first) + dot_nn(selector, second) + dot_nn(selector, third)


def norm_back(xhat, inverse, gain_row, incoming):
    scaled = incoming * gain_row
    inner = jnp.mean(scaled * xhat, axis=-1, keepdims=True)
    back = inverse * (scaled - jnp.mean(scaled, axis=-1, keepdims=True) - xhat * inner)
    gain_back = jnp.sum(incoming * xhat, axis=0, keepdims=True)
    return back, gain_back, jnp.sum(incoming, axis=0, keepdims=True)


def one_hot(positions, length):
    shape = (positions.shape[0], length)
    return (positions == lax.broadcasted_iota(jnp.int32, shape, 1)).astype(jnp.bfloat16)


def second_kernel(
    normed, part, got, norms, positions, live, cotangent, output, pulled, back, norm_grads
):
    slots = cotangent.shape[1]
    length = normed.shape[0] // cotangent.shape[0]
    norm_grads[...] = jnp.zeros_like(norm_grads)

    def step(seq, carry):
        at = pl.ds(pl.multiple_of(seq * length, length), length)
        to = pl.ds(pl.multiple_of(seq * slots, slots), slots)
        total = normed[at, :] + part[at, :] + got[at, :]
        xhat, _ = norm_stats(total)
        output[at, :] = (xhat * norms[2:3, :] + norms[3:4, :]).astype(jnp.bfloat16)
        selector = one_hot(positions[to, :], length)
        xhat, inverse = norm_stats(select_exact(selector, total))
        incoming = jnp.where(live[to, :] > 0, cotangent[seq].astype(jnp.float32), 0.0)
        slot_back, gain_back, shift_back = norm_back(xhat, inverse, norms[2:3, :], incoming)
        back[to, :] = slot_back
        pulled[to, :] = slot_back.astype(jnp.bfloat16)
        norm_grads[0:1, :] += gain_back
        norm_grads[1:2, :] += shift_back
        return carry

    lax.fori_loop(0, cotangent.shape[0], step, 0, unroll=True)


def second_norm(normed, part, got, norms, positions, live, cotangent):
    count, width = normed.shape
    slot_rows = positions.shape[0]
    return kernel_call(
        second_kernel,
        [
            like((count, width), jnp.bfloat16),
            like((slot_rows, width), jnp.bfloat16),
            like((slot_rows, width), jnp.float32),
            like((2, width), jnp.float32),
        ],
        [IN_VMEM] * 7,
        [],
        8 * slot_rows * 128 * width,
        16 * count * width,
    )(normed, part, got, norms, positions, live, cotangent)


def slot_kernel(count, rows, *refs):
    narrows, wide = refs[:4], refs[4 : 4 + count]
    work_rows, gelu_out, slope_out, hidden, gates, values, sems = refs[5 + count :]
    copies = load_pieces(with_lot(wide, 0), rows, gates, sems.at[0])
    copies += load_pieces(with_lot(wide, 1), rows, values, sems.at[1])
    size = narrows[0].shape[0]
    for k in range(4):
        work_rows[k * size : (k + 1) * size, :] = narrows[k][...]
    wait_all(copies)
    for column in range(0, gates.shape[1], 256):
        cut = slice(column, column + 256)
        gated = dot_nn(work_rows[...], gates[:, cut])
        valued = dot_nn(work_rows[...], values[:, cut])
        gelu, below = gelu_parts(gated)
        slope = below + gated * (0.3989422804014327 * jnp.exp(-0.5 * gated * gated))
        hidden[:, cut] = (gelu * valued).astype(jnp.bfloat16)
        gelu_out[:, cut] = gelu
        slope_out[:, cut] = valued * slope


def slot_front(rows, narrows, wide, earlier):
    size, width = narrows[0].shape
    low = jnp.bfloat16
    shape = (4 * size, width)
    return kernel_call(
        partial(slot_kernel, len(wide)),
        [like(shape, low), like(shape, jnp.float32), like(shape, jnp.float32), like(shape, low)],
        [IN_SMEM] + [IN_VMEM] * 4 + [ANYWHERE] * (len(wide) + 1),
        [pltpu.VMEM((width, width), low)] * 2 + [pltpu.SemaphoreType.DMA((2, 8))],
        0,
        0,
    )(rows, *narrows, *wide, earlier)


def back_kernel(count, lots, rows, *refs):
    pulls, gelu, slope = refs[0:4], refs[4], refs[5]
    wide, deep = refs[6 : 6 + count[0]], refs[6 + count[0] : 6 + count[0] + count[1]]
    keep, send, pull_rows, gate_back, value_back = refs[6 + count[0] + count[1] : -4]
    gates, values, downs, sems = refs[-4:]
    late = load_pieces(with_lot(wide, 0), rows, gates, sems.at[0])
    late += load_pieces(with_lot(wide, 1), rows, values, sems.at[1])
    copies = load_pieces(zip(deep, lots), rows, downs, sems.at[2])
    size = pulls[0].shape[0]
    for k in range(4):
        pull_rows[k * size : (k + 1) * size, :] = pulls[k][...]
    wait_all(copies)
    for column in range(0, gates.shape[1], 256):
        cut = slice(column, column + 256)
        hidden_back = dot_nn(pull_rows[...], downs[:, cut])
        gate_back[:, cut] = (hidden_back * slope[:, cut]).astype(jnp.bfloat16)
        value_back[:, cut] = (hidden_back * gelu[:, cut]).astype(jnp.bfloat16)
    wait_all(late)
    for target, start in ((send, 2), (keep, 0)):
        at = slice(start * size, (start + 2) * size)
        for column in range(0, gates.shape[0], 256):
            cut = slice(column, column + 256)
            total = dot_nt(gate_back[at, :], gates[cut, :])
            total = total + dot_nt(value_back[at, :], values[cut, :])
            target[0, :, cut] = total[:size]
            target[1, :, cut] = total[size:]


def ffn_back(rows, pulls, gelu, slope, wide, deep):
    size, width = pulls[0].shape
    low = jnp.bfloat16
    return kernel_call(
        partial(back_kernel, (len(wide), len(deep)), [lot for _, lot in deep]),
        [like((2, size, width), jnp.float32)] * 2 + [like((4 * size, width), low)] * 3,
        [IN_SMEM] + [IN_VMEM] * 6 + [ANYWHERE] * (len(wide) + len(deep)),
        [pltpu.VMEM((width, width), low)] * 3 + [pltpu.SemaphoreType.DMA((3, 8))],
        0,
        0,
    )(rows, *pulls, gelu, slope, *wide, *[group for group, _ in deep])


def store_pieces(total, rows, mine, other):
    count = total.shape[0] // 8
    for k in range(8):
        at = pl.ds(pl.multiple_of(rows[k], 32), count)
        to = mine if k < 4 else other
        to[k % 4, :count, :] = total[at, :].astype(jnp.bfloat16)


def grads_kernel(rows, work_rows, pull_rows, gate_back, value_back, hidden, *refs):
    total, pull_turned, work_turned = refs[-3:]
    pull_turned[...] = pull_rows[...].T
    work_turned[...] = work_rows[...].T
    factors = ((pull_turned, hidden), (work_turned, gate_back), (work_turned, value_back))
    for which, (left_op, right_op) in enumerate(factors):
        for column in range(0, total.shape[1], 256):
            cut = slice(column, column + 256)
            total[:, cut] = dot_nn(left_op[...], right_op[:, cut])
        lot = 0 if which == 2 else which
        outs = refs[2:4] if which == 2 else refs[0:2]
        store_pieces(total, rows, outs[0].at[:, lot], outs[1].at[:, lot])


def ffn_grads(rows, work_rows, pull_rows, gate_back, value_back, hidden):
    size, width = work_rows.shape
    return kernel_call(
        grads_kernel,
        [like((4, 2, width // 8, width), jnp.bfloat16)] * 2
        + [like((4, 1, width // 8, width), jnp.bfloat16)] * 2,
        [IN_SMEM] + [IN_VMEM] * 5,
        [pltpu.VMEM((width, width), jnp.float32)] + [pltpu.VMEM((width, size), jnp.bfloat16)] * 2,
        2 * size * width * width * 3,
        12 * width * width,
    )(rows, work_rows, pull_rows, gate_back, value_back, hidden)


def split_kernel(from_y, from_x, *refs):
    first, second, sems = refs[-3:]
    half = first.shape[0]
    copies = [
        pltpu.make_async_copy(from_y.at[pl.ds(0, half)], first, sems.at[0]),
        pltpu.make_async_copy(from_x.at[pl.ds(half, half)], second, sems.at[1]),
    ]
    for copy in copies:
        copy.start()
    wait_all(copies)


def split_halves(from_y, from_x, *earlier):
    half = like((from_y.shape[0] // 2,) + from_y.shape[1:], from_y.dtype)
    return kernel_call(
        split_kernel,
        [half, half],
        [ANYWHERE] * (2 + len(earlier)),
        [pltpu.SemaphoreType.DMA((2,))],
        0,
        0,
    )(from_y, from_x, *earlier)


def wide_sum(*blocks):
    return sum(block.astype(jnp.float32) for block in blocks)


def total_of(*blocks):
    return wide_sum(*blocks)


def corner_kernel(near, got, *refs):
    first, second = refs[-2:]
    for k in range(4):
        target = first if k < 2 else second
        target[k % 2] = wide_sum(near[k], got[k]).astype(jnp.bfloat16)


def corner_sum(near, got, *earlier):
    half = like((2,) + near.shape[1:], near.dtype)
    return kernel_call(
        corner_kernel, [half, half], [IN_VMEM] * 2 + [ANYWHERE] * len(earlier), [], 0, 0
    )(near, got, *earlier)


def side_kernel(first, near, got, corner, _, total):
    for k in range(4):
        parts = [near[k], got[k]] + ([corner[k - first]] if first <= k < first + 2 else [])
        total[k] = wide_sum(*parts).astype(jnp.bfloat16)


def side_sum(near, got, corner, first, earlier):
    return kernel_call(
        partial(side_kernel, first),
        [like(near.shape, near.dtype)],
        [IN_VMEM] * 3 + [ANYWHERE],
        [],
        0,
        0,
    )(near, got, corner, earlier)[0]


def chip_kernel(near, got, got_x, got_y, _, mine, far, side, last):
    for k, target in enumerate((mine, far, side, last)):
        total = wide_sum(near[k], got[k], got_x[k], got_y[k])
        target[...] = total.astype(target.dtype)


def chip_sum(near, got, got_x, got_y, earlier):
    piece = near.shape[1:]
    mine, far, side, last = kernel_call(
        chip_kernel,
        [like(piece, jnp.float32)] + [like(piece, near.dtype)] * 3,
        [IN_VMEM] * 4 + [ANYWHERE],
        [],
        0,
        0,
    )(near, got, got_x, got_y, earlier)
    return mine, side, far, last


def halves_kernel(mine, got, *refs):
    keep, send = refs[-2:]
    half = keep.shape[0]
    for k in range(half):
        keep[k] = wide_sum(mine[k], got[k]).astype(keep.dtype)
        send[k] = wide_sum(mine[half + k], got[half + k]).astype(send.dtype)


def halves_sum(mine, got, *earlier):
    half = like((mine.shape[0] // 2,) + mine.shape[1:], mine.dtype)
    return kernel_call(
        halves_kernel, [half, half], [IN_VMEM] * 2 + [ANYWHERE] * len(earlier), [], 0, 0
    )(mine, got, *earlier)


def row_gradient_kernel(placed, mixed_back, attend, _, output):
    for column in range(0, placed.shape[1], 256):
        cut = slice(column, column + 256)
        output[:, cut] = placed[:, cut] + dot_nt(mixed_back[...], attend[cut, :])


def row_gradient(placed, mixed_back, attend, earlier):
    count, width = placed.shape
    return kernel_call(
        row_gradient_kernel,
        [like(placed.shape, placed.dtype)],
        [IN_VMEM] * 3 + [ANYWHERE],
        [],
        2 * count * width * 3 * width,
        0,
    )(placed, mixed_back, attend, earlier)[0]


def slopes_of(head):
    return 2.0 ** (-8.0 * (head + 1) / HEADS)


def attend_kernel(
    extra,
    rows,
    columns,
    spots,
    second_grads,
    keep,
    got,
    second_back,
    slot_sum,
    norms,
    merge,
    mixed,
    slot_attended,
    start,
    positions,
    _,
    placed,
    mixed_back,
    norm_grads,
    *refs,
):
    near, far = refs[0:4], refs[4:8]
    merge_grad, total, branch, attended_back, first_back, turned, extras = refs[8:]
    width = norms.shape[1]
    slots = 32
    length = 128
    low = jnp.bfloat16
    scale = HEAD_DIM ** (-0.5)
    xhat, inverse = norm_stats(slot_sum[...])
    incoming = keep[...] + got[...].astype(jnp.float32) + second_back[...]
    slot_back, gain_back, shift_back = norm_back(xhat, inverse, norms[0:1, :], incoming)
    norm_grads[0:1, :] = gain_back
    norm_grads[1:2, :] = shift_back
    if extra:
        both = [gain_back, shift_back, second_grads[0:1, :], second_grads[1:2, :]]
        zero_rows = jnp.zeros((EXTRA - 1, width), jnp.float32)
        for block in range(4):
            whole = jnp.concatenate([both[block], zero_rows], axis=0)
            for spot in range(8):
                turn = (8 - spot) % 8 * (width // 8)
                extras[block, spot] = (pltpu.roll(whole, turn, 1) if turn else whole).astype(low)
    first_back[...] = slot_back
    branch[...] = slot_back.astype(low)
    attended_back[...] = dot_nt(branch[...], merge[...]).astype(low)
    merge_grad[...] = dot_tn(slot_attended[...], branch[...])
    lane_head = lax.broadcasted_iota(jnp.int32, (slots, width), 1) // HEAD_DIM

    def apart_heads(block):
        zero = jnp.zeros_like(block)
        return jnp.concatenate(
            [jnp.where(lane_head == head, block, zero) for head in range(HEADS)], axis=0
        )

    def join_heads(block):
        total = jnp.zeros((slots, width), jnp.float32)
        for head in range(HEADS):
            total = jnp.where(lane_head == head, block[head * slots : (head + 1) * slots], total)
        return total

    def step(seq, carry):
        at = pl.ds(pl.multiple_of(seq * length, length), length)
        to = pl.ds(pl.multiple_of(seq * slots, slots), slots)
        spots = positions[to, :]
        selector = one_hot(spots, length)
        apart = jnp.abs(
            spots - lax.broadcasted_iota(jnp.int32, (slots, length), 1)
        ).astype(jnp.float32)
        keys = mixed[at, width : 2 * width]
        values = mixed[at, 2 * width :]
        queries = apart_heads(dot_nn(selector, mixed[at, :width])).astype(low)
        heads_back = apart_heads(attended_back[to, :].astype(jnp.float32)).astype(low)
        bias = jnp.concatenate([apart * slopes_of(head) for head in range(HEADS)], axis=0)
        scores = dot_nt(queries, keys) * scale - bias
        exp_scores = jnp.exp(scores - jnp.max(scores, axis=-1, keepdims=True))
        probs = exp_scores / jnp.sum(exp_scores, axis=-1, keepdims=True)
        probs_back = dot_nt(heads_back, values)
        inner = jnp.sum(probs * probs_back, axis=-1, keepdims=True)
        scores_back = (probs * (probs_back - inner)).astype(low)
        queries_back = (join_heads(dot_nn(scores_back, keys)) * scale).astype(low)
        mixed_back[at, :width] = dot_tn(selector, queries_back).astype(low)
        mixed_back[at, width : 2 * width] = (dot_tn(scores_back, queries) * scale).astype(low)
        mixed_back[at, 2 * width :] = dot_tn(probs.astype(low), heads_back).astype(low)
        spread = (spots == lax.broadcasted_iota(jnp.int32, (slots, length), 1)).astype(jnp.float32)
        placed[at, :] = select_exact(jnp.transpose(spread).astype(low), first_back[to, :])
        return carry

    lax.fori_loop(0, mixed.shape[0] // length, step, 0, unroll=True)
    turned[...] = start[...].T
    for core, target in ((1, far), (0, near)):
        for k in range(2):
            base = 6 * (2 * core + k)
            for part in range(2):
                column = pl.ds(pl.multiple_of(columns[base] + 256 * part, 128), 256)
                total[:, 256 * part : 256 * part + 256] = dot_nn(turned[...], mixed_back[:, column])
            column = pl.ds(pl.multiple_of(columns[base + 1], 128), 128)
            total[:, 512:640] = merge_grad[:, column]
            column = pl.ds(pl.multiple_of(columns[base + 2], 128), 128)
            single = dot_nn(turned[...], mixed_back[:, column])
            column = pl.ds(pl.multiple_of(columns[base + 3], 128), 128)
            merged = pltpu.roll(merge_grad[:, column], 64, 1)
            attend_lane = lower_lanes(single.shape) == (columns[base + 4] == 0)
            total[:, 640:] = jnp.where(attend_lane, single, merged)
            sides = target[2 * k : 2 * k + 2]
            store_pieces(total, rows, *sides)
            if extra:
                for j in range(8):
                    sides[j // 4][j % 4, width // 8 :, :] = extras[columns[base + 5], spots[j]]


def attend_back(extra, rows, columns, spots, second_grads, *blocks):
    start, mixed = blocks[8], blocks[6]
    count, width = start.shape
    slot_rows = blocks[0].shape[0]
    low = jnp.bfloat16
    return kernel_call(
        partial(attend_kernel, extra),
        [
            like((count, width), jnp.float32),
            like(mixed.shape, low),
            like((2, width), jnp.float32),
        ]
        + [like((4, width // 8 + (EXTRA if extra else 0), width), low)] * 8,
        [IN_SMEM] * 3 + [IN_VMEM] * 11 + [ANYWHERE],
        [
            pltpu.VMEM((width, width), jnp.float32),
            pltpu.VMEM((width, width), jnp.float32),
            pltpu.VMEM((slot_rows, width), low),
            pltpu.VMEM((slot_rows, width), low),
            pltpu.VMEM((slot_rows, width), jnp.float32),
            pltpu.VMEM((width, count), low),
            pltpu.VMEM((4, 8, EXTRA, width), low),
        ],
        2 * count * width * 3 * width + 10 * 4 * 384 * 128 * width,
        20 * width * width,
    )(rows, columns, spots, second_grads, *blocks)


def adamw_step(master, first, second, gradient, step_value, decay):
    step_rate = peak_rate * jnp.minimum(
        step_value / warm_steps, (total_steps - step_value) / (total_steps - warm_steps)
    )
    fix_one = 1.0 - jnp.power(jnp.float32(beta_one), step_value)
    fix_two = 1.0 - jnp.power(jnp.float32(beta_two), step_value)
    moment = beta_one * first + (1.0 - beta_one) * gradient
    squares = beta_two * second + (1.0 - beta_two) * gradient * gradient
    updated = master - step_rate * (
        moment / fix_one / (jnp.sqrt(squares / fix_two) + adam_eps) + decay * master
    )
    return (moment, squares, updated)


def shards(
    hidden_rows,
    token_table,
    masked_positions,
    masked_counts,
    replace_rows,
    masked_cotangent,
    step_number,
    attend_master,
    merge_master,
    norms_master,
    gate_master,
    value_master,
    down_master,
    first_attend,
    first_merge,
    first_norms,
    first_gate,
    first_value,
    first_down,
    second_attend,
    second_merge,
    second_norms,
    second_gate,
    second_value,
    second_down,
):
    local_seqs, slot_count = masked_positions.shape
    local_rows, model_width = hidden_rows.shape
    length = local_rows // local_seqs
    slot_rows = local_seqs * slot_count
    dp_size = lax.axis_size("dp")
    core_at = lax.axis_index("mp") & 1
    x_at = lax.axis_index("mp") >> 1
    low = jnp.bfloat16
    rows = piece_rows(model_width)

    packed = pack_columns(attend_master.astype(low), merge_master.astype(low), core_at)[None]
    small = is_small()
    wide = jnp.stack([gate_master.astype(low), value_master.astype(low)])
    deep = down_master.astype(low).T[None]

    order = [(core, k) for core in range(2) for k in range(2)]
    places = [2 * (x_at ^ k) + (core_at ^ core) for core, k in order]
    table = jnp.array(
        [
            [0, 0, 512, 128, 0, 0],
            [640, 256, 512, 128, 1, 1],
            [1152, 384, 1664, 512, 0, 2],
            [1792, 640, 1664, 512, 1, 3],
        ],
        jnp.int32,
    )
    columns = jnp.concatenate([table[place] for place in places])
    places = jnp.stack(places).astype(jnp.int32)
    spots = piece_rows(8)
    if small:
        packed = jnp.concatenate([packed, split_low(norms_master)[None]], axis=1)
        packed_z = [packed] + [flip(packed, "dp", 2 * k) for k in (2, 1, 3)]
        deep = after(deep, packed)

    live_slots = jnp.arange(slot_count, dtype=jnp.int32)[None, :] < masked_counts[:, None]
    at_slot = masked_positions[:, :, None] == jnp.arange(length, dtype=jnp.int32)[None, None, :]
    place_bool = at_slot & live_slots[:, :, None]
    chosen = jnp.take(token_table, replace_rows.reshape(-1), axis=0).reshape(
        local_seqs, slot_count, model_width
    )
    swapped = jnp.einsum(
        "sjt,sjd->std", place_bool.astype(low), chosen, preferred_element_type=jnp.float32
    ).astype(low)
    replaced = jnp.any(place_bool, axis=1)[:, :, None]
    start_rows = jnp.where(
        replaced, swapped, hidden_rows.reshape(local_seqs, length, model_width)
    ).reshape(local_rows, model_width)
    positions = masked_positions.reshape(slot_rows, 1)
    live = live_slots.astype(jnp.float32).reshape(slot_rows, 1)
    indices = [rows, places, columns, spots, positions, live]
    if small:
        deep_y, deep_x = flip_y(deep), flip_x(deep)
        deep_parts = jnp.concatenate([deep, deep_y, deep_x, flip_x(deep_y)])
        packed_z[0] = after(packed_z[0], deep_parts, start_rows, *indices)
        wide_z = gather_z(after(wide, packed_z[1]))
        packed_z = jnp.stack(packed_z)
        packed_y, packed_x = flip_y(packed_z), flip_x(packed_z)
        first_half, second_half = split_halves(packed_y, packed_x, wide_z[2])
        packed_near = [packed_z, packed_y]
        packed_far = [packed_x, flip_x(first_half), flip_y(second_half)]
        wide_z[0] = after(wide_z[0], *packed_far[1:])
        deep_z = gather_z(after(deep_parts, *wide_z[1:])[None])
        wide_z = jnp.stack(wide_z)
        wide_y, wide_x = flip_y(wide_z), flip_x(wide_z)
        norms = jnp.zeros((4, model_width), jnp.float32)
    else:
        packed_near, packed_far = gather_whole(packed)
        norms = lax.all_gather(norms_master, "dp", axis=1, tiled=True)
        norms = lax.all_gather(norms, "mp", axis=0, tiled=True)

    packed_groups = [packed_near, packed_far]
    packed_groups += [[flip_core(part) for part in group] for group in packed_groups]
    (
        attend_full,
        merge_full,
        mixed,
        normed,
        narrow,
        narrow_end,
        slot_sum,
        slot_attended,
        slot_narrow,
        norms,
    ) = first_part(
        small,
        places,
        rows,
        spots,
        start_rows,
        norms,
        positions,
        packed_groups,
    )
    if small:
        first_half, second_half = split_halves(wide_y, wide_x, narrow)
        wide_near = [wide_z, wide_y]
        wide_far = [wide_x, flip_x(first_half), flip_y(second_half)]
        deep_near = [(part, (0, side)) for side in (0, 1) for part in deep_z]
        deep_far = [(part, (0, side)) for side in (2, 3) for part in deep_z]
    else:
        wide_near, wide_far = gather_whole(wide)
        deep_near, deep_far = (with_lot(group, 0) for group in gather_whole(deep))

    def over_group(block):
        other_x = flip_x(block)
        return [block, other_x, flip_core(block), flip_core(other_x)]

    narrows = over_group(after(slot_narrow, first_half) if small else slot_narrow)

    chip_rows = (narrow, narrow_end, flip_core(narrow), flip_core(narrow_end))
    hidden = ffn_front(rows, chip_rows, wide_near, wide_far, deep_z[1] if small else rows)
    work_rows, slot_gelu, slot_slope, slot_hidden = slot_front(rows, narrows, wide_near, hidden)
    ffn_mine, ffn_other = ffn_down(rows, hidden, deep_near, deep_far, slot_hidden)
    layer_output, pulled, second_back, second_grads = second_norm(
        normed, ffn_mine, flip_core(ffn_other), norms, positions, live, masked_cotangent
    )

    keep, send, pull_rows, gate_back, value_back = ffn_back(
        rows, over_group(pulled), slot_gelu, slot_slope, wide_near, deep_near
    )
    chip_back = keep + flip_core(send)
    pair_own, pair_far, value_own, value_far = ffn_grads(
        rows, work_rows, pull_rows, gate_back, value_back, slot_hidden
    )
    if small:
        pair_got = flip_y(pair_far)
    placed, mixed_back, first_grads, *parts = attend_back(
        small,
        rows,
        columns,
        spots,
        second_grads,
        chip_back[0],
        flip_x(chip_back[1].astype(low)),
        second_back,
        slot_sum,
        norms,
        merge_full,
        mixed,
        slot_attended,
        start_rows,
        positions,
        value_far,
    )
    near, far = parts[:4], parts[4:]
    got = [flip_core(part) for part in far]
    if small:
        value_got = flip_y(after(value_far, pair_got))
        corner_a, corner_b = corner_sum(near[3], got[3], *got[:3])
        corner_x, corner_y = flip_x(corner_a), flip_y(corner_b)
        pair_keep, pair_send = halves_sum(pair_own, pair_got, corner_a)
        pair_back = flip(pair_send, "dp", 2)
        to_y = side_sum(near[1], got[1], corner_x, 0, pair_send)
        got_y = flip_y(to_y)
        value_keep, value_send = halves_sum(value_own, value_got, to_y)
        value_back = flip(value_send, "dp", 2)
        to_x = side_sum(near[2], got[2], corner_y, 2, value_send)
        got_x = flip_x(to_x)
        pair_keep, pair_send = halves_sum(pair_keep, pair_back, to_x)
        pair_grad = total_of(pair_keep[0], flip(pair_send[0], "dp", 4))
        value_keep, value_send = halves_sum(value_keep, value_back, pair_send)
        gradient_value = total_of(value_keep[0], flip(value_send[0], "dp", 4))[0]
        input_gradient = row_gradient(placed, mixed_back, attend_full, value_send)
        mine, *sent = chip_sum(near[0], got[0], got_x, got_y, value_send)
        packed_grad = total_of(mine, *[flip(sent[k - 1], "dp", 2 * k) for k in (1, 2, 3)])
        gradient_down, gradient_gate = pair_grad[0].T, pair_grad[1]
    else:
        here, across_y, across_x, corner = (add_low(near[k], got[k]) for k in range(4))
        input_gradient = row_gradient(placed, mixed_back, attend_full, placed)
        gradient_down = from_pieces(pair_own[:, 0], pair_far[:, 0]).T
        gradient_gate = from_pieces(pair_own[:, 1], pair_far[:, 1])
        gradient_value = from_pieces(value_own[:, 0], value_far[:, 0])
        packed_grad = from_pieces(
            add_low(here, flip_x(across_x)), add_low(across_y, flip_x(corner))
        )
    own_rows = attend_master.shape[0]
    gradient_attend, gradient_merge = unpack_columns(packed_grad[:own_rows], core_at)
    if small:
        gradient_norms = packed_grad[own_rows : own_rows + 1, :own_rows]
    else:
        norm_parts = jnp.concatenate([first_grads, second_grads], axis=0)
        gradient_norms = lax.psum_scatter(norm_parts, "mp", scatter_dimension=0, tiled=True)
        gradient_norms = lax.psum_scatter(gradient_norms, "dp", scatter_dimension=1, tiled=True)

    step_value = step_number[0].astype(jnp.float32)
    moment_attend, squares_attend, updated_attend = adamw_step(
        attend_master, first_attend, second_attend, gradient_attend, step_value, decay_rate
    )
    moment_merge, squares_merge, updated_merge = adamw_step(
        merge_master, first_merge, second_merge, gradient_merge, step_value, decay_rate
    )
    moment_norms, squares_norms, updated_norms = adamw_step(
        norms_master, first_norms, second_norms, gradient_norms, step_value, 0.0
    )
    moment_gate, squares_gate, updated_gate = adamw_step(
        gate_master, first_gate, second_gate, gradient_gate, step_value, decay_rate
    )
    moment_value, squares_value, updated_value = adamw_step(
        value_master, first_value, second_value, gradient_value, step_value, decay_rate
    )
    moment_down, squares_down, updated_down = adamw_step(
        down_master, first_down, second_down, gradient_down, step_value, decay_rate
    )
    return (
        layer_output,
        input_gradient,
        gradient_attend,
        gradient_merge,
        gradient_norms,
        gradient_gate,
        gradient_value,
        gradient_down,
        moment_attend,
        moment_merge,
        moment_norms,
        moment_gate,
        moment_value,
        moment_down,
        squares_attend,
        squares_merge,
        squares_norms,
        squares_gate,
        squares_value,
        squares_down,
        updated_attend,
        updated_merge,
        updated_norms,
        updated_gate,
        updated_value,
        updated_down,
    )


def solution(mesh):
    return jax.shard_map(
        shards,
        mesh=mesh,
        in_specs=(
            P(("dp", "mp"), None),
            P(),
            P(("dp", "mp"), None),
            P(("dp", "mp")),
            P(("dp", "mp"), None),
            P(("dp", "mp"), None, None),
            P(),
            P("dp", "mp"),
            P("dp", "mp"),
            P("mp", "dp"),
            P("dp", "mp"),
            P("dp", "mp"),
            P("mp", "dp"),
            P("dp", "mp"),
            P("dp", "mp"),
            P("mp", "dp"),
            P("dp", "mp"),
            P("dp", "mp"),
            P("mp", "dp"),
            P("dp", "mp"),
            P("dp", "mp"),
            P("mp", "dp"),
            P("dp", "mp"),
            P("dp", "mp"),
            P("mp", "dp"),
        ),
        out_specs=(
            P(("dp", "mp"), None),
            P(("dp", "mp"), None),
            P("dp", "mp"),
            P("dp", "mp"),
            P("mp", "dp"),
            P("dp", "mp"),
            P("dp", "mp"),
            P("mp", "dp"),
            P("dp", "mp"),
            P("dp", "mp"),
            P("mp", "dp"),
            P("dp", "mp"),
            P("dp", "mp"),
            P("mp", "dp"),
            P("dp", "mp"),
            P("dp", "mp"),
            P("mp", "dp"),
            P("dp", "mp"),
            P("dp", "mp"),
            P("mp", "dp"),
            P("dp", "mp"),
            P("dp", "mp"),
            P("mp", "dp"),
            P("dp", "mp"),
            P("dp", "mp"),
            P("mp", "dp"),
        ),
        check_vma=False,
    )
```

```python
from functools import partial

import jax
import jax.numpy as jnp
from jax import lax
from jax.experimental import pallas as pl
from jax.experimental.pallas import tpu as pltpu
from jax.sharding import PartitionSpec as P

HEADS = 12
HEAD_DIM = 64


beta_one = 0.9
beta_two = 0.999
peak_rate = 1.0
warm_steps = 4.0
total_steps = 100.0
decay_rate = 0.01
adam_eps = 1e-08
norm_eps = 1e-05


def layer_norm(row_data, gain_row, shift_row):
    centered = row_data - jnp.mean(row_data, axis=-1, keepdims=True)
    spread = jnp.mean(centered * centered, axis=-1, keepdims=True)
    return centered * lax.rsqrt(spread + norm_eps) * gain_row + shift_row


def alibi_table(head_count, seq_len):
    slopes = jnp.exp2(-8.0 * jnp.arange(1, head_count + 1, dtype=jnp.float32) / head_count)
    places = jnp.arange(seq_len, dtype=jnp.float32)
    return slopes[:, None, None] * jnp.abs(places[:, None] - places[None, :])


def dot_nn(left_op, right_op):
    return lax.dot_general(
        left_op, right_op, (((1,), (0,)), ((), ())), preferred_element_type=jnp.float32
    )


def dot_nt(left_op, right_op):
    return lax.dot_general(
        left_op, right_op, (((1,), (1,)), ((), ())), preferred_element_type=jnp.float32
    )


def dot_tn(left_op, right_op):
    return lax.dot_general(
        left_op, right_op, (((0,), (0,)), ((), ())), preferred_element_type=jnp.float32
    )


def flip(block, axis, bits):
    size = lax.axis_size(axis)
    return lax.ppermute(block, axis, [(i, i ^ bits) for i in range(size)])


def flip_core(block):
    return flip(block, "mp", 1)


def flip_x(block):
    return flip(block, "mp", 2)


def flip_y(block):
    return flip(block, "dp", 1)


def norm_stats(row_data):
    centered = row_data - jnp.mean(row_data, axis=-1, keepdims=True)
    spread = jnp.mean(centered * centered, axis=-1, keepdims=True)
    inverse = lax.rsqrt(spread + norm_eps)
    return centered * inverse, inverse


def z_groups():
    size = lax.axis_size("dp")
    return [list(range(low, size, 2)) for low in range(2)]


def pass_on(*refs):
    pass


def after(block, *others):
    return pl.pallas_call(
        pass_on,
        out_shape=jax.ShapeDtypeStruct(block.shape, block.dtype),
        in_specs=[pl.BlockSpec(memory_space=pl.ANY)] * (1 + len(others)),
        out_specs=pl.BlockSpec(memory_space=pl.ANY),
        input_output_aliases={0: 0},
        cost_estimate=pl.CostEstimate(flops=0, bytes_accessed=0, transcendentals=0),
    )(block, *others)


def is_small():
    return lax.axis_size("dp") == 8


def gather_z(block):
    far = flip(block, "dp", 4)
    return [block, far, flip(block, "dp", 2), flip(far, "dp", 2)]


def piece_rows(features):
    at = jnp.arange(8, dtype=jnp.int32)
    if is_small():
        along_z = ((at & 1) << 1) + ((at >> 1) & 1)
        at = (2 * along_z + (at >> 2)) ^ lax.axis_index("dp")
    return at * (features // 8)


def gather_whole(block):
    whole = lax.all_gather(block, "dp", axis=1, tiled=True)
    lots, features, columns = whole.shape
    whole = whole.reshape(lots, 8, features // 8, columns).transpose(1, 0, 2, 3)
    return [whole], [flip_x(whole)]


def add_low(*parts):
    return sum(part.astype(jnp.float32) for part in parts).astype(jnp.bfloat16)


def sum_dp(whole):
    return lax.psum_scatter(whole.astype(jnp.float32), "dp", scatter_dimension=0, tiled=True)


def from_pieces(*parts):
    whole = jnp.concatenate(parts, axis=0)
    return sum_dp(whole.reshape(-1, whole.shape[-1]))


MIB = 1024 * 1024
ANYWHERE = pl.BlockSpec(memory_space=pl.ANY)
IN_VMEM = pl.BlockSpec(memory_space=pltpu.VMEM)
IN_SMEM = pl.BlockSpec(memory_space=pltpu.SMEM)


def kernel_call(body, outs, specs, scratch, limit):
    return pl.pallas_call(
        body,
        out_shape=outs,
        in_specs=specs,
        out_specs=[IN_VMEM] * len(outs),
        scratch_shapes=scratch,
        compiler_params=pltpu.CompilerParams(vmem_limit_bytes=limit * MIB),
        cost_estimate=pl.CostEstimate(flops=0, bytes_accessed=0, transcendentals=0),
    )


def like(shape, dtype):
    return jax.ShapeDtypeStruct(shape, dtype)


def with_lot(groups, lot):
    return [(group, (i, lot)) for group in groups for i in range(group.shape[0])]


def load_pieces(pieces, rows, total, sems):
    copies = []
    count = total.shape[0] // 8
    for k, (group, at) in enumerate(pieces):
        to = total.at[pl.ds(pl.multiple_of(rows[k], 32), count), :]
        copies.append(pltpu.make_async_copy(group.at[(*at, pl.ds(0, count))], to, sems.at[k]))
        copies[-1].start()
    return copies


EXTRA = 16


def load_extras(groups, spots, total, sems):
    copies = []
    for group in groups:
        for i in range(group.shape[0]):
            k = len(copies)
            source = group.at[i, 0, pl.ds(group.shape[2] - EXTRA, EXTRA), :]
            copies.append(pltpu.make_async_copy(source, total.at[spots[k]], sems.at[k]))
            copies[-1].start()
    return copies


def split_low(block):
    parts = []
    for _ in range(3):
        part = lax.reduce_precision(block, 8, 7)
        parts.append(jnp.pad(part.astype(jnp.bfloat16), ((0, EXTRA - 1), (0, 128 - block.shape[1]))))
        block = block - part
    return jnp.pad(jnp.concatenate(parts, axis=1), ((0, 0), (0, 384)))


def wait_all(copies):
    for copy in copies:
        copy.wait()


def gelu_parts(gated):
    below = 0.5 + 0.5 * lax.erf(gated * 0.7071067811865476)
    return gated * below, below


def lower_lanes(shape):
    return lax.broadcasted_iota(jnp.int32, shape, 1) < 64


def unpack_columns_of(blocks, attend, merge):
    for block, (column, merge_column) in enumerate(((0, 0), (640, 256), (1152, 384), (1792, 640))):
        attend[:, column : column + 512] = blocks[block, :, :512]
        merge[:, merge_column : merge_column + 128] = blocks[block, :, 512:640]
    for pair, (column, merge_column) in enumerate(((512, 128), (1664, 512))):
        even = blocks[2 * pair, :, 640:].astype(jnp.float32)
        odd = blocks[2 * pair + 1, :, 640:].astype(jnp.float32)
        lower = lower_lanes(even.shape)
        attend[:, column : column + 128] = jnp.where(lower, even, odd).astype(jnp.bfloat16)
        mixed_up = pltpu.roll(jnp.where(lower, odd, even), 64, 1)
        merge[:, merge_column : merge_column + 128] = mixed_up.astype(jnp.bfloat16)


def first_kernel(counts, extra, places, rows, spots, start, norms_given, positions, *refs):
    low = jnp.bfloat16
    groups = []
    for count in counts:
        groups.append(refs[:count])
        refs = refs[count:]
    attend, merge, mixed, normed, *narrow, slot_sum, slot_attended, slot_narrow, norms = refs[:10]
    blocks, attended, scores, extras, sems = refs[10:]
    copies = []
    for at, group in enumerate(groups):
        copies += load_pieces(with_lot(group, 0), rows, blocks.at[places[at]], sems.at[0, at])
        if extra:
            copies += load_extras(group, spots, extras.at[places[at]], sems.at[1, at])
    wait_all(copies)
    if extra:
        for block in range(4):
            whole = jnp.zeros((8, norms.shape[1]), jnp.float32)
            for spot in range(8):
                parts = extras[block, spot].astype(jnp.float32)[:8, :]
                value = parts[:, :128] + parts[:, 128:256] + parts[:, 256:384]
                value = jnp.concatenate([value, jnp.zeros((8, norms.shape[1] - 128), jnp.float32)], axis=1)
                whole = whole + (pltpu.roll(value, spot * (norms.shape[1] // 8), 1) if spot else value)
            norms[block : block + 1, :] = whole[:1, :]
    else:
        norms[...] = norms_given[...]
    unpack_columns_of(blocks, attend, merge)
    width = merge.shape[0]
    length = 128
    slots = 32
    scale = HEAD_DIM ** (-0.5)
    for column in range(0, 3 * width, 256):
        cut = slice(column, column + 256)
        mixed[:, cut] = dot_nn(start[...], attend[:, cut]).astype(low)
    shape = (length, length)
    apart = jnp.abs(
        lax.broadcasted_iota(jnp.int32, shape, 0) - lax.broadcasted_iota(jnp.int32, shape, 1)
    ).astype(jnp.float32)
    lower = lower_lanes(shape)

    def step(target, first, seq, carry):
        at = pl.ds(pl.multiple_of(seq * length, length), length)
        to = pl.ds(pl.multiple_of(seq * slots, slots), slots)
        for pair in range(HEADS // 2):
            column = 2 * HEAD_DIM * pair
            queries = mixed[at, column : column + 128]
            keys = mixed[at, width + column : width + column + 128]
            zero = jnp.zeros_like(queries)
            for half in range(2):
                own = jnp.where(lower, queries, zero) if half == 0 else jnp.where(lower, zero, queries)
                head = 2 * pair + half
                scores[head] = dot_nt(own, keys) * scale - apart * slopes_of(head)
        raised = scores[...]
        raised = jnp.exp(raised - jnp.max(raised, axis=-1, keepdims=True))
        scores[...] = raised / jnp.sum(raised, axis=-1, keepdims=True)
        for pair in range(HEADS // 2):
            column = 2 * HEAD_DIM * pair
            values = mixed[at, 2 * width + column : 2 * width + column + 128]
            heads = [dot_nn(scores[2 * pair + half].astype(low), values) for half in range(2)]
            attended[at, column : column + 128] = jnp.where(lower, heads[0], heads[1]).astype(low)
        total = start[at, :].astype(jnp.float32) + dot_nn(attended[at, :], merge[...])
        xhat, _ = norm_stats(total)
        rows = xhat * norms[0:1, :] + norms[1:2, :]
        normed[at, :] = rows
        target[pl.ds(pl.multiple_of((seq - first) * length, length), length), :] = rows.astype(low)
        selector = one_hot(positions[to, :], length)
        slot_sum[to, :] = select_exact(selector, total)
        slot_attended[to, :] = dot_nn(selector, attended[at, :]).astype(low)
        slot_narrow[to, :] = dot_nn(selector, rows.astype(low)).astype(low)
        return carry

    seqs = start.shape[0] // length // 2
    lax.fori_loop(0, seqs, partial(step, narrow[0], 0), 0, unroll=True)
    lax.fori_loop(seqs, 2 * seqs, partial(step, narrow[1], seqs), 0, unroll=True)


def first_part(extra, places, rows, spots, start, norms, positions, groups):
    count, width = start.shape
    slot_rows = positions.shape[0]
    low = jnp.bfloat16
    return kernel_call(
        partial(first_kernel, [len(group) for group in groups], extra),
        [
            like((width, 3 * width), low),
            like((width, width), low),
            like((count, 3 * width), low),
            like((count, width), jnp.float32),
            like((count // 2, width), low),
            like((count // 2, width), low),
            like((slot_rows, width), jnp.float32),
            like((slot_rows, width), low),
            like((slot_rows, width), low),
            like((4, width), jnp.float32),
        ],
        [IN_SMEM] * 3 + [IN_VMEM] * 3 + [ANYWHERE] * sum(map(len, groups)),
        [
            pltpu.VMEM((4, width, width), low),
            pltpu.VMEM((count, width), low),
            pltpu.VMEM((HEADS, 128, 128), jnp.float32),
            pltpu.VMEM((4, 8, EXTRA, width), low),
            pltpu.SemaphoreType.DMA((2, 4, 8)),
        ], 30)(places, rows, spots, start, norms, positions, *sum(groups, []))


def pack_columns(attend, merge, core_at):
    even = jnp.concatenate(
        [attend[:, :512], merge[:, :128], attend[:, 512:], merge[:, 128:]], axis=1
    )
    odd = jnp.concatenate([attend[:, 64:], merge[:, 64:], merge[:, :64], attend[:, :64]], axis=1)
    return jnp.where(core_at == 0, even, odd)


def unpack_columns(packed, core_at):
    even = jnp.concatenate([packed[:, :512], packed[:, 640:704]], axis=1)
    odd = jnp.concatenate([packed[:, 704:], packed[:, :512]], axis=1)
    even_merge = jnp.concatenate([packed[:, 512:640], packed[:, 704:]], axis=1)
    odd_merge = jnp.concatenate([packed[:, 640:704], packed[:, 512:640]], axis=1)
    return jnp.where(core_at == 0, even, odd), jnp.where(core_at == 0, even_merge, odd_merge)


def front_kernel(count, rows, *refs):
    sources, refs = refs[:4], refs[4:]
    near, far = refs[: count[0]], refs[count[0] : count[0] + count[1]]
    hidden, gates, values, sems = refs[-4:]
    copies = []
    for k, groups in enumerate((near, far)):
        copies.append(
            load_pieces(with_lot(groups, 0), rows, gates.at[k], sems.at[k, 0])
            + load_pieces(with_lot(groups, 1), rows, values.at[k], sems.at[k, 1])
        )
    quarter = sources[0].shape[0]
    for k in range(2):
        wait_all(copies[k])
        for part, source in enumerate(sources):
            start = part * quarter

            def step(tile, carry, k=k, start=start, source=source):
                block = source[pl.ds(pl.multiple_of(tile * 256, 256), 256), :]
                to = pl.ds(pl.multiple_of(start + tile * 256, 256), 256)
                for column in range(0, gates.shape[2], 256):
                    cut = slice(column, column + 256)
                    gated = dot_nn(block, gates[k, :, cut])
                    valued = dot_nn(block, values[k, :, cut])
                    hidden[k, to, cut] = (gelu_parts(gated)[0] * valued).astype(jnp.bfloat16)
                return carry

            lax.fori_loop(0, source.shape[0] // 256, step, 0)


def ffn_front(rows, sources, near, far, *earlier):
    quarter, width = sources[0].shape
    return kernel_call(
        partial(front_kernel, (len(near), len(far))),
        [like((2, 4 * quarter, width), jnp.bfloat16)],
        [IN_SMEM] + [IN_VMEM] * 4 + [ANYWHERE] * (len(near) + len(far) + len(earlier)),
        [
            pltpu.VMEM((2, width, width), jnp.bfloat16),
            pltpu.VMEM((2, width, width), jnp.bfloat16),
            pltpu.SemaphoreType.DMA((2, 2, 8)),
        ], 18)(rows, *sources, *near, *far, *earlier)[0]


def down_kernel(lots, rows, hidden, *refs):
    split, end = len(lots[0]), len(lots[0]) + len(lots[1])
    mine, other, downs, sems = refs[end + 1 :]
    copies = load_pieces(zip(refs[:split], lots[0]), rows, downs.at[0], sems.at[0])
    copies += load_pieces(zip(refs[split:end], lots[1]), rows, downs.at[1], sems.at[1])
    wait_all(copies)
    half = mine.shape[0]
    for column in range(0, downs.shape[1], 256):
        cut = slice(column, column + 256)
        total = dot_nt(hidden[0], downs[0, cut, :]) + dot_nt(hidden[1], downs[1, cut, :])
        mine[:, cut] = total[:half]
        other[:, cut] = total[half:]


def ffn_down(rows, hidden, near, far, earlier):
    both, width = hidden.shape[1:]
    return kernel_call(
        partial(down_kernel, [[lot for _, lot in group] for group in (near, far)]),
        [like((both // 2, width), jnp.float32)] * 2,
        [IN_SMEM, IN_VMEM] + [ANYWHERE] * (len(near) + len(far) + 1),
        [pltpu.VMEM((2, width, width), jnp.bfloat16), pltpu.SemaphoreType.DMA((2, 8))], 16)(rows, hidden, *[group for group, _ in near + far], earlier)


def select_exact(selector, block):
    first = block.astype(jnp.bfloat16)
    rest = block - first.astype(jnp.float32)
    second = rest.astype(jnp.bfloat16)
    third = (rest - second.astype(jnp.float32)).astype(jnp.bfloat16)
    return dot_nn(selector, first) + dot_nn(selector, second) + dot_nn(selector, third)


def norm_back(xhat, inverse, gain_row, incoming):
    scaled = incoming * gain_row
    inner = jnp.mean(scaled * xhat, axis=-1, keepdims=True)
    back = inverse * (scaled - jnp.mean(scaled, axis=-1, keepdims=True) - xhat * inner)
    gain_back = jnp.sum(incoming * xhat, axis=0, keepdims=True)
    return back, gain_back, jnp.sum(incoming, axis=0, keepdims=True)


def one_hot(positions, length):
    shape = (positions.shape[0], length)
    return (positions == lax.broadcasted_iota(jnp.int32, shape, 1)).astype(jnp.bfloat16)


def second_kernel(
    normed, part, got, norms, positions, live, cotangent, output, pulled, back, norm_grads
):
    slots = cotangent.shape[1]
    length = normed.shape[0] // cotangent.shape[0]
    norm_grads[...] = jnp.zeros_like(norm_grads)

    def step(seq, carry):
        at = pl.ds(pl.multiple_of(seq * length, length), length)
        to = pl.ds(pl.multiple_of(seq * slots, slots), slots)
        total = normed[at, :] + part[at, :] + got[at, :]
        xhat, _ = norm_stats(total)
        output[at, :] = (xhat * norms[2:3, :] + norms[3:4, :]).astype(jnp.bfloat16)
        selector = one_hot(positions[to, :], length)
        xhat, inverse = norm_stats(select_exact(selector, total))
        incoming = jnp.where(live[to, :] > 0, cotangent[seq].astype(jnp.float32), 0.0)
        slot_back, gain_back, shift_back = norm_back(xhat, inverse, norms[2:3, :], incoming)
        back[to, :] = slot_back
        pulled[to, :] = slot_back.astype(jnp.bfloat16)
        norm_grads[0:1, :] += gain_back
        norm_grads[1:2, :] += shift_back
        return carry

    lax.fori_loop(0, cotangent.shape[0], step, 0, unroll=True)


def second_norm(normed, part, got, norms, positions, live, cotangent):
    count, width = normed.shape
    slot_rows = positions.shape[0]
    return kernel_call(
        second_kernel,
        [
            like((count, width), jnp.bfloat16),
            like((slot_rows, width), jnp.bfloat16),
            like((slot_rows, width), jnp.float32),
            like((2, width), jnp.float32),
        ],
        [IN_VMEM] * 7,
        [], 14)(normed, part, got, norms, positions, live, cotangent)


def back_kernel(count, lots, rows, *refs):
    pulls, narrows = refs[0:4], refs[4:8]
    wide, deep = refs[8 : 8 + count[0]], refs[8 + count[0] : 8 + count[0] + count[1]]
    keep, send, pull_rows, work_rows, gate_back, value_back, hidden = refs[
        8 + count[0] + count[1] : -4
    ]
    gates, values, downs, sems = refs[-4:]
    copies = load_pieces(with_lot(wide, 0), rows, gates, sems.at[0])
    copies += load_pieces(with_lot(wide, 1), rows, values, sems.at[1])
    copies += load_pieces(zip(deep, lots), rows, downs, sems.at[2])
    size = pulls[0].shape[0]
    for k in range(4):
        pull_rows[k * size : (k + 1) * size, :] = pulls[k][...]
        work_rows[k * size : (k + 1) * size, :] = narrows[k][...]
    wait_all(copies)
    for column in range(0, gates.shape[1], 256):
        cut = slice(column, column + 256)
        gated = dot_nn(work_rows[...], gates[:, cut])
        valued = dot_nn(work_rows[...], values[:, cut])
        hidden_back = dot_nn(pull_rows[...], downs[:, cut])
        gelu, below = gelu_parts(gated)
        slope = below + gated * (0.3989422804014327 * jnp.exp(-0.5 * gated * gated))
        hidden[:, cut] = (gelu * valued).astype(jnp.bfloat16)
        gate_back[:, cut] = (hidden_back * valued * slope).astype(jnp.bfloat16)
        value_back[:, cut] = (hidden_back * gelu).astype(jnp.bfloat16)
    for column in range(0, gates.shape[0], 256):
        cut = slice(column, column + 256)
        total = dot_nt(gate_back[...], gates[cut, :]) + dot_nt(value_back[...], values[cut, :])
        for k, target in enumerate((keep, keep, send, send)):
            target[k % 2, :, cut] = total[k * size : (k + 1) * size]


def ffn_back(rows, pulls, narrows, wide, deep):
    size, width = pulls[0].shape
    low = jnp.bfloat16
    return kernel_call(
        partial(back_kernel, (len(wide), len(deep)), [lot for _, lot in deep]),
        [like((2, size, width), jnp.float32)] * 2 + [like((4 * size, width), low)] * 5,
        [IN_SMEM] + [IN_VMEM] * 8 + [ANYWHERE] * (len(wide) + len(deep)),
        [pltpu.VMEM((width, width), low)] * 3 + [pltpu.SemaphoreType.DMA((3, 8))], 22)(rows, *pulls, *narrows, *wide, *[group for group, _ in deep])


def store_pieces(total, rows, mine, other):
    count = total.shape[0] // 8
    for k in range(8):
        at = pl.ds(pl.multiple_of(rows[k], 32), count)
        to = mine if k < 4 else other
        to[k % 4, :count, :] = total[at, :]


def grads_kernel(lots, rows, *refs):
    factors, refs = refs[: 2 * lots], refs[-3 - lots :]
    mine, other, total, turned = refs[0], refs[1], refs[2], refs[3:]
    for lot in range(lots):
        turned[lot][...] = factors[2 * lot][...].T
    for lot in range(lots):
        for column in range(0, total.shape[1], 256):
            cut = slice(column, column + 256)
            product = dot_nn(turned[lot][...], factors[2 * lot + 1][:, cut])
            total[:, cut] = product.astype(jnp.bfloat16)
        store_pieces(total, rows, mine.at[:, lot], other.at[:, lot])


def ffn_grads(rows, factors, *earlier):
    size, width = factors[0].shape
    lots = len(factors) // 2
    low = jnp.bfloat16
    return kernel_call(
        partial(grads_kernel, lots),
        [like((4, lots, width // 8, width), low)] * 2,
        [IN_SMEM] + [IN_VMEM] * len(factors) + [ANYWHERE] * len(earlier),
        [pltpu.VMEM((width, width), low)] + [pltpu.VMEM((width, size), low)] * lots, 16)(rows, *factors, *earlier)


def split_kernel(from_y, from_x, *refs):
    first, second, sems = refs[-3:]
    half = first.shape[0]
    copies = [
        pltpu.make_async_copy(from_y.at[pl.ds(0, half)], first, sems.at[0]),
        pltpu.make_async_copy(from_x.at[pl.ds(half, half)], second, sems.at[1]),
    ]
    for copy in copies:
        copy.start()
    wait_all(copies)


def split_halves(from_y, from_x, *earlier):
    half = like((from_y.shape[0] // 2,) + from_y.shape[1:], from_y.dtype)
    return kernel_call(
        split_kernel,
        [half, half],
        [ANYWHERE] * (2 + len(earlier)),
        [pltpu.SemaphoreType.DMA((2,))], 6)(from_y, from_x, *earlier)


def cast_kernel(first, second, _, both):
    both[0] = first[...].astype(jnp.bfloat16)
    both[1] = second[...].astype(jnp.bfloat16)


def cast_wide(first, second, earlier):
    return kernel_call(
        cast_kernel,
        [like((2,) + first.shape, jnp.bfloat16)],
        [IN_VMEM] * 2 + [ANYWHERE],
        [], 4)(first, second, earlier)[0]


def wide_sum(*blocks):
    return sum(block.astype(jnp.float32) for block in blocks)


def total_of(*blocks):
    return wide_sum(*blocks)


def corner_kernel(near, got, *refs):
    first, second = refs[-2:]
    for k in range(4):
        target = first if k < 2 else second
        target[k % 2] = wide_sum(near[k], got[k]).astype(jnp.bfloat16)


def corner_sum(near, got, *earlier):
    half = like((2,) + near.shape[1:], near.dtype)
    return kernel_call(
        corner_kernel, [half, half], [IN_VMEM] * 2 + [ANYWHERE] * len(earlier), [], 6)(near, got, *earlier)


def sides_kernel(near_y, got_y, near_x, got_x, corner_x, corner_y, _, to_x, to_y):
    for k in range(4):
        corner = [corner_x[k]] if k < 2 else []
        to_y[k] = wide_sum(near_y[k], got_y[k], *corner).astype(jnp.bfloat16)
        corner = [corner_y[k - 2]] if k >= 2 else []
        to_x[k] = wide_sum(near_x[k], got_x[k], *corner).astype(jnp.bfloat16)


def sides_sum(near, got, corner_x, corner_y, earlier):
    side = like(near[1].shape, near[1].dtype)
    return kernel_call(sides_kernel, [side, side], [IN_VMEM] * 6 + [ANYWHERE], [], 10)(
        near[1], got[1], near[2], got[2], corner_x, corner_y, earlier
    )


def chip_kernel(near, got, got_x, got_y, _, mine, far, side, last):
    for k, target in enumerate((mine, far, side, last)):
        total = wide_sum(near[k], got[k], got_x[k], got_y[k])
        target[...] = total.astype(target.dtype)


def chip_sum(near, got, got_x, got_y, earlier):
    piece = near.shape[1:]
    mine, far, side, last = kernel_call(
        chip_kernel,
        [like(piece, jnp.float32)] + [like(piece, near.dtype)] * 3,
        [IN_VMEM] * 4 + [ANYWHERE],
        [], 8)(near, got, got_x, got_y, earlier)
    return mine, side, far, last


def halves_kernel(mine, got, *refs):
    keep, send = refs[-2:]
    half = keep.shape[0]
    for k in range(half):
        keep[k] = wide_sum(mine[k], got[k]).astype(keep.dtype)
        send[k] = wide_sum(mine[half + k], got[half + k]).astype(send.dtype)


def halves_sum(mine, got, *earlier):
    half = like((mine.shape[0] // 2,) + mine.shape[1:], mine.dtype)
    return kernel_call(
        halves_kernel, [half, half], [IN_VMEM] * 2 + [ANYWHERE] * len(earlier), [], 8)(mine, got, *earlier)


def row_gradient_kernel(placed, mixed_back, attend, _, output):
    for column in range(0, placed.shape[1], 256):
        cut = slice(column, column + 256)
        output[:, cut] = placed[:, cut] + dot_nt(mixed_back[...], attend[cut, :])


def row_gradient(placed, mixed_back, attend, earlier):
    count, width = placed.shape
    return kernel_call(
        row_gradient_kernel,
        [like(placed.shape, placed.dtype)],
        [IN_VMEM] * 3 + [ANYWHERE],
        [], 14)(placed, mixed_back, attend, earlier)[0]


def slopes_of(head):
    return 2.0 ** (-8.0 * (head + 1) / HEADS)


def attend_kernel(
    extra,
    rows,
    columns,
    spots,
    second_grads,
    keep,
    got,
    second_back,
    slot_sum,
    norms,
    merge,
    mixed,
    slot_attended,
    start,
    positions,
    _,
    placed,
    mixed_back,
    norm_grads,
    *refs,
):
    near, far = refs[0:4], refs[4:8]
    merge_grad, total, branch, attended_back, first_back, turned, extras = refs[8:]
    width = norms.shape[1]
    slots = 32
    length = 128
    low = jnp.bfloat16
    scale = HEAD_DIM ** (-0.5)
    xhat, inverse = norm_stats(slot_sum[...])
    incoming = keep[...] + got[...].astype(jnp.float32) + second_back[...]
    slot_back, gain_back, shift_back = norm_back(xhat, inverse, norms[0:1, :], incoming)
    norm_grads[0:1, :] = gain_back
    norm_grads[1:2, :] = shift_back
    if extra:
        both = [gain_back, shift_back, second_grads[0:1, :], second_grads[1:2, :]]
        zero_rows = jnp.zeros((EXTRA - 1, width), jnp.float32)
        for block in range(4):
            whole = jnp.concatenate([both[block], zero_rows], axis=0)
            for spot in range(8):
                turn = (8 - spot) % 8 * (width // 8)
                extras[block, spot] = (pltpu.roll(whole, turn, 1) if turn else whole).astype(low)
    first_back[...] = slot_back
    branch[...] = slot_back.astype(low)
    attended_back[...] = dot_nt(branch[...], merge[...]).astype(low)
    merge_grad[...] = dot_tn(slot_attended[...], branch[...])
    lane_head = lax.broadcasted_iota(jnp.int32, (slots, width), 1) // HEAD_DIM

    def apart_heads(block):
        zero = jnp.zeros_like(block)
        return jnp.concatenate(
            [jnp.where(lane_head == head, block, zero) for head in range(HEADS)], axis=0
        )

    def join_heads(block):
        total = jnp.zeros((slots, width), jnp.float32)
        for head in range(HEADS):
            total = jnp.where(lane_head == head, block[head * slots : (head + 1) * slots], total)
        return total

    def step(seq, carry):
        at = pl.ds(pl.multiple_of(seq * length, length), length)
        to = pl.ds(pl.multiple_of(seq * slots, slots), slots)
        spots = positions[to, :]
        selector = one_hot(spots, length)
        apart = jnp.abs(
            spots - lax.broadcasted_iota(jnp.int32, (slots, length), 1)
        ).astype(jnp.float32)
        keys = mixed[at, width : 2 * width]
        values = mixed[at, 2 * width :]
        queries = apart_heads(dot_nn(selector, mixed[at, :width])).astype(low)
        heads_back = apart_heads(attended_back[to, :].astype(jnp.float32)).astype(low)
        bias = jnp.concatenate([apart * slopes_of(head) for head in range(HEADS)], axis=0)
        scores = dot_nt(queries, keys) * scale - bias
        exp_scores = jnp.exp(scores - jnp.max(scores, axis=-1, keepdims=True))
        probs = exp_scores / jnp.sum(exp_scores, axis=-1, keepdims=True)
        probs_back = dot_nt(heads_back, values)
        inner = jnp.sum(probs * probs_back, axis=-1, keepdims=True)
        scores_back = (probs * (probs_back - inner)).astype(low)
        queries_back = (join_heads(dot_nn(scores_back, keys)) * scale).astype(low)
        mixed_back[at, :width] = dot_tn(selector, queries_back).astype(low)
        mixed_back[at, width : 2 * width] = (dot_tn(scores_back, queries) * scale).astype(low)
        mixed_back[at, 2 * width :] = dot_tn(probs.astype(low), heads_back).astype(low)
        spread = (spots == lax.broadcasted_iota(jnp.int32, (slots, length), 1)).astype(jnp.float32)
        placed[at, :] = select_exact(jnp.transpose(spread).astype(low), first_back[to, :])
        return carry

    lax.fori_loop(0, mixed.shape[0] // length, step, 0, unroll=True)
    turned[...] = start[...].T
    for core, target in ((1, far), (0, near)):
        for k in range(2):
            base = 6 * (2 * core + k)
            for part in range(2):
                column = pl.ds(pl.multiple_of(columns[base] + 256 * part, 128), 256)
                product = dot_nn(turned[...], mixed_back[:, column])
                total[:, 256 * part : 256 * part + 256] = product.astype(low)
            column = pl.ds(pl.multiple_of(columns[base + 1], 128), 128)
            total[:, 512:640] = merge_grad[:, column].astype(low)
            column = pl.ds(pl.multiple_of(columns[base + 2], 128), 128)
            single = dot_nn(turned[...], mixed_back[:, column])
            column = pl.ds(pl.multiple_of(columns[base + 3], 128), 128)
            merged = pltpu.roll(merge_grad[:, column], 64, 1)
            attend_lane = lower_lanes(single.shape) == (columns[base + 4] == 0)
            total[:, 640:] = jnp.where(attend_lane, single, merged).astype(low)
            sides = target[2 * k : 2 * k + 2]
            store_pieces(total, rows, *sides)
            if extra:
                for j in range(8):
                    sides[j // 4][j % 4, width // 8 :, :] = extras[columns[base + 5], spots[j]]


def attend_back(extra, rows, columns, spots, second_grads, *blocks):
    start, mixed = blocks[8], blocks[6]
    count, width = start.shape
    slot_rows = blocks[0].shape[0]
    low = jnp.bfloat16
    return kernel_call(
        partial(attend_kernel, extra),
        [
            like((count, width), jnp.float32),
            like(mixed.shape, low),
            like((2, width), jnp.float32),
        ]
        + [like((4, width // 8 + (EXTRA if extra else 0), width), low)] * 8,
        [IN_SMEM] * 3 + [IN_VMEM] * 11 + [ANYWHERE],
        [
            pltpu.VMEM((width, width), jnp.float32),
            pltpu.VMEM((width, width), low),
            pltpu.VMEM((slot_rows, width), low),
            pltpu.VMEM((slot_rows, width), low),
            pltpu.VMEM((slot_rows, width), jnp.float32),
            pltpu.VMEM((width, count), low),
            pltpu.VMEM((4, 8, EXTRA, width), low),
        ], 32)(rows, columns, spots, second_grads, *blocks)


def adamw_step(master, first, second, gradient, step_value, decay):
    step_rate = peak_rate * jnp.minimum(
        step_value / warm_steps, (total_steps - step_value) / (total_steps - warm_steps)
    )
    fix_one = 1.0 - jnp.power(jnp.float32(beta_one), step_value)
    fix_two = 1.0 - jnp.power(jnp.float32(beta_two), step_value)
    moment = beta_one * first + (1.0 - beta_one) * gradient
    squares = beta_two * second + (1.0 - beta_two) * gradient * gradient
    updated = master - step_rate * (
        moment / fix_one / (jnp.sqrt(squares / fix_two) + adam_eps) + decay * master
    )
    return (moment, squares, updated)


def shards(
    hidden_rows,
    token_table,
    masked_positions,
    masked_counts,
    replace_rows,
    masked_cotangent,
    step_number,
    attend_master,
    merge_master,
    norms_master,
    gate_master,
    value_master,
    down_master,
    first_attend,
    first_merge,
    first_norms,
    first_gate,
    first_value,
    first_down,
    second_attend,
    second_merge,
    second_norms,
    second_gate,
    second_value,
    second_down,
):
    local_seqs, slot_count = masked_positions.shape
    local_rows, model_width = hidden_rows.shape
    length = local_rows // local_seqs
    slot_rows = local_seqs * slot_count
    dp_size = lax.axis_size("dp")
    core_at = lax.axis_index("mp") & 1
    x_at = lax.axis_index("mp") >> 1
    low = jnp.bfloat16
    rows = piece_rows(model_width)

    packed = pack_columns(attend_master.astype(low), merge_master.astype(low), core_at)[None]
    small = is_small()
    deep = down_master.astype(low).T[None]

    order = [(core, k) for core in range(2) for k in range(2)]
    places = [2 * (x_at ^ k) + (core_at ^ core) for core, k in order]
    table = jnp.array(
        [
            [0, 0, 512, 128, 0, 0],
            [640, 256, 512, 128, 1, 1],
            [1152, 384, 1664, 512, 0, 2],
            [1792, 640, 1664, 512, 1, 3],
        ],
        jnp.int32,
    )
    columns = jnp.concatenate([table[place] for place in places])
    places = jnp.stack(places).astype(jnp.int32)
    spots = piece_rows(8)
    if small:
        packed = jnp.concatenate([packed, split_low(norms_master)[None]], axis=1)
        packed_z = [packed] + [flip(packed, "dp", 2 * k) for k in (2, 1, 3)]
        wide = cast_wide(gate_master, value_master, packed_z[2])

    live_slots = jnp.arange(slot_count, dtype=jnp.int32)[None, :] < masked_counts[:, None]
    at_slot = masked_positions[:, :, None] == jnp.arange(length, dtype=jnp.int32)[None, None, :]
    place_bool = at_slot & live_slots[:, :, None]
    chosen = jnp.take(token_table, replace_rows.reshape(-1), axis=0).reshape(
        local_seqs, slot_count, model_width
    )
    swapped = jnp.einsum(
        "sjt,sjd->std", place_bool.astype(low), chosen, preferred_element_type=jnp.float32
    ).astype(low)
    replaced = jnp.any(place_bool, axis=1)[:, :, None]
    start_rows = jnp.where(
        replaced, swapped, hidden_rows.reshape(local_seqs, length, model_width)
    ).reshape(local_rows, model_width)
    positions = masked_positions.reshape(slot_rows, 1)
    live = live_slots.astype(jnp.float32).reshape(slot_rows, 1)
    indices = [rows, places, columns, spots, positions, live]
    if small:
        deep = after(deep, start_rows)
        deep_y, deep_x = flip_y(deep), flip_x(deep)
        deep_parts = jnp.concatenate([deep, deep_y, deep_x, flip_x(deep_y)])
        packed_z[0] = after(packed_z[0], wide, deep_parts, *indices)
        wide_z = gather_z(after(wide, packed_z[1], packed_z[3]))
        packed_z = jnp.stack(packed_z)
        packed_y, packed_x = flip_y(packed_z), flip_x(packed_z)
        first_half, second_half = split_halves(packed_y, packed_x, wide_z[1], wide_z[2])
        packed_near = [packed_z, packed_y]
        packed_far = [packed_x, flip_x(first_half), flip_y(second_half)]
        wide_z[0] = after(wide_z[0], *packed_far[1:])
        deep_z = gather_z(after(deep_parts, *wide_z[1:])[None])
        wide_z = jnp.stack(wide_z)
        wide_y, wide_x = flip_y(wide_z), flip_x(wide_z)
        norms = jnp.zeros((4, model_width), jnp.float32)
    else:
        packed_near, packed_far = gather_whole(packed)
        norms = lax.all_gather(norms_master, "dp", axis=1, tiled=True)
        norms = lax.all_gather(norms, "mp", axis=0, tiled=True)

    packed_groups = [packed_near, packed_far]
    packed_groups += [[flip_core(part) for part in group] for group in packed_groups]
    (
        attend_full,
        merge_full,
        mixed,
        normed,
        narrow,
        narrow_end,
        slot_sum,
        slot_attended,
        slot_narrow,
        norms,
    ) = first_part(
        small,
        places,
        rows,
        spots,
        start_rows,
        norms,
        positions,
        packed_groups,
    )
    if small:
        first_half, second_half = split_halves(wide_y, wide_x, narrow)
        wide_near = [wide_z, wide_y]
        wide_far = [wide_x, flip_x(first_half), flip_y(second_half)]
        deep_near = [(part, (0, side)) for side in (0, 1) for part in deep_z]
        deep_far = [(part, (0, side)) for side in (2, 3) for part in deep_z]
    else:
        wide_near, wide_far = gather_whole(
            jnp.stack([gate_master.astype(low), value_master.astype(low)])
        )
        deep_near, deep_far = (with_lot(group, 0) for group in gather_whole(deep))

    def over_group(block):
        other_x = flip_x(block)
        return [block, other_x, flip_core(block), flip_core(other_x)]


    chip_rows = (narrow, narrow_end, flip_core(narrow), flip_core(narrow_end))
    earlier = [deep_z[1] if small else rows]
    hidden = ffn_front(rows, chip_rows, wide_near, wide_far, *earlier)
    narrows = over_group(after(slot_narrow, hidden))
    ffn_mine, ffn_other = ffn_down(rows, hidden, deep_near, deep_far, rows)
    layer_output, pulled, second_back, second_grads = second_norm(
        normed, ffn_mine, flip_core(ffn_other), norms, positions, live, masked_cotangent
    )

    keep, send, *factors = ffn_back(rows, over_group(pulled), narrows, wide_near, deep_near)
    pull_rows, work_rows, gate_back, value_back, slot_hidden = factors
    chip_back = keep + flip_core(send)
    pair_own, pair_far = ffn_grads(rows, (pull_rows, slot_hidden, work_rows, gate_back))
    value_own, value_far = ffn_grads(rows, (work_rows, value_back), pair_own)
    if small:
        pair_got = flip_y(pair_far)
    placed, mixed_back, first_grads, *parts = attend_back(
        small,
        rows,
        columns,
        spots,
        second_grads,
        chip_back[0],
        flip_x(chip_back[1].astype(low)),
        second_back,
        slot_sum,
        norms,
        merge_full,
        mixed,
        slot_attended,
        start_rows,
        positions,
        value_far,
    )
    near, far = parts[:4], parts[4:]
    got = [flip_core(part) for part in far]
    if small:
        value_got = flip_y(after(value_far, pair_got))
        corner_a, corner_b = corner_sum(near[3], got[3], *got[:3])
        corner_x, corner_y = flip_x(corner_a), flip_y(corner_b)
        pair_keep, pair_send = halves_sum(pair_own, pair_got, corner_a)
        pair_back = flip(pair_send, "dp", 2)
        to_x, to_y = sides_sum(near, got, corner_x, corner_y, value_got)
        got_x, got_y = flip_x(to_x), flip_y(to_y)
        value_keep, value_send = halves_sum(value_own, value_got, to_x)
        value_back = flip(value_send, "dp", 2)
        pair_keep, pair_send = halves_sum(pair_keep, pair_back, value_send)
        pair_last = flip(pair_send[0], "dp", 4)
        input_gradient = row_gradient(placed, mixed_back, attend_full, pair_send)
        value_keep, value_send = halves_sum(value_keep, value_back, input_gradient)
        value_last = flip(value_send[0], "dp", 4)
        mine, *sent = chip_sum(near[0], got[0], got_x, got_y, input_gradient)
        pair_grad = total_of(pair_keep[0], after(pair_last, mine))
        gradient_value = total_of(value_keep[0], after(value_last, mine))[0]
        packed_grad = total_of(mine, *[flip(sent[k - 1], "dp", 2 * k) for k in (1, 2, 3)])
        gradient_down, gradient_gate = pair_grad[0].T, pair_grad[1]
    else:
        here, across_y, across_x, corner = (add_low(near[k], got[k]) for k in range(4))
        input_gradient = row_gradient(placed, mixed_back, attend_full, placed)
        gradient_down = from_pieces(pair_own[:, 0], pair_far[:, 0]).T
        gradient_gate = from_pieces(pair_own[:, 1], pair_far[:, 1])
        gradient_value = from_pieces(value_own[:, 0], value_far[:, 0])
        packed_grad = from_pieces(
            add_low(here, flip_x(across_x)), add_low(across_y, flip_x(corner))
        )
    own_rows = attend_master.shape[0]
    gradient_attend, gradient_merge = unpack_columns(packed_grad[:own_rows], core_at)
    if small:
        gradient_norms = packed_grad[own_rows : own_rows + 1, :own_rows]
    else:
        norm_parts = jnp.concatenate([first_grads, second_grads], axis=0)
        gradient_norms = lax.psum_scatter(norm_parts, "mp", scatter_dimension=0, tiled=True)
        gradient_norms = lax.psum_scatter(gradient_norms, "dp", scatter_dimension=1, tiled=True)

    step_value = step_number[0].astype(jnp.float32)
    moment_attend, squares_attend, updated_attend = adamw_step(
        attend_master, first_attend, second_attend, gradient_attend, step_value, decay_rate
    )
    moment_merge, squares_merge, updated_merge = adamw_step(
        merge_master, first_merge, second_merge, gradient_merge, step_value, decay_rate
    )
    moment_norms, squares_norms, updated_norms = adamw_step(
        norms_master, first_norms, second_norms, gradient_norms, step_value, 0.0
    )
    moment_gate, squares_gate, updated_gate = adamw_step(
        gate_master, first_gate, second_gate, gradient_gate, step_value, decay_rate
    )
    moment_value, squares_value, updated_value = adamw_step(
        value_master, first_value, second_value, gradient_value, step_value, decay_rate
    )
    moment_down, squares_down, updated_down = adamw_step(
        down_master, first_down, second_down, gradient_down, step_value, decay_rate
    )
    return (
        layer_output,
        input_gradient,
        gradient_attend,
        gradient_merge,
        gradient_norms,
        gradient_gate,
        gradient_value,
        gradient_down,
        moment_attend,
        moment_merge,
        moment_norms,
        moment_gate,
        moment_value,
        moment_down,
        squares_attend,
        squares_merge,
        squares_norms,
        squares_gate,
        squares_value,
        squares_down,
        updated_attend,
        updated_merge,
        updated_norms,
        updated_gate,
        updated_value,
        updated_down,
    )


def solution(mesh):
    return jax.shard_map(
        shards,
        mesh=mesh,
        in_specs=(
            P(("dp", "mp"), None),
            P(),
            P(("dp", "mp"), None),
            P(("dp", "mp")),
            P(("dp", "mp"), None),
            P(("dp", "mp"), None, None),
            P(),
            P("dp", "mp"),
            P("dp", "mp"),
            P("mp", "dp"),
            P("dp", "mp"),
            P("dp", "mp"),
            P("mp", "dp"),
            P("dp", "mp"),
            P("dp", "mp"),
            P("mp", "dp"),
            P("dp", "mp"),
            P("dp", "mp"),
            P("mp", "dp"),
            P("dp", "mp"),
            P("dp", "mp"),
            P("mp", "dp"),
            P("dp", "mp"),
            P("dp", "mp"),
            P("mp", "dp"),
        ),
        out_specs=(
            P(("dp", "mp"), None),
            P(("dp", "mp"), None),
            P("dp", "mp"),
            P("dp", "mp"),
            P("mp", "dp"),
            P("dp", "mp"),
            P("dp", "mp"),
            P("mp", "dp"),
            P("dp", "mp"),
            P("dp", "mp"),
            P("mp", "dp"),
            P("dp", "mp"),
            P("dp", "mp"),
            P("mp", "dp"),
            P("dp", "mp"),
            P("dp", "mp"),
            P("mp", "dp"),
            P("dp", "mp"),
            P("dp", "mp"),
            P("mp", "dp"),
            P("dp", "mp"),
            P("dp", "mp"),
            P("mp", "dp"),
            P("dp", "mp"),
            P("dp", "mp"),
            P("mp", "dp"),
        ),
        check_vma=False,
    )
```

```python
from functools import partial

import jax
import jax.numpy as jnp
from jax import lax
from jax.experimental import pallas as pl
from jax.experimental.pallas import tpu as pltpu
from jax.sharding import PartitionSpec as P

HEADS = 12
HEAD_DIM = 64


beta_one = 0.9
beta_two = 0.999
peak_rate = 1.0
warm_steps = 4.0
total_steps = 100.0
decay_rate = 0.01
adam_eps = 1e-08
norm_eps = 1e-05


def layer_norm(row_data, gain_row, shift_row):
    centered = row_data - jnp.mean(row_data, axis=-1, keepdims=True)
    spread = jnp.mean(centered * centered, axis=-1, keepdims=True)
    return centered * lax.rsqrt(spread + norm_eps) * gain_row + shift_row


def alibi_table(head_count, seq_len):
    slopes = jnp.exp2(-8.0 * jnp.arange(1, head_count + 1, dtype=jnp.float32) / head_count)
    places = jnp.arange(seq_len, dtype=jnp.float32)
    return slopes[:, None, None] * jnp.abs(places[:, None] - places[None, :])


def dot_nn(left_op, right_op):
    return lax.dot_general(
        left_op, right_op, (((1,), (0,)), ((), ())), preferred_element_type=jnp.float32
    )


def dot_nt(left_op, right_op):
    return lax.dot_general(
        left_op, right_op, (((1,), (1,)), ((), ())), preferred_element_type=jnp.float32
    )


def dot_tn(left_op, right_op):
    return lax.dot_general(
        left_op, right_op, (((0,), (0,)), ((), ())), preferred_element_type=jnp.float32
    )


def flip(block, axis, bits):
    size = lax.axis_size(axis)
    return lax.ppermute(block, axis, [(i, i ^ bits) for i in range(size)])


def flip_core(block):
    return flip(block, "mp", 1)


def flip_x(block):
    return flip(block, "mp", 2)


def flip_y(block):
    return flip(block, "dp", 1)


def norm_stats(row_data):
    centered = row_data - jnp.mean(row_data, axis=-1, keepdims=True)
    spread = jnp.mean(centered * centered, axis=-1, keepdims=True)
    inverse = lax.rsqrt(spread + norm_eps)
    return centered * inverse, inverse


def z_groups():
    size = lax.axis_size("dp")
    return [list(range(low, size, 2)) for low in range(2)]


def pass_on(*refs):
    pass


def after(block, *others):
    return pl.pallas_call(
        pass_on,
        out_shape=jax.ShapeDtypeStruct(block.shape, block.dtype),
        in_specs=[pl.BlockSpec(memory_space=pl.ANY)] * (1 + len(others)),
        out_specs=pl.BlockSpec(memory_space=pl.ANY),
        input_output_aliases={0: 0},
        cost_estimate=pl.CostEstimate(flops=0, bytes_accessed=0, transcendentals=0),
    )(block, *others)


def is_small():
    return lax.axis_size("dp") == 8


def gather_z(block):
    far = flip(block, "dp", 4)
    return [block, far, flip(block, "dp", 2), flip(far, "dp", 2)]


def piece_rows(features):
    at = jnp.arange(8, dtype=jnp.int32)
    if is_small():
        along_z = ((at & 1) << 1) + ((at >> 1) & 1)
        at = (2 * along_z + (at >> 2)) ^ lax.axis_index("dp")
    return at * (features // 8)


def gather_whole(block):
    whole = lax.all_gather(block, "dp", axis=1, tiled=True)
    lots, features, columns = whole.shape
    whole = whole.reshape(lots, 8, features // 8, columns).transpose(1, 0, 2, 3)
    return [whole], [flip_x(whole)]


def add_low(*parts):
    return sum(part.astype(jnp.float32) for part in parts).astype(jnp.bfloat16)


def sum_dp(whole):
    return lax.psum_scatter(whole.astype(jnp.float32), "dp", scatter_dimension=0, tiled=True)


def from_pieces(*parts):
    whole = jnp.concatenate(parts, axis=0)
    return sum_dp(whole.reshape(-1, whole.shape[-1]))


MIB = 1024 * 1024
ANYWHERE = pl.BlockSpec(memory_space=pl.ANY)
IN_VMEM = pl.BlockSpec(memory_space=pltpu.VMEM)
IN_SMEM = pl.BlockSpec(memory_space=pltpu.SMEM)


def kernel_call(body, outs, specs, scratch, limit):
    return pl.pallas_call(
        body,
        out_shape=outs,
        in_specs=specs,
        out_specs=[IN_VMEM] * len(outs),
        scratch_shapes=scratch,
        compiler_params=pltpu.CompilerParams(vmem_limit_bytes=limit * MIB),
        cost_estimate=pl.CostEstimate(flops=0, bytes_accessed=0, transcendentals=0),
    )


def like(shape, dtype):
    return jax.ShapeDtypeStruct(shape, dtype)


def with_lot(groups, lot):
    return [(group, (i, lot)) for group in groups for i in range(group.shape[0])]


def load_pieces(pieces, rows, total, sems):
    copies = []
    count = total.shape[0] // 8
    for k, (group, at) in enumerate(pieces):
        to = total.at[pl.ds(pl.multiple_of(rows[k], 32), count), :]
        copies.append(pltpu.make_async_copy(group.at[(*at, pl.ds(0, count))], to, sems.at[k]))
        copies[-1].start()
    return copies


EXTRA = 16


def load_extras(groups, spots, total, sems):
    copies = []
    for group in groups:
        for i in range(group.shape[0]):
            k = len(copies)
            source = group.at[i, 0, pl.ds(group.shape[2] - EXTRA, EXTRA), :]
            copies.append(pltpu.make_async_copy(source, total.at[spots[k]], sems.at[k]))
            copies[-1].start()
    return copies


def split_low(block):
    parts = []
    for _ in range(3):
        part = lax.reduce_precision(block, 8, 7)
        parts.append(jnp.pad(part.astype(jnp.bfloat16), ((0, EXTRA - 1), (0, 128 - block.shape[1]))))
        block = block - part
    return jnp.pad(jnp.concatenate(parts, axis=1), ((0, 0), (0, 384)))


def wait_all(copies):
    for copy in copies:
        copy.wait()


def gelu_parts(gated):
    below = 0.5 + 0.5 * lax.erf(gated * 0.7071067811865476)
    return gated * below, below


def lower_lanes(shape):
    return lax.broadcasted_iota(jnp.int32, shape, 1) < 64


def unpack_columns_of(blocks, attend, merge):
    for block, (column, merge_column) in enumerate(((0, 0), (640, 256), (1152, 384), (1792, 640))):
        attend[:, column : column + 512] = blocks[block, :, :512]
        merge[:, merge_column : merge_column + 128] = blocks[block, :, 512:640]
    for pair, (column, merge_column) in enumerate(((512, 128), (1664, 512))):
        even = blocks[2 * pair, :, 640:].astype(jnp.float32)
        odd = blocks[2 * pair + 1, :, 640:].astype(jnp.float32)
        lower = lower_lanes(even.shape)
        attend[:, column : column + 128] = jnp.where(lower, even, odd).astype(jnp.bfloat16)
        mixed_up = pltpu.roll(jnp.where(lower, odd, even), 64, 1)
        merge[:, merge_column : merge_column + 128] = mixed_up.astype(jnp.bfloat16)


def first_kernel(counts, extra, places, rows, spots, start, norms_given, positions, *refs):
    low = jnp.bfloat16
    groups = []
    for count in counts:
        groups.append(refs[:count])
        refs = refs[count:]
    attend, merge, mixed, normed, *narrow, slot_sum, slot_attended, slot_narrow, norms = refs[:10]
    blocks, attended, scores, extras, sems = refs[10:]
    copies = []
    for at, group in enumerate(groups):
        copies += load_pieces(with_lot(group, 0), rows, blocks.at[places[at]], sems.at[0, at])
        if extra:
            copies += load_extras(group, spots, extras.at[places[at]], sems.at[1, at])
    wait_all(copies)
    if extra:
        for block in range(4):
            whole = jnp.zeros((8, norms.shape[1]), jnp.float32)
            for spot in range(8):
                parts = extras[block, spot].astype(jnp.float32)[:8, :]
                value = parts[:, :128] + parts[:, 128:256] + parts[:, 256:384]
                value = jnp.concatenate([value, jnp.zeros((8, norms.shape[1] - 128), jnp.float32)], axis=1)
                whole = whole + (pltpu.roll(value, spot * (norms.shape[1] // 8), 1) if spot else value)
            norms[block : block + 1, :] = whole[:1, :]
    else:
        norms[...] = norms_given[...]
    unpack_columns_of(blocks, attend, merge)
    width = merge.shape[0]
    length = 128
    slots = 32
    scale = HEAD_DIM ** (-0.5)
    for column in range(0, 3 * width, 256):
        cut = slice(column, column + 256)
        mixed[:, cut] = dot_nn(start[...], attend[:, cut]).astype(low)
    shape = (length, length)
    apart = jnp.abs(
        lax.broadcasted_iota(jnp.int32, shape, 0) - lax.broadcasted_iota(jnp.int32, shape, 1)
    ).astype(jnp.float32)
    lower = lower_lanes(shape)

    def step(target, first, seq, carry):
        at = pl.ds(pl.multiple_of(seq * length, length), length)
        to = pl.ds(pl.multiple_of(seq * slots, slots), slots)
        for pair in range(HEADS // 2):
            column = 2 * HEAD_DIM * pair
            queries = mixed[at, column : column + 128]
            keys = mixed[at, width + column : width + column + 128]
            zero = jnp.zeros_like(queries)
            for half in range(2):
                own = jnp.where(lower, queries, zero) if half == 0 else jnp.where(lower, zero, queries)
                head = 2 * pair + half
                scores[head] = dot_nt(own, keys) * scale - apart * slopes_of(head)
        raised = scores[...]
        raised = jnp.exp(raised - jnp.max(raised, axis=-1, keepdims=True))
        scores[...] = raised / jnp.sum(raised, axis=-1, keepdims=True)
        for pair in range(HEADS // 2):
            column = 2 * HEAD_DIM * pair
            values = mixed[at, 2 * width + column : 2 * width + column + 128]
            heads = [dot_nn(scores[2 * pair + half].astype(low), values) for half in range(2)]
            attended[at, column : column + 128] = jnp.where(lower, heads[0], heads[1]).astype(low)
        total = start[at, :].astype(jnp.float32) + dot_nn(attended[at, :], merge[...])
        xhat, _ = norm_stats(total)
        rows = xhat * norms[0:1, :] + norms[1:2, :]
        normed[at, :] = rows
        target[pl.ds(pl.multiple_of((seq - first) * length, length), length), :] = rows.astype(low)
        selector = one_hot(positions[to, :], length)
        slot_sum[to, :] = select_exact(selector, total)
        slot_attended[to, :] = dot_nn(selector, attended[at, :]).astype(low)
        slot_narrow[to, :] = dot_nn(selector, rows.astype(low)).astype(low)
        return carry

    seqs = start.shape[0] // length // 2
    lax.fori_loop(0, seqs, partial(step, narrow[0], 0), 0, unroll=True)
    lax.fori_loop(seqs, 2 * seqs, partial(step, narrow[1], seqs), 0, unroll=True)


def first_part(extra, places, rows, spots, start, norms, positions, groups):
    count, width = start.shape
    slot_rows = positions.shape[0]
    low = jnp.bfloat16
    return kernel_call(
        partial(first_kernel, [len(group) for group in groups], extra),
        [
            like((width, 3 * width), low),
            like((width, width), low),
            like((count, 3 * width), low),
            like((count, width), jnp.float32),
            like((count // 2, width), low),
            like((count // 2, width), low),
            like((slot_rows, width), jnp.float32),
            like((slot_rows, width), low),
            like((slot_rows, width), low),
            like((4, width), jnp.float32),
        ],
        [IN_SMEM] * 3 + [IN_VMEM] * 3 + [ANYWHERE] * sum(map(len, groups)),
        [
            pltpu.VMEM((4, width, width), low),
            pltpu.VMEM((count, width), low),
            pltpu.VMEM((HEADS, 128, 128), jnp.float32),
            pltpu.VMEM((4, 8, EXTRA, width), low),
            pltpu.SemaphoreType.DMA((2, 4, 8)),
        ], 30)(places, rows, spots, start, norms, positions, *sum(groups, []))


def pack_columns(attend, merge, core_at):
    even = jnp.concatenate(
        [attend[:, :512], merge[:, :128], attend[:, 512:], merge[:, 128:]], axis=1
    )
    odd = jnp.concatenate([attend[:, 64:], merge[:, 64:], merge[:, :64], attend[:, :64]], axis=1)
    return jnp.where(core_at == 0, even, odd)


def unpack_columns(packed, core_at):
    even = jnp.concatenate([packed[:, :512], packed[:, 640:704]], axis=1)
    odd = jnp.concatenate([packed[:, 704:], packed[:, :512]], axis=1)
    even_merge = jnp.concatenate([packed[:, 512:640], packed[:, 704:]], axis=1)
    odd_merge = jnp.concatenate([packed[:, 640:704], packed[:, 512:640]], axis=1)
    return jnp.where(core_at == 0, even, odd), jnp.where(core_at == 0, even_merge, odd_merge)


def front_kernel(count, rows, *refs):
    sources, refs = refs[:4], refs[4:]
    near, far = refs[: count[0]], refs[count[0] : count[0] + count[1]]
    hidden, gates, values, sems = refs[-4:]
    copies = []
    for k, groups in enumerate((near, far)):
        copies.append(
            load_pieces(with_lot(groups, 0), rows, gates.at[k], sems.at[k, 0])
            + load_pieces(with_lot(groups, 1), rows, values.at[k], sems.at[k, 1])
        )
    quarter = sources[0].shape[0]
    for k in range(2):
        wait_all(copies[k])
        for part, source in enumerate(sources):
            start = part * quarter

            def step(tile, carry, k=k, start=start, source=source):
                block = source[pl.ds(pl.multiple_of(tile * 256, 256), 256), :]
                to = pl.ds(pl.multiple_of(start + tile * 256, 256), 256)
                for column in range(0, gates.shape[2], 256):
                    cut = slice(column, column + 256)
                    gated = dot_nn(block, gates[k, :, cut])
                    valued = dot_nn(block, values[k, :, cut])
                    hidden[k, to, cut] = (gelu_parts(gated)[0] * valued).astype(jnp.bfloat16)
                return carry

            lax.fori_loop(0, source.shape[0] // 256, step, 0)


def ffn_front(rows, sources, near, far, *earlier):
    quarter, width = sources[0].shape
    return kernel_call(
        partial(front_kernel, (len(near), len(far))),
        [like((2, 4 * quarter, width), jnp.bfloat16)],
        [IN_SMEM] + [IN_VMEM] * 4 + [ANYWHERE] * (len(near) + len(far) + len(earlier)),
        [
            pltpu.VMEM((2, width, width), jnp.bfloat16),
            pltpu.VMEM((2, width, width), jnp.bfloat16),
            pltpu.SemaphoreType.DMA((2, 2, 8)),
        ], 18)(rows, *sources, *near, *far, *earlier)[0]


def down_kernel(lots, rows, hidden, *refs):
    split, end = len(lots[0]), len(lots[0]) + len(lots[1])
    mine, other, downs, sems = refs[end + 1 :]
    copies = load_pieces(zip(refs[:split], lots[0]), rows, downs.at[0], sems.at[0])
    copies += load_pieces(zip(refs[split:end], lots[1]), rows, downs.at[1], sems.at[1])
    wait_all(copies)
    half = mine.shape[0]
    for part, target in ((1, other), (0, mine)):

        def step(tile, carry, part=part, target=target):
            at = pl.ds(pl.multiple_of(part * half + tile * 256, 256), 256)
            to = pl.ds(pl.multiple_of(tile * 256, 256), 256)
            target[to, :] = dot_nt(hidden[0, at, :], downs[0]) + dot_nt(hidden[1, at, :], downs[1])
            return carry

        lax.fori_loop(0, half // 256, step, 0)


def ffn_down(rows, hidden, near, far, earlier):
    both, width = hidden.shape[1:]
    return kernel_call(
        partial(down_kernel, [[lot for _, lot in group] for group in (near, far)]),
        [like((both // 2, width), jnp.float32)] * 2,
        [IN_SMEM, IN_VMEM] + [ANYWHERE] * (len(near) + len(far) + 1),
        [pltpu.VMEM((2, width, width), jnp.bfloat16), pltpu.SemaphoreType.DMA((2, 8))], 16)(rows, hidden, *[group for group, _ in near + far], earlier)


def select_exact(selector, block):
    first = block.astype(jnp.bfloat16)
    rest = block - first.astype(jnp.float32)
    second = rest.astype(jnp.bfloat16)
    third = (rest - second.astype(jnp.float32)).astype(jnp.bfloat16)
    return dot_nn(selector, first) + dot_nn(selector, second) + dot_nn(selector, third)


def norm_back(xhat, inverse, gain_row, incoming):
    scaled = incoming * gain_row
    inner = jnp.mean(scaled * xhat, axis=-1, keepdims=True)
    back = inverse * (scaled - jnp.mean(scaled, axis=-1, keepdims=True) - xhat * inner)
    gain_back = jnp.sum(incoming * xhat, axis=0, keepdims=True)
    return back, gain_back, jnp.sum(incoming, axis=0, keepdims=True)


def one_hot(positions, length):
    shape = (positions.shape[0], length)
    return (positions == lax.broadcasted_iota(jnp.int32, shape, 1)).astype(jnp.bfloat16)


def second_kernel(
    normed, part, got, norms, positions, live, cotangent, output, pulled, back, norm_grads
):
    slots = cotangent.shape[1]
    length = normed.shape[0] // cotangent.shape[0]
    norm_grads[...] = jnp.zeros_like(norm_grads)

    def step(seq, carry):
        at = pl.ds(pl.multiple_of(seq * length, length), length)
        to = pl.ds(pl.multiple_of(seq * slots, slots), slots)
        total = normed[at, :] + part[at, :] + got[at, :]
        xhat, _ = norm_stats(total)
        output[at, :] = (xhat * norms[2:3, :] + norms[3:4, :]).astype(jnp.bfloat16)
        selector = one_hot(positions[to, :], length)
        xhat, inverse = norm_stats(select_exact(selector, total))
        incoming = jnp.where(live[to, :] > 0, cotangent[seq].astype(jnp.float32), 0.0)
        slot_back, gain_back, shift_back = norm_back(xhat, inverse, norms[2:3, :], incoming)
        back[to, :] = slot_back
        pulled[to, :] = slot_back.astype(jnp.bfloat16)
        norm_grads[0:1, :] += gain_back
        norm_grads[1:2, :] += shift_back
        return carry

    lax.fori_loop(0, cotangent.shape[0], step, 0, unroll=True)


def second_norm(normed, part, got, norms, positions, live, cotangent):
    count, width = normed.shape
    slot_rows = positions.shape[0]
    return kernel_call(
        second_kernel,
        [
            like((count, width), jnp.bfloat16),
            like((slot_rows, width), jnp.bfloat16),
            like((slot_rows, width), jnp.float32),
            like((2, width), jnp.float32),
        ],
        [IN_VMEM] * 7,
        [], 14)(normed, part, got, norms, positions, live, cotangent)


def back_kernel(count, lots, rows, *refs):
    pulls, narrows = refs[0:4], refs[4:8]
    wide, deep = refs[8 : 8 + count[0]], refs[8 + count[0] : 8 + count[0] + count[1]]
    keep, send, pull_rows, work_rows, gate_back, value_back, hidden = refs[
        8 + count[0] + count[1] : -4
    ]
    gates, values, downs, sems = refs[-4:]
    copies = load_pieces(with_lot(wide, 0), rows, gates, sems.at[0])
    copies += load_pieces(with_lot(wide, 1), rows, values, sems.at[1])
    copies += load_pieces(zip(deep, lots), rows, downs, sems.at[2])
    size = pulls[0].shape[0]
    for k in range(4):
        pull_rows[k * size : (k + 1) * size, :] = pulls[k][...]
        work_rows[k * size : (k + 1) * size, :] = narrows[k][...]
    wait_all(copies)
    for column in range(0, gates.shape[1], 256):
        cut = slice(column, column + 256)
        gated = dot_nn(work_rows[...], gates[:, cut])
        valued = dot_nn(work_rows[...], values[:, cut])
        hidden_back = dot_nn(pull_rows[...], downs[:, cut])
        gelu, below = gelu_parts(gated)
        slope = below + gated * (0.3989422804014327 * jnp.exp(-0.5 * gated * gated))
        hidden[:, cut] = (gelu * valued).astype(jnp.bfloat16)
        gate_back[:, cut] = (hidden_back * valued * slope).astype(jnp.bfloat16)
        value_back[:, cut] = (hidden_back * gelu).astype(jnp.bfloat16)
    for column in range(0, gates.shape[0], 256):
        cut = slice(column, column + 256)
        total = dot_nt(gate_back[...], gates[cut, :]) + dot_nt(value_back[...], values[cut, :])
        for k, target in enumerate((keep, keep, send, send)):
            target[k % 2, :, cut] = total[k * size : (k + 1) * size]


def ffn_back(rows, pulls, narrows, wide, deep):
    size, width = pulls[0].shape
    low = jnp.bfloat16
    return kernel_call(
        partial(back_kernel, (len(wide), len(deep)), [lot for _, lot in deep]),
        [like((2, size, width), jnp.float32)] * 2 + [like((4 * size, width), low)] * 5,
        [IN_SMEM] + [IN_VMEM] * 8 + [ANYWHERE] * (len(wide) + len(deep)),
        [pltpu.VMEM((width, width), low)] * 3 + [pltpu.SemaphoreType.DMA((3, 8))], 22)(rows, *pulls, *narrows, *wide, *[group for group, _ in deep])


def store_pieces(total, rows, mine, other):
    count = total.shape[0] // 8
    for k in range(8):
        at = pl.ds(pl.multiple_of(rows[k], 32), count)
        to = mine if k < 4 else other
        to[k % 4, :count, :] = total[at, :]


def grads_kernel(lots, rows, *refs):
    factors, refs = refs[: 2 * lots], refs[-3 - lots :]
    mine, other, total, turned = refs[0], refs[1], refs[2], refs[3:]
    for lot in range(lots):
        turned[lot][...] = factors[2 * lot][...].T
    for lot in range(lots):
        for column in range(0, total.shape[1], 256):
            cut = slice(column, column + 256)
            product = dot_nn(turned[lot][...], factors[2 * lot + 1][:, cut])
            total[:, cut] = product.astype(jnp.bfloat16)
        store_pieces(total, rows, mine.at[:, lot], other.at[:, lot])


def ffn_grads(rows, factors, *earlier):
    size, width = factors[0].shape
    lots = len(factors) // 2
    low = jnp.bfloat16
    return kernel_call(
        partial(grads_kernel, lots),
        [like((4, lots, width // 8, width), low)] * 2,
        [IN_SMEM] + [IN_VMEM] * len(factors) + [ANYWHERE] * len(earlier),
        [pltpu.VMEM((width, width), low)] + [pltpu.VMEM((width, size), low)] * lots, 16)(rows, *factors, *earlier)


def split_kernel(from_y, from_x, *refs):
    first, second, sems = refs[-3:]
    half = first.shape[0]
    copies = [
        pltpu.make_async_copy(from_y.at[pl.ds(0, half)], first, sems.at[0]),
        pltpu.make_async_copy(from_x.at[pl.ds(half, half)], second, sems.at[1]),
    ]
    for copy in copies:
        copy.start()
    wait_all(copies)


def split_halves(from_y, from_x, *earlier):
    half = like((from_y.shape[0] // 2,) + from_y.shape[1:], from_y.dtype)
    return kernel_call(
        split_kernel,
        [half, half],
        [ANYWHERE] * (2 + len(earlier)),
        [pltpu.SemaphoreType.DMA((2,))], 6)(from_y, from_x, *earlier)


def cast_kernel(first, second, _, both):
    both[0] = first[...].astype(jnp.bfloat16)
    both[1] = second[...].astype(jnp.bfloat16)


def cast_wide(first, second, earlier):
    return kernel_call(
        cast_kernel,
        [like((2,) + first.shape, jnp.bfloat16)],
        [IN_VMEM] * 2 + [ANYWHERE],
        [], 4)(first, second, earlier)[0]


def wide_sum(*blocks):
    return sum(block.astype(jnp.float32) for block in blocks)


def total_of(*blocks):
    return wide_sum(*blocks)


def corner_kernel(near, got, *refs):
    first, second = refs[-2:]
    for k in range(4):
        target = first if k < 2 else second
        target[k % 2] = wide_sum(near[k], got[k]).astype(jnp.bfloat16)


def corner_sum(near, got, *earlier):
    half = like((2,) + near.shape[1:], near.dtype)
    return kernel_call(
        corner_kernel, [half, half], [IN_VMEM] * 2 + [ANYWHERE] * len(earlier), [], 6)(near, got, *earlier)


def sides_kernel(near_y, got_y, near_x, got_x, corner_x, corner_y, _, to_x, to_y):
    for k in range(4):
        corner = [corner_x[k]] if k < 2 else []
        to_y[k] = wide_sum(near_y[k], got_y[k], *corner).astype(jnp.bfloat16)
        corner = [corner_y[k - 2]] if k >= 2 else []
        to_x[k] = wide_sum(near_x[k], got_x[k], *corner).astype(jnp.bfloat16)


def sides_sum(near, got, corner_x, corner_y, earlier):
    side = like(near[1].shape, near[1].dtype)
    return kernel_call(sides_kernel, [side, side], [IN_VMEM] * 6 + [ANYWHERE], [], 10)(
        near[1], got[1], near[2], got[2], corner_x, corner_y, earlier
    )


def chip_kernel(near, got, got_x, got_y, _, mine, far, side, last):
    for k, target in enumerate((mine, far, side, last)):
        total = wide_sum(near[k], got[k], got_x[k], got_y[k])
        target[...] = total.astype(target.dtype)


def chip_sum(near, got, got_x, got_y, earlier):
    piece = near.shape[1:]
    mine, far, side, last = kernel_call(
        chip_kernel,
        [like(piece, jnp.float32)] + [like(piece, near.dtype)] * 3,
        [IN_VMEM] * 4 + [ANYWHERE],
        [], 8)(near, got, got_x, got_y, earlier)
    return mine, side, far, last


def halves_kernel(mine, got, *refs):
    keep, send = refs[-2:]
    half = keep.shape[0]
    for k in range(half):
        keep[k] = wide_sum(mine[k], got[k]).astype(keep.dtype)
        send[k] = wide_sum(mine[half + k], got[half + k]).astype(send.dtype)


def halves_sum(mine, got, *earlier):
    half = like((mine.shape[0] // 2,) + mine.shape[1:], mine.dtype)
    return kernel_call(
        halves_kernel, [half, half], [IN_VMEM] * 2 + [ANYWHERE] * len(earlier), [], 8)(mine, got, *earlier)


def row_gradient_kernel(placed, mixed_back, attend, _, output):
    for column in range(0, placed.shape[1], 256):
        cut = slice(column, column + 256)
        output[:, cut] = placed[:, cut] + dot_nt(mixed_back[...], attend[cut, :])


def row_gradient(placed, mixed_back, attend, earlier):
    count, width = placed.shape
    return kernel_call(
        row_gradient_kernel,
        [like(placed.shape, placed.dtype)],
        [IN_VMEM] * 3 + [ANYWHERE],
        [], 14)(placed, mixed_back, attend, earlier)[0]


def slopes_of(head):
    return 2.0 ** (-8.0 * (head + 1) / HEADS)


def attend_kernel(
    extra,
    rows,
    columns,
    spots,
    second_grads,
    keep,
    got,
    second_back,
    slot_sum,
    norms,
    merge,
    mixed,
    slot_attended,
    start,
    positions,
    _,
    placed,
    mixed_back,
    norm_grads,
    *refs,
):
    near, far = refs[0:4], refs[4:8]
    merge_grad, total, branch, attended_back, first_back, turned, extras = refs[8:]
    width = norms.shape[1]
    slots = 32
    length = 128
    low = jnp.bfloat16
    scale = HEAD_DIM ** (-0.5)
    xhat, inverse = norm_stats(slot_sum[...])
    incoming = keep[...] + got[...].astype(jnp.float32) + second_back[...]
    slot_back, gain_back, shift_back = norm_back(xhat, inverse, norms[0:1, :], incoming)
    norm_grads[0:1, :] = gain_back
    norm_grads[1:2, :] = shift_back
    if extra:
        both = [gain_back, shift_back, second_grads[0:1, :], second_grads[1:2, :]]
        zero_rows = jnp.zeros((EXTRA - 1, width), jnp.float32)
        for block in range(4):
            whole = jnp.concatenate([both[block], zero_rows], axis=0)
            for spot in range(8):
                turn = (8 - spot) % 8 * (width // 8)
                extras[block, spot] = (pltpu.roll(whole, turn, 1) if turn else whole).astype(low)
    first_back[...] = slot_back
    branch[...] = slot_back.astype(low)
    attended_back[...] = dot_nt(branch[...], merge[...]).astype(low)
    merge_grad[...] = dot_tn(slot_attended[...], branch[...])
    lane_head = lax.broadcasted_iota(jnp.int32, (slots, width), 1) // HEAD_DIM

    def apart_heads(block):
        zero = jnp.zeros_like(block)
        return jnp.concatenate(
            [jnp.where(lane_head == head, block, zero) for head in range(HEADS)], axis=0
        )

    def join_heads(block):
        total = jnp.zeros((slots, width), jnp.float32)
        for head in range(HEADS):
            total = jnp.where(lane_head == head, block[head * slots : (head + 1) * slots], total)
        return total

    def step(seq, carry):
        at = pl.ds(pl.multiple_of(seq * length, length), length)
        to = pl.ds(pl.multiple_of(seq * slots, slots), slots)
        spots = positions[to, :]
        selector = one_hot(spots, length)
        apart = jnp.abs(
            spots - lax.broadcasted_iota(jnp.int32, (slots, length), 1)
        ).astype(jnp.float32)
        keys = mixed[at, width : 2 * width]
        values = mixed[at, 2 * width :]
        queries = apart_heads(dot_nn(selector, mixed[at, :width])).astype(low)
        heads_back = apart_heads(attended_back[to, :].astype(jnp.float32)).astype(low)
        bias = jnp.concatenate([apart * slopes_of(head) for head in range(HEADS)], axis=0)
        scores = dot_nt(queries, keys) * scale - bias
        exp_scores = jnp.exp(scores - jnp.max(scores, axis=-1, keepdims=True))
        probs = exp_scores / jnp.sum(exp_scores, axis=-1, keepdims=True)
        probs_back = dot_nt(heads_back, values)
        inner = jnp.sum(probs * probs_back, axis=-1, keepdims=True)
        scores_back = (probs * (probs_back - inner)).astype(low)
        queries_back = (join_heads(dot_nn(scores_back, keys)) * scale).astype(low)
        mixed_back[at, :width] = dot_tn(selector, queries_back).astype(low)
        mixed_back[at, width : 2 * width] = (dot_tn(scores_back, queries) * scale).astype(low)
        mixed_back[at, 2 * width :] = dot_tn(probs.astype(low), heads_back).astype(low)
        spread = (spots == lax.broadcasted_iota(jnp.int32, (slots, length), 1)).astype(jnp.float32)
        placed[at, :] = select_exact(jnp.transpose(spread).astype(low), first_back[to, :])
        return carry

    lax.fori_loop(0, mixed.shape[0] // length, step, 0, unroll=True)
    turned[...] = start[...].T
    for core, target in ((1, far), (0, near)):
        for k in range(2):
            base = 6 * (2 * core + k)
            for part in range(2):
                column = pl.ds(pl.multiple_of(columns[base] + 256 * part, 128), 256)
                product = dot_nn(turned[...], mixed_back[:, column])
                total[:, 256 * part : 256 * part + 256] = product.astype(low)
            column = pl.ds(pl.multiple_of(columns[base + 1], 128), 128)
            total[:, 512:640] = merge_grad[:, column].astype(low)
            column = pl.ds(pl.multiple_of(columns[base + 2], 128), 128)
            single = dot_nn(turned[...], mixed_back[:, column])
            column = pl.ds(pl.multiple_of(columns[base + 3], 128), 128)
            merged = pltpu.roll(merge_grad[:, column], 64, 1)
            attend_lane = lower_lanes(single.shape) == (columns[base + 4] == 0)
            total[:, 640:] = jnp.where(attend_lane, single, merged).astype(low)
            sides = target[2 * k : 2 * k + 2]
            store_pieces(total, rows, *sides)
            if extra:
                for j in range(8):
                    sides[j // 4][j % 4, width // 8 :, :] = extras[columns[base + 5], spots[j]]


def attend_back(extra, rows, columns, spots, second_grads, *blocks):
    start, mixed = blocks[8], blocks[6]
    count, width = start.shape
    slot_rows = blocks[0].shape[0]
    low = jnp.bfloat16
    return kernel_call(
        partial(attend_kernel, extra),
        [
            like((count, width), jnp.float32),
            like(mixed.shape, low),
            like((2, width), jnp.float32),
        ]
        + [like((4, width // 8 + (EXTRA if extra else 0), width), low)] * 8,
        [IN_SMEM] * 3 + [IN_VMEM] * 11 + [ANYWHERE],
        [
            pltpu.VMEM((width, width), jnp.float32),
            pltpu.VMEM((width, width), low),
            pltpu.VMEM((slot_rows, width), low),
            pltpu.VMEM((slot_rows, width), low),
            pltpu.VMEM((slot_rows, width), jnp.float32),
            pltpu.VMEM((width, count), low),
            pltpu.VMEM((4, 8, EXTRA, width), low),
        ], 32)(rows, columns, spots, second_grads, *blocks)


def adamw_step(master, first, second, gradient, step_value, decay):
    step_rate = peak_rate * jnp.minimum(
        step_value / warm_steps, (total_steps - step_value) / (total_steps - warm_steps)
    )
    fix_one = 1.0 - jnp.power(jnp.float32(beta_one), step_value)
    fix_two = 1.0 - jnp.power(jnp.float32(beta_two), step_value)
    moment = beta_one * first + (1.0 - beta_one) * gradient
    squares = beta_two * second + (1.0 - beta_two) * gradient * gradient
    updated = master - step_rate * (
        moment / fix_one / (jnp.sqrt(squares / fix_two) + adam_eps) + decay * master
    )
    return (moment, squares, updated)


def shards(
    hidden_rows,
    token_table,
    masked_positions,
    masked_counts,
    replace_rows,
    masked_cotangent,
    step_number,
    attend_master,
    merge_master,
    norms_master,
    gate_master,
    value_master,
    down_master,
    first_attend,
    first_merge,
    first_norms,
    first_gate,
    first_value,
    first_down,
    second_attend,
    second_merge,
    second_norms,
    second_gate,
    second_value,
    second_down,
):
    local_seqs, slot_count = masked_positions.shape
    local_rows, model_width = hidden_rows.shape
    length = local_rows // local_seqs
    slot_rows = local_seqs * slot_count
    dp_size = lax.axis_size("dp")
    core_at = lax.axis_index("mp") & 1
    x_at = lax.axis_index("mp") >> 1
    low = jnp.bfloat16
    rows = piece_rows(model_width)

    packed = pack_columns(attend_master.astype(low), merge_master.astype(low), core_at)[None]
    small = is_small()
    deep = down_master.astype(low).T[None]

    order = [(core, k) for core in range(2) for k in range(2)]
    places = [2 * (x_at ^ k) + (core_at ^ core) for core, k in order]
    table = jnp.array(
        [
            [0, 0, 512, 128, 0, 0],
            [640, 256, 512, 128, 1, 1],
            [1152, 384, 1664, 512, 0, 2],
            [1792, 640, 1664, 512, 1, 3],
        ],
        jnp.int32,
    )
    columns = jnp.concatenate([table[place] for place in places])
    places = jnp.stack(places).astype(jnp.int32)
    spots = piece_rows(8)
    if small:
        packed = jnp.concatenate([packed, split_low(norms_master)[None]], axis=1)
        packed_z = [packed] + [flip(packed, "dp", 2 * k) for k in (2, 1, 3)]
        wide = cast_wide(gate_master, value_master, packed_z[2])

    live_slots = jnp.arange(slot_count, dtype=jnp.int32)[None, :] < masked_counts[:, None]
    at_slot = masked_positions[:, :, None] == jnp.arange(length, dtype=jnp.int32)[None, None, :]
    place_bool = at_slot & live_slots[:, :, None]
    chosen = jnp.take(token_table, replace_rows.reshape(-1), axis=0).reshape(
        local_seqs, slot_count, model_width
    )
    swapped = jnp.einsum(
        "sjt,sjd->std", place_bool.astype(low), chosen, preferred_element_type=jnp.float32
    ).astype(low)
    replaced = jnp.any(place_bool, axis=1)[:, :, None]
    start_rows = jnp.where(
        replaced, swapped, hidden_rows.reshape(local_seqs, length, model_width)
    ).reshape(local_rows, model_width)
    positions = masked_positions.reshape(slot_rows, 1)
    live = live_slots.astype(jnp.float32).reshape(slot_rows, 1)
    indices = [rows, places, columns, spots, positions, live]
    if small:
        deep = after(deep, start_rows)
        deep_y, deep_x = flip_y(deep), flip_x(deep)
        deep_parts = jnp.concatenate([deep, deep_y, deep_x, flip_x(deep_y)])
        packed_z[0] = after(packed_z[0], wide, deep_parts, *indices)
        wide_z = gather_z(after(wide, packed_z[1], packed_z[3]))
        packed_z = jnp.stack(packed_z)
        packed_y, packed_x = flip_y(packed_z), flip_x(packed_z)
        first_half, second_half = split_halves(packed_y, packed_x, wide_z[1], wide_z[2])
        packed_near = [packed_z, packed_y]
        packed_far = [packed_x, flip_x(first_half), flip_y(second_half)]
        wide_z[0] = after(wide_z[0], *packed_far[1:])
        deep_z = gather_z(after(deep_parts, *wide_z[1:])[None])
        wide_z = jnp.stack(wide_z)
        wide_y, wide_x = flip_y(wide_z), flip_x(wide_z)
        norms = jnp.zeros((4, model_width), jnp.float32)
    else:
        packed_near, packed_far = gather_whole(packed)
        norms = lax.all_gather(norms_master, "dp", axis=1, tiled=True)
        norms = lax.all_gather(norms, "mp", axis=0, tiled=True)

    packed_groups = [packed_near, packed_far]
    packed_groups += [[flip_core(part) for part in group] for group in packed_groups]
    (
        attend_full,
        merge_full,
        mixed,
        normed,
        narrow,
        narrow_end,
        slot_sum,
        slot_attended,
        slot_narrow,
        norms,
    ) = first_part(
        small,
        places,
        rows,
        spots,
        start_rows,
        norms,
        positions,
        packed_groups,
    )
    if small:
        first_half, second_half = split_halves(wide_y, wide_x, narrow, deep_z[2])
        wide_near = [wide_z, wide_y]
        wide_far = [wide_x, flip_x(first_half), flip_y(second_half)]
        deep_near = [(part, (0, side)) for side in (0, 1) for part in deep_z]
        deep_far = [(part, (0, side)) for side in (2, 3) for part in deep_z]
    else:
        wide_near, wide_far = gather_whole(
            jnp.stack([gate_master.astype(low), value_master.astype(low)])
        )
        deep_near, deep_far = (with_lot(group, 0) for group in gather_whole(deep))

    def over_group(block):
        other_x = flip_x(block)
        return [block, other_x, flip_core(block), flip_core(other_x)]


    chip_rows = (narrow, narrow_end, flip_core(narrow), flip_core(narrow_end))
    earlier = [deep_z[1] if small else rows]
    hidden = ffn_front(rows, chip_rows, wide_near, wide_far, *earlier)
    narrows = over_group(after(slot_narrow, hidden))
    ffn_mine, ffn_other = ffn_down(rows, hidden, deep_near, deep_far, rows)
    layer_output, pulled, second_back, second_grads = second_norm(
        normed, ffn_mine, flip_core(ffn_other), norms, positions, live, masked_cotangent
    )

    keep, send, *factors = ffn_back(rows, over_group(pulled), narrows, wide_near, deep_near)
    pull_rows, work_rows, gate_back, value_back, slot_hidden = factors
    chip_back = keep + flip_core(send)
    pair_own, pair_far = ffn_grads(rows, (pull_rows, slot_hidden, work_rows, gate_back))
    value_own, value_far = ffn_grads(rows, (work_rows, value_back), pair_own)
    if small:
        pair_got = flip_y(pair_far)
    placed, mixed_back, first_grads, *parts = attend_back(
        small,
        rows,
        columns,
        spots,
        second_grads,
        chip_back[0],
        flip_x(chip_back[1].astype(low)),
        second_back,
        slot_sum,
        norms,
        merge_full,
        mixed,
        slot_attended,
        start_rows,
        positions,
        value_far,
    )
    near, far = parts[:4], parts[4:]
    got = [flip_core(part) for part in far]
    if small:
        value_got = flip_y(value_far)
        corner_a, corner_b = corner_sum(near[3], got[3], *got[:3])
        corner_x, corner_y = flip_x(corner_a), flip_y(corner_b)
        pair_keep, pair_send = halves_sum(pair_own, pair_got, corner_a)
        pair_back = flip(pair_send, "dp", 2)
        to_x, to_y = sides_sum(near, got, corner_x, corner_y, value_got)
        got_x, got_y = flip_x(to_x), flip_y(to_y)
        value_keep, value_send = halves_sum(value_own, value_got, to_x)
        value_back = flip(value_send, "dp", 2)
        pair_keep, pair_send = halves_sum(pair_keep, pair_back, value_send)
        pair_last = flip(pair_send[0], "dp", 4)
        input_gradient = row_gradient(placed, mixed_back, attend_full, pair_send)
        value_keep, value_send = halves_sum(value_keep, value_back, input_gradient)
        value_last = flip(value_send[0], "dp", 4)
        mine, *sent = chip_sum(near[0], got[0], got_x, got_y, input_gradient)
        pair_grad = total_of(pair_keep[0], after(pair_last, mine))
        gradient_value = total_of(value_keep[0], after(value_last, mine))[0]
        packed_grad = total_of(mine, *[flip(sent[k - 1], "dp", 2 * k) for k in (1, 2, 3)])
        gradient_down, gradient_gate = pair_grad[0].T, pair_grad[1]
    else:
        here, across_y, across_x, corner = (add_low(near[k], got[k]) for k in range(4))
        input_gradient = row_gradient(placed, mixed_back, attend_full, placed)
        gradient_down = from_pieces(pair_own[:, 0], pair_far[:, 0]).T
        gradient_gate = from_pieces(pair_own[:, 1], pair_far[:, 1])
        gradient_value = from_pieces(value_own[:, 0], value_far[:, 0])
        packed_grad = from_pieces(
            add_low(here, flip_x(across_x)), add_low(across_y, flip_x(corner))
        )
    own_rows = attend_master.shape[0]
    gradient_attend, gradient_merge = unpack_columns(packed_grad[:own_rows], core_at)
    if small:
        gradient_norms = packed_grad[own_rows : own_rows + 1, :own_rows]
    else:
        norm_parts = jnp.concatenate([first_grads, second_grads], axis=0)
        gradient_norms = lax.psum_scatter(norm_parts, "mp", scatter_dimension=0, tiled=True)
        gradient_norms = lax.psum_scatter(gradient_norms, "dp", scatter_dimension=1, tiled=True)

    step_value = step_number[0].astype(jnp.float32)
    moment_attend, squares_attend, updated_attend = adamw_step(
        attend_master, first_attend, second_attend, gradient_attend, step_value, decay_rate
    )
    moment_merge, squares_merge, updated_merge = adamw_step(
        merge_master, first_merge, second_merge, gradient_merge, step_value, decay_rate
    )
    moment_norms, squares_norms, updated_norms = adamw_step(
        norms_master, first_norms, second_norms, gradient_norms, step_value, 0.0
    )
    moment_gate, squares_gate, updated_gate = adamw_step(
        gate_master, first_gate, second_gate, gradient_gate, step_value, decay_rate
    )
    moment_value, squares_value, updated_value = adamw_step(
        value_master, first_value, second_value, gradient_value, step_value, decay_rate
    )
    moment_down, squares_down, updated_down = adamw_step(
        down_master, first_down, second_down, gradient_down, step_value, decay_rate
    )
    return (
        layer_output,
        input_gradient,
        gradient_attend,
        gradient_merge,
        gradient_norms,
        gradient_gate,
        gradient_value,
        gradient_down,
        moment_attend,
        moment_merge,
        moment_norms,
        moment_gate,
        moment_value,
        moment_down,
        squares_attend,
        squares_merge,
        squares_norms,
        squares_gate,
        squares_value,
        squares_down,
        updated_attend,
        updated_merge,
        updated_norms,
        updated_gate,
        updated_value,
        updated_down,
    )


def solution(mesh):
    return jax.shard_map(
        shards,
        mesh=mesh,
        in_specs=(
            P(("dp", "mp"), None),
            P(),
            P(("dp", "mp"), None),
            P(("dp", "mp")),
            P(("dp", "mp"), None),
            P(("dp", "mp"), None, None),
            P(),
            P("dp", "mp"),
            P("dp", "mp"),
            P("mp", "dp"),
            P("dp", "mp"),
            P("dp", "mp"),
            P("mp", "dp"),
            P("dp", "mp"),
            P("dp", "mp"),
            P("mp", "dp"),
            P("dp", "mp"),
            P("dp", "mp"),
            P("mp", "dp"),
            P("dp", "mp"),
            P("dp", "mp"),
            P("mp", "dp"),
            P("dp", "mp"),
            P("dp", "mp"),
            P("mp", "dp"),
        ),
        out_specs=(
            P(("dp", "mp"), None),
            P(("dp", "mp"), None),
            P("dp", "mp"),
            P("dp", "mp"),
            P("mp", "dp"),
            P("dp", "mp"),
            P("dp", "mp"),
            P("mp", "dp"),
            P("dp", "mp"),
            P("dp", "mp"),
            P("mp", "dp"),
            P("dp", "mp"),
            P("dp", "mp"),
            P("mp", "dp"),
            P("dp", "mp"),
            P("dp", "mp"),
            P("mp", "dp"),
            P("dp", "mp"),
            P("dp", "mp"),
            P("mp", "dp"),
            P("dp", "mp"),
            P("dp", "mp"),
            P("mp", "dp"),
            P("dp", "mp"),
            P("dp", "mp"),
            P("mp", "dp"),
        ),
        check_vma=False,
    )
```

```python
from functools import partial

import jax
import jax.numpy as jnp
from jax import lax
from jax.experimental import pallas as pl
from jax.experimental.pallas import tpu as pltpu
from jax.sharding import PartitionSpec as P

HEADS = 12
HEAD_DIM = 64


beta_one = 0.9
beta_two = 0.999
peak_rate = 1.0
warm_steps = 4.0
total_steps = 100.0
decay_rate = 0.01
adam_eps = 1e-08
norm_eps = 1e-05


def layer_norm(row_data, gain_row, shift_row):
    centered = row_data - jnp.mean(row_data, axis=-1, keepdims=True)
    spread = jnp.mean(centered * centered, axis=-1, keepdims=True)
    return centered * lax.rsqrt(spread + norm_eps) * gain_row + shift_row


def alibi_table(head_count, seq_len):
    slopes = jnp.exp2(-8.0 * jnp.arange(1, head_count + 1, dtype=jnp.float32) / head_count)
    places = jnp.arange(seq_len, dtype=jnp.float32)
    return slopes[:, None, None] * jnp.abs(places[:, None] - places[None, :])


def dot_nn(left_op, right_op):
    return lax.dot_general(
        left_op, right_op, (((1,), (0,)), ((), ())), preferred_element_type=jnp.float32
    )


def dot_nt(left_op, right_op):
    return lax.dot_general(
        left_op, right_op, (((1,), (1,)), ((), ())), preferred_element_type=jnp.float32
    )


def dot_tn(left_op, right_op):
    return lax.dot_general(
        left_op, right_op, (((0,), (0,)), ((), ())), preferred_element_type=jnp.float32
    )


def flip(block, axis, bits):
    size = lax.axis_size(axis)
    return lax.ppermute(block, axis, [(i, i ^ bits) for i in range(size)])


def flip_core(block):
    return flip(block, "mp", 1)


def flip_x(block):
    return flip(block, "mp", 2)


def flip_y(block):
    return flip(block, "dp", 1)


def norm_stats(row_data):
    centered = row_data - jnp.mean(row_data, axis=-1, keepdims=True)
    spread = jnp.mean(centered * centered, axis=-1, keepdims=True)
    inverse = lax.rsqrt(spread + norm_eps)
    return centered * inverse, inverse


def z_groups():
    size = lax.axis_size("dp")
    return [list(range(low, size, 2)) for low in range(2)]


def pass_on(*refs):
    pass


def after(block, *others):
    return pl.pallas_call(
        pass_on,
        out_shape=jax.ShapeDtypeStruct(block.shape, block.dtype),
        in_specs=[pl.BlockSpec(memory_space=pl.ANY)] * (1 + len(others)),
        out_specs=pl.BlockSpec(memory_space=pl.ANY),
        input_output_aliases={0: 0},
        cost_estimate=pl.CostEstimate(flops=0, bytes_accessed=0, transcendentals=0),
    )(block, *others)


def is_small():
    return lax.axis_size("dp") == 8


def gather_z(block):
    far = flip(block, "dp", 4)
    return [block, far, flip(block, "dp", 2), flip(far, "dp", 2)]


def piece_rows(features):
    at = jnp.arange(8, dtype=jnp.int32)
    if is_small():
        along_z = ((at & 1) << 1) + ((at >> 1) & 1)
        at = (2 * along_z + (at >> 2)) ^ lax.axis_index("dp")
    return at * (features // 8)


def gather_whole(block):
    whole = lax.all_gather(block, "dp", axis=1, tiled=True)
    lots, features, columns = whole.shape
    whole = whole.reshape(lots, 8, features // 8, columns).transpose(1, 0, 2, 3)
    return [whole], [flip_x(whole)]


def add_low(*parts):
    return sum(part.astype(jnp.float32) for part in parts).astype(jnp.bfloat16)


def sum_dp(whole):
    return lax.psum_scatter(whole.astype(jnp.float32), "dp", scatter_dimension=0, tiled=True)


def from_pieces(*parts):
    whole = jnp.concatenate(parts, axis=0)
    return sum_dp(whole.reshape(-1, whole.shape[-1]))


MIB = 1024 * 1024
ANYWHERE = pl.BlockSpec(memory_space=pl.ANY)
IN_VMEM = pl.BlockSpec(memory_space=pltpu.VMEM)
IN_SMEM = pl.BlockSpec(memory_space=pltpu.SMEM)


def kernel_call(body, outs, specs, scratch, limit):
    return pl.pallas_call(
        body,
        out_shape=outs,
        in_specs=specs,
        out_specs=[IN_VMEM] * len(outs),
        scratch_shapes=scratch,
        compiler_params=pltpu.CompilerParams(vmem_limit_bytes=limit * MIB),
        cost_estimate=pl.CostEstimate(flops=0, bytes_accessed=0, transcendentals=0),
    )


def like(shape, dtype):
    return jax.ShapeDtypeStruct(shape, dtype)


def with_lot(groups, lot):
    return [(group, (i, lot)) for group in groups for i in range(group.shape[0])]


def load_pieces(pieces, rows, total, sems):
    copies = []
    count = total.shape[0] // 8
    for k, (group, at) in enumerate(pieces):
        to = total.at[pl.ds(pl.multiple_of(rows[k], 32), count), :]
        copies.append(pltpu.make_async_copy(group.at[(*at, pl.ds(0, count))], to, sems.at[k]))
        copies[-1].start()
    return copies


EXTRA = 16


def load_extras(groups, spots, total, sems):
    copies = []
    for group in groups:
        for i in range(group.shape[0]):
            k = len(copies)
            source = group.at[i, 0, pl.ds(group.shape[2] - EXTRA, EXTRA), :]
            copies.append(pltpu.make_async_copy(source, total.at[spots[k]], sems.at[k]))
            copies[-1].start()
    return copies


def split_low(block):
    parts = []
    for _ in range(3):
        part = lax.reduce_precision(block, 8, 7)
        parts.append(jnp.pad(part.astype(jnp.bfloat16), ((0, EXTRA - 1), (0, 128 - block.shape[1]))))
        block = block - part
    return jnp.pad(jnp.concatenate(parts, axis=1), ((0, 0), (0, 384)))


def wait_all(copies):
    for copy in copies:
        copy.wait()


def gelu_parts(gated):
    below = 0.5 + 0.5 * lax.erf(gated * 0.7071067811865476)
    return gated * below, below


def lower_lanes(shape):
    return lax.broadcasted_iota(jnp.int32, shape, 1) < 64


def unpack_columns_of(blocks, attend, merge):
    for block, (column, merge_column) in enumerate(((0, 0), (640, 256), (1152, 384), (1792, 640))):
        attend[:, column : column + 512] = blocks[block, :, :512]
        merge[:, merge_column : merge_column + 128] = blocks[block, :, 512:640]
    for pair, (column, merge_column) in enumerate(((512, 128), (1664, 512))):
        even = blocks[2 * pair, :, 640:].astype(jnp.float32)
        odd = blocks[2 * pair + 1, :, 640:].astype(jnp.float32)
        lower = lower_lanes(even.shape)
        attend[:, column : column + 128] = jnp.where(lower, even, odd).astype(jnp.bfloat16)
        mixed_up = pltpu.roll(jnp.where(lower, odd, even), 64, 1)
        merge[:, merge_column : merge_column + 128] = mixed_up.astype(jnp.bfloat16)


def first_kernel(counts, extra, places, rows, spots, start, norms_given, positions, *refs):
    low = jnp.bfloat16
    groups = []
    for count in counts:
        groups.append(refs[:count])
        refs = refs[count:]
    attend, merge, mixed, normed, *narrow, slot_sum, slot_attended, slot_narrow, norms = refs[:10]
    blocks, attended, scores, extras, sems = refs[10:]
    copies = []
    for at, group in enumerate(groups):
        copies += load_pieces(with_lot(group, 0), rows, blocks.at[places[at]], sems.at[0, at])
        if extra:
            copies += load_extras(group, spots, extras.at[places[at]], sems.at[1, at])
    wait_all(copies)
    if extra:
        for block in range(4):
            whole = jnp.zeros((8, norms.shape[1]), jnp.float32)
            for spot in range(8):
                parts = extras[block, spot].astype(jnp.float32)[:8, :]
                value = parts[:, :128] + parts[:, 128:256] + parts[:, 256:384]
                value = jnp.concatenate([value, jnp.zeros((8, norms.shape[1] - 128), jnp.float32)], axis=1)
                whole = whole + (pltpu.roll(value, spot * (norms.shape[1] // 8), 1) if spot else value)
            norms[block : block + 1, :] = whole[:1, :]
    else:
        norms[...] = norms_given[...]
    unpack_columns_of(blocks, attend, merge)
    width = merge.shape[0]
    length = 128
    slots = 32
    scale = HEAD_DIM ** (-0.5)
    for column in range(0, 3 * width, 256):
        cut = slice(column, column + 256)
        mixed[:, cut] = dot_nn(start[...], attend[:, cut]).astype(low)
    shape = (length, length)
    apart = jnp.abs(
        lax.broadcasted_iota(jnp.int32, shape, 0) - lax.broadcasted_iota(jnp.int32, shape, 1)
    ).astype(jnp.float32)
    lower = lower_lanes(shape)

    def step(target, first, seq, carry):
        at = pl.ds(pl.multiple_of(seq * length, length), length)
        to = pl.ds(pl.multiple_of(seq * slots, slots), slots)
        for pair in range(HEADS // 2):
            column = 2 * HEAD_DIM * pair
            queries = mixed[at, column : column + 128]
            keys = mixed[at, width + column : width + column + 128]
            zero = jnp.zeros_like(queries)
            for half in range(2):
                own = jnp.where(lower, queries, zero) if half == 0 else jnp.where(lower, zero, queries)
                head = 2 * pair + half
                scores[head] = dot_nt(own, keys) * scale - apart * slopes_of(head)
        raised = scores[...]
        raised = jnp.exp(raised - jnp.max(raised, axis=-1, keepdims=True))
        scores[...] = raised / jnp.sum(raised, axis=-1, keepdims=True)
        for pair in range(HEADS // 2):
            column = 2 * HEAD_DIM * pair
            values = mixed[at, 2 * width + column : 2 * width + column + 128]
            heads = [dot_nn(scores[2 * pair + half].astype(low), values) for half in range(2)]
            attended[at, column : column + 128] = jnp.where(lower, heads[0], heads[1]).astype(low)
        total = start[at, :].astype(jnp.float32) + dot_nn(attended[at, :], merge[...])
        xhat, _ = norm_stats(total)
        rows = xhat * norms[0:1, :] + norms[1:2, :]
        normed[at, :] = rows
        target[pl.ds(pl.multiple_of((seq - first) * length, length), length), :] = rows.astype(low)
        selector = one_hot(positions[to, :], length)
        slot_sum[to, :] = select_exact(selector, total)
        slot_attended[to, :] = dot_nn(selector, attended[at, :]).astype(low)
        slot_narrow[to, :] = dot_nn(selector, rows.astype(low)).astype(low)
        return carry

    seqs = start.shape[0] // length // 2
    lax.fori_loop(0, seqs, partial(step, narrow[0], 0), 0, unroll=True)
    lax.fori_loop(seqs, 2 * seqs, partial(step, narrow[1], seqs), 0, unroll=True)


def first_part(extra, places, rows, spots, start, norms, positions, groups):
    count, width = start.shape
    slot_rows = positions.shape[0]
    low = jnp.bfloat16
    return kernel_call(
        partial(first_kernel, [len(group) for group in groups], extra),
        [
            like((width, 3 * width), low),
            like((width, width), low),
            like((count, 3 * width), low),
            like((count, width), jnp.float32),
            like((count // 2, width), low),
            like((count // 2, width), low),
            like((slot_rows, width), jnp.float32),
            like((slot_rows, width), low),
            like((slot_rows, width), low),
            like((4, width), jnp.float32),
        ],
        [IN_SMEM] * 3 + [IN_VMEM] * 3 + [ANYWHERE] * sum(map(len, groups)),
        [
            pltpu.VMEM((4, width, width), low),
            pltpu.VMEM((count, width), low),
            pltpu.VMEM((HEADS, 128, 128), jnp.float32),
            pltpu.VMEM((4, 8, EXTRA, width), low),
            pltpu.SemaphoreType.DMA((2, 4, 8)),
        ], 30)(places, rows, spots, start, norms, positions, *sum(groups, []))


def pack_columns(attend, merge, core_at):
    even = jnp.concatenate(
        [attend[:, :512], merge[:, :128], attend[:, 512:], merge[:, 128:]], axis=1
    )
    odd = jnp.concatenate([attend[:, 64:], merge[:, 64:], merge[:, :64], attend[:, :64]], axis=1)
    return jnp.where(core_at == 0, even, odd)


def unpack_columns(packed, core_at):
    even = jnp.concatenate([packed[:, :512], packed[:, 640:704]], axis=1)
    odd = jnp.concatenate([packed[:, 704:], packed[:, :512]], axis=1)
    even_merge = jnp.concatenate([packed[:, 512:640], packed[:, 704:]], axis=1)
    odd_merge = jnp.concatenate([packed[:, 640:704], packed[:, 512:640]], axis=1)
    return jnp.where(core_at == 0, even, odd), jnp.where(core_at == 0, even_merge, odd_merge)


def front_kernel(count, rows, *refs):
    sources, refs = refs[:4], refs[4:]
    near, far = refs[: count[0]], refs[count[0] : count[0] + count[1]]
    hidden, gates, values, sems = refs[-4:]
    copies = []
    for k, groups in enumerate((near, far)):
        copies.append(
            load_pieces(with_lot(groups, 0), rows, gates.at[k], sems.at[k, 0])
            + load_pieces(with_lot(groups, 1), rows, values.at[k], sems.at[k, 1])
        )
    quarter = sources[0].shape[0]
    for k in range(2):
        wait_all(copies[k])
        for part, source in enumerate(sources):
            start = part * quarter

            def step(tile, carry, k=k, start=start, source=source):
                block = source[pl.ds(pl.multiple_of(tile * 256, 256), 256), :]
                to = pl.ds(pl.multiple_of(start + tile * 256, 256), 256)
                for column in range(0, gates.shape[2], 256):
                    cut = slice(column, column + 256)
                    gated = dot_nn(block, gates[k, :, cut])
                    valued = dot_nn(block, values[k, :, cut])
                    hidden[k, to, cut] = (gelu_parts(gated)[0] * valued).astype(jnp.bfloat16)
                return carry

            lax.fori_loop(0, source.shape[0] // 256, step, 0)


def ffn_front(rows, sources, near, far, *earlier):
    quarter, width = sources[0].shape
    return kernel_call(
        partial(front_kernel, (len(near), len(far))),
        [like((2, 4 * quarter, width), jnp.bfloat16)],
        [IN_SMEM] + [IN_VMEM] * 4 + [ANYWHERE] * (len(near) + len(far) + len(earlier)),
        [
            pltpu.VMEM((2, width, width), jnp.bfloat16),
            pltpu.VMEM((2, width, width), jnp.bfloat16),
            pltpu.SemaphoreType.DMA((2, 2, 8)),
        ], 18)(rows, *sources, *near, *far, *earlier)[0]


def down_kernel(lots, rows, hidden, *refs):
    split, end = len(lots[0]), len(lots[0]) + len(lots[1])
    mine, other, downs, sems = refs[end + 1 :]
    copies = load_pieces(zip(refs[:split], lots[0]), rows, downs.at[0], sems.at[0])
    copies += load_pieces(zip(refs[split:end], lots[1]), rows, downs.at[1], sems.at[1])
    wait_all(copies)
    half = mine.shape[0]
    for part, target in ((1, other), (0, mine)):

        def step(tile, carry, part=part, target=target):
            at = pl.ds(pl.multiple_of(part * half + tile * 256, 256), 256)
            to = pl.ds(pl.multiple_of(tile * 256, 256), 256)
            target[to, :] = dot_nt(hidden[0, at, :], downs[0]) + dot_nt(hidden[1, at, :], downs[1])
            return carry

        lax.fori_loop(0, half // 256, step, 0)


def ffn_down(rows, hidden, near, far, earlier):
    both, width = hidden.shape[1:]
    return kernel_call(
        partial(down_kernel, [[lot for _, lot in group] for group in (near, far)]),
        [like((both // 2, width), jnp.float32)] * 2,
        [IN_SMEM, IN_VMEM] + [ANYWHERE] * (len(near) + len(far) + 1),
        [pltpu.VMEM((2, width, width), jnp.bfloat16), pltpu.SemaphoreType.DMA((2, 8))], 16)(rows, hidden, *[group for group, _ in near + far], earlier)


def select_exact(selector, block):
    first = block.astype(jnp.bfloat16)
    rest = block - first.astype(jnp.float32)
    second = rest.astype(jnp.bfloat16)
    third = (rest - second.astype(jnp.float32)).astype(jnp.bfloat16)
    return dot_nn(selector, first) + dot_nn(selector, second) + dot_nn(selector, third)


def norm_back(xhat, inverse, gain_row, incoming):
    scaled = incoming * gain_row
    inner = jnp.mean(scaled * xhat, axis=-1, keepdims=True)
    back = inverse * (scaled - jnp.mean(scaled, axis=-1, keepdims=True) - xhat * inner)
    gain_back = jnp.sum(incoming * xhat, axis=0, keepdims=True)
    return back, gain_back, jnp.sum(incoming, axis=0, keepdims=True)


def one_hot(positions, length):
    shape = (positions.shape[0], length)
    return (positions == lax.broadcasted_iota(jnp.int32, shape, 1)).astype(jnp.bfloat16)


def second_kernel(
    normed, part, got, norms, positions, live, cotangent, output, pulled, back, norm_grads
):
    slots = cotangent.shape[1]
    length = normed.shape[0] // cotangent.shape[0]
    norm_grads[...] = jnp.zeros_like(norm_grads)

    def step(seq, carry):
        at = pl.ds(pl.multiple_of(seq * length, length), length)
        to = pl.ds(pl.multiple_of(seq * slots, slots), slots)
        total = normed[at, :] + part[at, :] + got[at, :]
        xhat, _ = norm_stats(total)
        output[at, :] = (xhat * norms[2:3, :] + norms[3:4, :]).astype(jnp.bfloat16)
        selector = one_hot(positions[to, :], length)
        xhat, inverse = norm_stats(select_exact(selector, total))
        incoming = jnp.where(live[to, :] > 0, cotangent[seq].astype(jnp.float32), 0.0)
        slot_back, gain_back, shift_back = norm_back(xhat, inverse, norms[2:3, :], incoming)
        back[to, :] = slot_back
        pulled[to, :] = slot_back.astype(jnp.bfloat16)
        norm_grads[0:1, :] += gain_back
        norm_grads[1:2, :] += shift_back
        return carry

    lax.fori_loop(0, cotangent.shape[0], step, 0, unroll=True)


def second_norm(normed, part, got, norms, positions, live, cotangent):
    count, width = normed.shape
    slot_rows = positions.shape[0]
    return kernel_call(
        second_kernel,
        [
            like((count, width), jnp.bfloat16),
            like((slot_rows, width), jnp.bfloat16),
            like((slot_rows, width), jnp.float32),
            like((2, width), jnp.float32),
        ],
        [IN_VMEM] * 7,
        [], 14)(normed, part, got, norms, positions, live, cotangent)


def back_kernel(count, lots, rows, *refs):
    pulls, narrows = refs[0:4], refs[4:8]
    wide, deep = refs[8 : 8 + count[0]], refs[8 + count[0] : 8 + count[0] + count[1]]
    keep, send, pull_rows, work_rows, gate_back, value_back, hidden = refs[
        8 + count[0] + count[1] : -4
    ]
    gates, values, downs, sems = refs[-4:]
    copies = load_pieces(with_lot(wide, 0), rows, gates, sems.at[0])
    copies += load_pieces(with_lot(wide, 1), rows, values, sems.at[1])
    copies += load_pieces(zip(deep, lots), rows, downs, sems.at[2])
    size = pulls[0].shape[0]
    for k in range(4):
        pull_rows[k * size : (k + 1) * size, :] = pulls[k][...]
        work_rows[k * size : (k + 1) * size, :] = narrows[k][...]
    wait_all(copies)
    for column in range(0, gates.shape[1], 256):
        cut = slice(column, column + 256)
        gated = dot_nn(work_rows[...], gates[:, cut])
        valued = dot_nn(work_rows[...], values[:, cut])
        hidden_back = dot_nn(pull_rows[...], downs[:, cut])
        gelu, below = gelu_parts(gated)
        slope = below + gated * (0.3989422804014327 * jnp.exp(-0.5 * gated * gated))
        hidden[:, cut] = (gelu * valued).astype(jnp.bfloat16)
        gate_back[:, cut] = (hidden_back * valued * slope).astype(jnp.bfloat16)
        value_back[:, cut] = (hidden_back * gelu).astype(jnp.bfloat16)
    for column in range(0, gates.shape[0], 256):
        cut = slice(column, column + 256)
        total = dot_nt(gate_back[...], gates[cut, :]) + dot_nt(value_back[...], values[cut, :])
        for k, target in enumerate((keep, keep, send, send)):
            target[k % 2, :, cut] = total[k * size : (k + 1) * size]


def ffn_back(rows, pulls, narrows, wide, deep):
    size, width = pulls[0].shape
    low = jnp.bfloat16
    return kernel_call(
        partial(back_kernel, (len(wide), len(deep)), [lot for _, lot in deep]),
        [like((2, size, width), jnp.float32)] * 2 + [like((4 * size, width), low)] * 5,
        [IN_SMEM] + [IN_VMEM] * 8 + [ANYWHERE] * (len(wide) + len(deep)),
        [pltpu.VMEM((width, width), low)] * 3 + [pltpu.SemaphoreType.DMA((3, 8))], 22)(rows, *pulls, *narrows, *wide, *[group for group, _ in deep])


def store_pieces(total, rows, mine, other):
    count = total.shape[0] // 8
    for k in range(8):
        at = pl.ds(pl.multiple_of(rows[k], 32), count)
        to = mine if k < 4 else other
        to[k % 4, :count, :] = total[at, :]


def grads_kernel(lots, rows, *refs):
    factors, refs = refs[: 2 * lots], refs[-3 - lots :]
    mine, other, total, turned = refs[0], refs[1], refs[2], refs[3:]
    for lot in range(lots):
        turned[lot][...] = factors[2 * lot][...].T
    for lot in range(lots):
        for column in range(0, total.shape[1], 256):
            cut = slice(column, column + 256)
            product = dot_nn(turned[lot][...], factors[2 * lot + 1][:, cut])
            total[:, cut] = product.astype(jnp.bfloat16)
        store_pieces(total, rows, mine.at[:, lot], other.at[:, lot])


def ffn_grads(rows, factors, *earlier):
    size, width = factors[0].shape
    lots = len(factors) // 2
    low = jnp.bfloat16
    return kernel_call(
        partial(grads_kernel, lots),
        [like((4, lots, width // 8, width), low)] * 2,
        [IN_SMEM] + [IN_VMEM] * len(factors) + [ANYWHERE] * len(earlier),
        [pltpu.VMEM((width, width), low)] + [pltpu.VMEM((width, size), low)] * lots, 16)(rows, *factors, *earlier)


def split_kernel(from_y, from_x, *refs):
    first, second, sems = refs[-3:]
    half = first.shape[0]
    copies = [
        pltpu.make_async_copy(from_y.at[pl.ds(0, half)], first, sems.at[0]),
        pltpu.make_async_copy(from_x.at[pl.ds(half, half)], second, sems.at[1]),
    ]
    for copy in copies:
        copy.start()
    wait_all(copies)


def split_halves(from_y, from_x, *earlier):
    half = like((from_y.shape[0] // 2,) + from_y.shape[1:], from_y.dtype)
    return kernel_call(
        split_kernel,
        [half, half],
        [ANYWHERE] * (2 + len(earlier)),
        [pltpu.SemaphoreType.DMA((2,))], 6)(from_y, from_x, *earlier)


def cast_kernel(first, second, _, both):
    both[0] = first[...].astype(jnp.bfloat16)
    both[1] = second[...].astype(jnp.bfloat16)


def cast_wide(first, second, earlier):
    return kernel_call(
        cast_kernel,
        [like((2,) + first.shape, jnp.bfloat16)],
        [IN_VMEM] * 2 + [ANYWHERE],
        [], 4)(first, second, earlier)[0]


def wide_sum(*blocks):
    return sum(block.astype(jnp.float32) for block in blocks)


def total_of(*blocks):
    return wide_sum(*blocks)


def corner_kernel(near, got, *refs):
    first, second = refs[-2:]
    for k in range(4):
        target = first if k < 2 else second
        target[k % 2] = wide_sum(near[k], got[k]).astype(jnp.bfloat16)


def corner_sum(near, got, *earlier):
    half = like((2,) + near.shape[1:], near.dtype)
    return kernel_call(
        corner_kernel, [half, half], [IN_VMEM] * 2 + [ANYWHERE] * len(earlier), [], 6)(near, got, *earlier)


def sides_kernel(near_y, got_y, near_x, got_x, corner_x, corner_y, _, to_x, to_y):
    for k in range(4):
        corner = [corner_x[k]] if k < 2 else []
        to_y[k] = wide_sum(near_y[k], got_y[k], *corner).astype(jnp.bfloat16)
        corner = [corner_y[k - 2]] if k >= 2 else []
        to_x[k] = wide_sum(near_x[k], got_x[k], *corner).astype(jnp.bfloat16)


def sides_sum(near, got, corner_x, corner_y, earlier):
    side = like(near[1].shape, near[1].dtype)
    return kernel_call(sides_kernel, [side, side], [IN_VMEM] * 6 + [ANYWHERE], [], 10)(
        near[1], got[1], near[2], got[2], corner_x, corner_y, earlier
    )


def chip_kernel(near, got, got_x, got_y, _, mine, far, side, last):
    for k, target in enumerate((mine, far, side, last)):
        total = wide_sum(near[k], got[k], got_x[k], got_y[k])
        target[...] = total.astype(target.dtype)


def chip_sum(near, got, got_x, got_y, earlier):
    piece = near.shape[1:]
    mine, far, side, last = kernel_call(
        chip_kernel,
        [like(piece, jnp.float32)] + [like(piece, near.dtype)] * 3,
        [IN_VMEM] * 4 + [ANYWHERE],
        [], 8)(near, got, got_x, got_y, earlier)
    return mine, side, far, last


def halves_kernel(mine, got, *refs):
    keep, send = refs[-2:]
    half = keep.shape[0]
    for k in range(half):
        keep[k] = wide_sum(mine[k], got[k]).astype(keep.dtype)
        send[k] = wide_sum(mine[half + k], got[half + k]).astype(send.dtype)


def halves_sum(mine, got, *earlier):
    half = like((mine.shape[0] // 2,) + mine.shape[1:], mine.dtype)
    return kernel_call(
        halves_kernel, [half, half], [IN_VMEM] * 2 + [ANYWHERE] * len(earlier), [], 8)(mine, got, *earlier)


def row_gradient_kernel(placed, mixed_back, attend, _, output):
    for column in range(0, placed.shape[1], 256):
        cut = slice(column, column + 256)
        output[:, cut] = placed[:, cut] + dot_nt(mixed_back[...], attend[cut, :])


def row_gradient(placed, mixed_back, attend, earlier):
    count, width = placed.shape
    return kernel_call(
        row_gradient_kernel,
        [like(placed.shape, placed.dtype)],
        [IN_VMEM] * 3 + [ANYWHERE],
        [], 14)(placed, mixed_back, attend, earlier)[0]


def slopes_of(head):
    return 2.0 ** (-8.0 * (head + 1) / HEADS)


def attend_kernel(
    extra,
    rows,
    columns,
    spots,
    second_grads,
    keep,
    got,
    second_back,
    slot_sum,
    norms,
    merge,
    mixed,
    slot_attended,
    start,
    positions,
    _,
    placed,
    mixed_back,
    norm_grads,
    *refs,
):
    near, far = refs[0:4], refs[4:8]
    merge_grad, total, branch, attended_back, first_back, turned, extras = refs[8:]
    width = norms.shape[1]
    slots = 32
    length = 128
    low = jnp.bfloat16
    scale = HEAD_DIM ** (-0.5)
    xhat, inverse = norm_stats(slot_sum[...])
    incoming = keep[...] + got[...].astype(jnp.float32) + second_back[...]
    slot_back, gain_back, shift_back = norm_back(xhat, inverse, norms[0:1, :], incoming)
    norm_grads[0:1, :] = gain_back
    norm_grads[1:2, :] = shift_back
    if extra:
        both = [gain_back, shift_back, second_grads[0:1, :], second_grads[1:2, :]]
        zero_rows = jnp.zeros((EXTRA - 1, width), jnp.float32)
        for block in range(4):
            whole = jnp.concatenate([both[block], zero_rows], axis=0)
            for spot in range(8):
                turn = (8 - spot) % 8 * (width // 8)
                extras[block, spot] = (pltpu.roll(whole, turn, 1) if turn else whole).astype(low)
    first_back[...] = slot_back
    branch[...] = slot_back.astype(low)
    attended_back[...] = dot_nt(branch[...], merge[...]).astype(low)
    merge_grad[...] = dot_tn(slot_attended[...], branch[...])
    lane_head = lax.broadcasted_iota(jnp.int32, (slots, width), 1) // HEAD_DIM

    def apart_heads(block):
        zero = jnp.zeros_like(block)
        return jnp.concatenate(
            [jnp.where(lane_head == head, block, zero) for head in range(HEADS)], axis=0
        )

    def join_heads(block):
        total = jnp.zeros((slots, width), jnp.float32)
        for head in range(HEADS):
            total = jnp.where(lane_head == head, block[head * slots : (head + 1) * slots], total)
        return total

    def step(seq, carry):
        at = pl.ds(pl.multiple_of(seq * length, length), length)
        to = pl.ds(pl.multiple_of(seq * slots, slots), slots)
        spots = positions[to, :]
        selector = one_hot(spots, length)
        apart = jnp.abs(
            spots - lax.broadcasted_iota(jnp.int32, (slots, length), 1)
        ).astype(jnp.float32)
        keys = mixed[at, width : 2 * width]
        values = mixed[at, 2 * width :]
        queries = apart_heads(dot_nn(selector, mixed[at, :width])).astype(low)
        heads_back = apart_heads(attended_back[to, :].astype(jnp.float32)).astype(low)
        bias = jnp.concatenate([apart * slopes_of(head) for head in range(HEADS)], axis=0)
        scores = dot_nt(queries, keys) * scale - bias
        exp_scores = jnp.exp(scores - jnp.max(scores, axis=-1, keepdims=True))
        probs = exp_scores / jnp.sum(exp_scores, axis=-1, keepdims=True)
        probs_back = dot_nt(heads_back, values)
        inner = jnp.sum(probs * probs_back, axis=-1, keepdims=True)
        scores_back = (probs * (probs_back - inner)).astype(low)
        queries_back = (join_heads(dot_nn(scores_back, keys)) * scale).astype(low)
        mixed_back[at, :width] = dot_tn(selector, queries_back).astype(low)
        mixed_back[at, width : 2 * width] = (dot_tn(scores_back, queries) * scale).astype(low)
        mixed_back[at, 2 * width :] = dot_tn(probs.astype(low), heads_back).astype(low)
        spread = (spots == lax.broadcasted_iota(jnp.int32, (slots, length), 1)).astype(jnp.float32)
        placed[at, :] = select_exact(jnp.transpose(spread).astype(low), first_back[to, :])
        return carry

    lax.fori_loop(0, mixed.shape[0] // length, step, 0, unroll=True)
    turned[...] = start[...].T
    for core, target in ((1, far), (0, near)):
        for k in range(2):
            base = 6 * (2 * core + k)
            for part in range(2):
                column = pl.ds(pl.multiple_of(columns[base] + 256 * part, 128), 256)
                product = dot_nn(turned[...], mixed_back[:, column])
                total[:, 256 * part : 256 * part + 256] = product.astype(low)
            column = pl.ds(pl.multiple_of(columns[base + 1], 128), 128)
            total[:, 512:640] = merge_grad[:, column].astype(low)
            column = pl.ds(pl.multiple_of(columns[base + 2], 128), 128)
            single = dot_nn(turned[...], mixed_back[:, column])
            column = pl.ds(pl.multiple_of(columns[base + 3], 128), 128)
            merged = pltpu.roll(merge_grad[:, column], 64, 1)
            attend_lane = lower_lanes(single.shape) == (columns[base + 4] == 0)
            total[:, 640:] = jnp.where(attend_lane, single, merged).astype(low)
            sides = target[2 * k : 2 * k + 2]
            store_pieces(total, rows, *sides)
            if extra:
                for j in range(8):
                    sides[j // 4][j % 4, width // 8 :, :] = extras[columns[base + 5], spots[j]]


def attend_back(extra, rows, columns, spots, second_grads, *blocks):
    start, mixed = blocks[8], blocks[6]
    count, width = start.shape
    slot_rows = blocks[0].shape[0]
    low = jnp.bfloat16
    return kernel_call(
        partial(attend_kernel, extra),
        [
            like((count, width), jnp.float32),
            like(mixed.shape, low),
            like((2, width), jnp.float32),
        ]
        + [like((4, width // 8 + (EXTRA if extra else 0), width), low)] * 8,
        [IN_SMEM] * 3 + [IN_VMEM] * 11 + [ANYWHERE],
        [
            pltpu.VMEM((width, width), jnp.float32),
            pltpu.VMEM((width, width), low),
            pltpu.VMEM((slot_rows, width), low),
            pltpu.VMEM((slot_rows, width), low),
            pltpu.VMEM((slot_rows, width), jnp.float32),
            pltpu.VMEM((width, count), low),
            pltpu.VMEM((4, 8, EXTRA, width), low),
        ], 32)(rows, columns, spots, second_grads, *blocks)


def adamw_step(master, first, second, gradient, step_value, decay):
    step_rate = peak_rate * jnp.minimum(
        step_value / warm_steps, (total_steps - step_value) / (total_steps - warm_steps)
    )
    fix_one = 1.0 - jnp.power(jnp.float32(beta_one), step_value)
    fix_two = 1.0 - jnp.power(jnp.float32(beta_two), step_value)
    moment = beta_one * first + (1.0 - beta_one) * gradient
    squares = beta_two * second + (1.0 - beta_two) * gradient * gradient
    updated = master - step_rate * (
        moment / fix_one / (jnp.sqrt(squares / fix_two) + adam_eps) + decay * master
    )
    return (moment, squares, updated)


def shards(
    hidden_rows,
    token_table,
    masked_positions,
    masked_counts,
    replace_rows,
    masked_cotangent,
    step_number,
    attend_master,
    merge_master,
    norms_master,
    gate_master,
    value_master,
    down_master,
    first_attend,
    first_merge,
    first_norms,
    first_gate,
    first_value,
    first_down,
    second_attend,
    second_merge,
    second_norms,
    second_gate,
    second_value,
    second_down,
):
    local_seqs, slot_count = masked_positions.shape
    local_rows, model_width = hidden_rows.shape
    length = local_rows // local_seqs
    slot_rows = local_seqs * slot_count
    dp_size = lax.axis_size("dp")
    core_at = lax.axis_index("mp") & 1
    x_at = lax.axis_index("mp") >> 1
    low = jnp.bfloat16
    rows = piece_rows(model_width)

    packed = pack_columns(attend_master.astype(low), merge_master.astype(low), core_at)[None]
    small = is_small()
    deep = down_master.astype(low).T[None]

    order = [(core, k) for core in range(2) for k in range(2)]
    places = [2 * (x_at ^ k) + (core_at ^ core) for core, k in order]
    table = jnp.array(
        [
            [0, 0, 512, 128, 0, 0],
            [640, 256, 512, 128, 1, 1],
            [1152, 384, 1664, 512, 0, 2],
            [1792, 640, 1664, 512, 1, 3],
        ],
        jnp.int32,
    )
    columns = jnp.concatenate([table[place] for place in places])
    places = jnp.stack(places).astype(jnp.int32)
    spots = piece_rows(8)
    if small:
        packed = jnp.concatenate([packed, split_low(norms_master)[None]], axis=1)
        packed_z = [packed] + [flip(packed, "dp", 2 * k) for k in (2, 1, 3)]
        wide = cast_wide(gate_master, value_master, packed_z[2])

        deep = after(deep, packed_z[2])
        deep_y, deep_x = flip_y(deep), flip_x(deep)
        replace_rows = after(replace_rows, deep_y)

    live_slots = jnp.arange(slot_count, dtype=jnp.int32)[None, :] < masked_counts[:, None]
    at_slot = masked_positions[:, :, None] == jnp.arange(length, dtype=jnp.int32)[None, None, :]
    place_bool = at_slot & live_slots[:, :, None]
    chosen = jnp.take(token_table, replace_rows.reshape(-1), axis=0).reshape(
        local_seqs, slot_count, model_width
    )
    swapped = jnp.einsum(
        "sjt,sjd->std", place_bool.astype(low), chosen, preferred_element_type=jnp.float32
    ).astype(low)
    replaced = jnp.any(place_bool, axis=1)[:, :, None]
    start_rows = jnp.where(
        replaced, swapped, hidden_rows.reshape(local_seqs, length, model_width)
    ).reshape(local_rows, model_width)
    positions = masked_positions.reshape(slot_rows, 1)
    live = live_slots.astype(jnp.float32).reshape(slot_rows, 1)
    indices = [rows, places, columns, spots, positions, live]
    if small:
        deep_parts = jnp.concatenate([deep, deep_y, deep_x, flip_x(deep_y)])
        packed_z[0] = after(packed_z[0], wide, deep_parts, *indices)
        wide_z = gather_z(after(wide, packed_z[1], packed_z[3]))
        packed_z = jnp.stack(packed_z)
        packed_y, packed_x = flip_y(packed_z), flip_x(packed_z)
        first_half, second_half = split_halves(packed_y, packed_x, wide_z[1], wide_z[2], start_rows)
        packed_near = [packed_z, packed_y]
        packed_far = [packed_x, flip_x(first_half), flip_y(second_half)]
        wide_z[0] = after(wide_z[0], *packed_far[1:])
        deep_z = gather_z(after(deep_parts, *wide_z[1:])[None])
        wide_z = jnp.stack(wide_z)
        wide_y, wide_x = flip_y(wide_z), flip_x(wide_z)
        norms = jnp.zeros((4, model_width), jnp.float32)
    else:
        packed_near, packed_far = gather_whole(packed)
        norms = lax.all_gather(norms_master, "dp", axis=1, tiled=True)
        norms = lax.all_gather(norms, "mp", axis=0, tiled=True)

    packed_groups = [packed_near, packed_far]
    packed_groups += [[flip_core(part) for part in group] for group in packed_groups]
    (
        attend_full,
        merge_full,
        mixed,
        normed,
        narrow,
        narrow_end,
        slot_sum,
        slot_attended,
        slot_narrow,
        norms,
    ) = first_part(
        small,
        places,
        rows,
        spots,
        start_rows,
        norms,
        positions,
        packed_groups,
    )
    if small:
        first_half, second_half = split_halves(wide_y, wide_x, narrow, deep_z[2])
        wide_near = [wide_z, wide_y]
        wide_far = [wide_x, flip_x(first_half), flip_y(second_half)]
        deep_near = [(part, (0, side)) for side in (0, 1) for part in deep_z]
        deep_far = [(part, (0, side)) for side in (2, 3) for part in deep_z]
    else:
        wide_near, wide_far = gather_whole(
            jnp.stack([gate_master.astype(low), value_master.astype(low)])
        )
        deep_near, deep_far = (with_lot(group, 0) for group in gather_whole(deep))

    def over_group(block):
        other_x = flip_x(block)
        return [block, other_x, flip_core(block), flip_core(other_x)]


    chip_rows = (narrow, narrow_end, flip_core(narrow), flip_core(narrow_end))
    earlier = [deep_z[1] if small else rows]
    hidden = ffn_front(rows, chip_rows, wide_near, wide_far, *earlier)
    narrows = over_group(after(slot_narrow, hidden))
    ffn_mine, ffn_other = ffn_down(rows, hidden, deep_near, deep_far, rows)
    layer_output, pulled, second_back, second_grads = second_norm(
        normed, ffn_mine, flip_core(ffn_other), norms, positions, live, masked_cotangent
    )

    keep, send, *factors = ffn_back(rows, over_group(pulled), narrows, wide_near, deep_near)
    pull_rows, work_rows, gate_back, value_back, slot_hidden = factors
    chip_back = keep + flip_core(send)
    pair_own, pair_far = ffn_grads(rows, (pull_rows, slot_hidden, work_rows, gate_back))
    value_own, value_far = ffn_grads(rows, (work_rows, value_back), pair_own)
    if small:
        pair_got = flip_y(pair_far)
    placed, mixed_back, first_grads, *parts = attend_back(
        small,
        rows,
        columns,
        spots,
        second_grads,
        chip_back[0],
        flip_x(chip_back[1].astype(low)),
        second_back,
        slot_sum,
        norms,
        merge_full,
        mixed,
        slot_attended,
        start_rows,
        positions,
        value_far,
    )
    near, far = parts[:4], parts[4:]
    got = [flip_core(part) for part in far]
    if small:
        value_got = flip_y(value_far)
        corner_a, corner_b = corner_sum(near[3], got[3], *got[:3])
        corner_x, corner_y = flip_x(corner_a), flip_y(corner_b)
        pair_keep, pair_send = halves_sum(pair_own, pair_got, corner_a)
        pair_back = flip(pair_send, "dp", 2)
        to_x, to_y = sides_sum(near, got, corner_x, corner_y, value_got)
        got_x, got_y = flip_x(to_x), flip_y(to_y)
        value_keep, value_send = halves_sum(value_own, value_got, to_x)
        value_back = flip(value_send, "dp", 2)
        pair_keep, pair_send = halves_sum(pair_keep, pair_back, value_send)
        pair_last = flip(pair_send[0], "dp", 4)
        input_gradient = row_gradient(placed, mixed_back, attend_full, pair_send)
        value_keep, value_send = halves_sum(value_keep, value_back, input_gradient)
        value_last = flip(value_send[0], "dp", 4)
        mine, *sent = chip_sum(near[0], got[0], got_x, got_y, input_gradient)
        pair_grad = total_of(pair_keep[0], after(pair_last, mine))
        gradient_value = total_of(value_keep[0], after(value_last, mine))[0]
        packed_grad = total_of(mine, *[flip(sent[k - 1], "dp", 2 * k) for k in (1, 2, 3)])
        gradient_down, gradient_gate = pair_grad[0].T, pair_grad[1]
    else:
        here, across_y, across_x, corner = (add_low(near[k], got[k]) for k in range(4))
        input_gradient = row_gradient(placed, mixed_back, attend_full, placed)
        gradient_down = from_pieces(pair_own[:, 0], pair_far[:, 0]).T
        gradient_gate = from_pieces(pair_own[:, 1], pair_far[:, 1])
        gradient_value = from_pieces(value_own[:, 0], value_far[:, 0])
        packed_grad = from_pieces(
            add_low(here, flip_x(across_x)), add_low(across_y, flip_x(corner))
        )
    own_rows = attend_master.shape[0]
    gradient_attend, gradient_merge = unpack_columns(packed_grad[:own_rows], core_at)
    if small:
        gradient_norms = packed_grad[own_rows : own_rows + 1, :own_rows]
    else:
        norm_parts = jnp.concatenate([first_grads, second_grads], axis=0)
        gradient_norms = lax.psum_scatter(norm_parts, "mp", scatter_dimension=0, tiled=True)
        gradient_norms = lax.psum_scatter(gradient_norms, "dp", scatter_dimension=1, tiled=True)

    step_value = step_number[0].astype(jnp.float32)
    moment_attend, squares_attend, updated_attend = adamw_step(
        attend_master, first_attend, second_attend, gradient_attend, step_value, decay_rate
    )
    moment_merge, squares_merge, updated_merge = adamw_step(
        merge_master, first_merge, second_merge, gradient_merge, step_value, decay_rate
    )
    moment_norms, squares_norms, updated_norms = adamw_step(
        norms_master, first_norms, second_norms, gradient_norms, step_value, 0.0
    )
    moment_gate, squares_gate, updated_gate = adamw_step(
        gate_master, first_gate, second_gate, gradient_gate, step_value, decay_rate
    )
    moment_value, squares_value, updated_value = adamw_step(
        value_master, first_value, second_value, gradient_value, step_value, decay_rate
    )
    moment_down, squares_down, updated_down = adamw_step(
        down_master, first_down, second_down, gradient_down, step_value, decay_rate
    )
    return (
        layer_output,
        input_gradient,
        gradient_attend,
        gradient_merge,
        gradient_norms,
        gradient_gate,
        gradient_value,
        gradient_down,
        moment_attend,
        moment_merge,
        moment_norms,
        moment_gate,
        moment_value,
        moment_down,
        squares_attend,
        squares_merge,
        squares_norms,
        squares_gate,
        squares_value,
        squares_down,
        updated_attend,
        updated_merge,
        updated_norms,
        updated_gate,
        updated_value,
        updated_down,
    )


def solution(mesh):
    return jax.shard_map(
        shards,
        mesh=mesh,
        in_specs=(
            P(("dp", "mp"), None),
            P(),
            P(("dp", "mp"), None),
            P(("dp", "mp")),
            P(("dp", "mp"), None),
            P(("dp", "mp"), None, None),
            P(),
            P("dp", "mp"),
            P("dp", "mp"),
            P("mp", "dp"),
            P("dp", "mp"),
            P("dp", "mp"),
            P("mp", "dp"),
            P("dp", "mp"),
            P("dp", "mp"),
            P("mp", "dp"),
            P("dp", "mp"),
            P("dp", "mp"),
            P("mp", "dp"),
            P("dp", "mp"),
            P("dp", "mp"),
            P("mp", "dp"),
            P("dp", "mp"),
            P("dp", "mp"),
            P("mp", "dp"),
        ),
        out_specs=(
            P(("dp", "mp"), None),
            P(("dp", "mp"), None),
            P("dp", "mp"),
            P("dp", "mp"),
            P("mp", "dp"),
            P("dp", "mp"),
            P("dp", "mp"),
            P("mp", "dp"),
            P("dp", "mp"),
            P("dp", "mp"),
            P("mp", "dp"),
            P("dp", "mp"),
            P("dp", "mp"),
            P("mp", "dp"),
            P("dp", "mp"),
            P("dp", "mp"),
            P("mp", "dp"),
            P("dp", "mp"),
            P("dp", "mp"),
            P("mp", "dp"),
            P("dp", "mp"),
            P("dp", "mp"),
            P("mp", "dp"),
            P("dp", "mp"),
            P("dp", "mp"),
            P("mp", "dp"),
        ),
        check_vma=False,
    )
```

```python
from functools import partial

import jax
import jax.numpy as jnp
from jax import lax
from jax.experimental import pallas as pl
from jax.experimental.pallas import tpu as pltpu
from jax.sharding import PartitionSpec as P

HEADS = 12
HEAD_DIM = 64


beta_one = 0.9
beta_two = 0.999
peak_rate = 1.0
warm_steps = 4.0
total_steps = 100.0
decay_rate = 0.01
adam_eps = 1e-08
norm_eps = 1e-05


def layer_norm(row_data, gain_row, shift_row):
    centered = row_data - jnp.mean(row_data, axis=-1, keepdims=True)
    spread = jnp.mean(centered * centered, axis=-1, keepdims=True)
    return centered * lax.rsqrt(spread + norm_eps) * gain_row + shift_row


def alibi_table(head_count, seq_len):
    slopes = jnp.exp2(-8.0 * jnp.arange(1, head_count + 1, dtype=jnp.float32) / head_count)
    places = jnp.arange(seq_len, dtype=jnp.float32)
    return slopes[:, None, None] * jnp.abs(places[:, None] - places[None, :])


def dot_nn(left_op, right_op):
    return lax.dot_general(
        left_op, right_op, (((1,), (0,)), ((), ())), preferred_element_type=jnp.float32
    )


def dot_nt(left_op, right_op):
    return lax.dot_general(
        left_op, right_op, (((1,), (1,)), ((), ())), preferred_element_type=jnp.float32
    )


def dot_tn(left_op, right_op):
    return lax.dot_general(
        left_op, right_op, (((0,), (0,)), ((), ())), preferred_element_type=jnp.float32
    )


def flip(block, axis, bits):
    size = lax.axis_size(axis)
    return lax.ppermute(block, axis, [(i, i ^ bits) for i in range(size)])


def flip_core(block):
    return flip(block, "mp", 1)


def flip_x(block):
    return flip(block, "mp", 2)


def flip_y(block):
    return flip(block, "dp", 1)


def norm_stats(row_data):
    centered = row_data - jnp.mean(row_data, axis=-1, keepdims=True)
    spread = jnp.mean(centered * centered, axis=-1, keepdims=True)
    inverse = lax.rsqrt(spread + norm_eps)
    return centered * inverse, inverse


def z_groups():
    size = lax.axis_size("dp")
    return [list(range(low, size, 2)) for low in range(2)]


def pass_on(*refs):
    pass


def after(block, *others):
    return pl.pallas_call(
        pass_on,
        out_shape=jax.ShapeDtypeStruct(block.shape, block.dtype),
        in_specs=[pl.BlockSpec(memory_space=pl.ANY)] * (1 + len(others)),
        out_specs=pl.BlockSpec(memory_space=pl.ANY),
        input_output_aliases={0: 0},
        cost_estimate=pl.CostEstimate(flops=0, bytes_accessed=0, transcendentals=0),
    )(block, *others)


def is_small():
    return lax.axis_size("dp") == 8


def gather_z(block):
    far = flip(block, "dp", 4)
    return [block, far, flip(block, "dp", 2), flip(far, "dp", 2)]


def piece_rows(features):
    at = jnp.arange(8, dtype=jnp.int32)
    if is_small():
        along_z = ((at & 1) << 1) + ((at >> 1) & 1)
        at = (2 * along_z + (at >> 2)) ^ lax.axis_index("dp")
    return at * (features // 8)


def gather_whole(block):
    whole = lax.all_gather(block, "dp", axis=1, tiled=True)
    lots, features, columns = whole.shape
    whole = whole.reshape(lots, 8, features // 8, columns).transpose(1, 0, 2, 3)
    return [whole], [flip_x(whole)]


def add_low(*parts):
    return sum(part.astype(jnp.float32) for part in parts).astype(jnp.bfloat16)


def sum_dp(whole):
    return lax.psum_scatter(whole.astype(jnp.float32), "dp", scatter_dimension=0, tiled=True)


def from_pieces(*parts):
    whole = jnp.concatenate(parts, axis=0)
    return sum_dp(whole.reshape(-1, whole.shape[-1]))


MIB = 1024 * 1024
ANYWHERE = pl.BlockSpec(memory_space=pl.ANY)
IN_VMEM = pl.BlockSpec(memory_space=pltpu.VMEM)
IN_SMEM = pl.BlockSpec(memory_space=pltpu.SMEM)


def kernel_call(body, outs, specs, scratch, limit, flops=0):
    return pl.pallas_call(
        body,
        out_shape=outs,
        in_specs=specs,
        out_specs=[IN_VMEM] * len(outs),
        scratch_shapes=scratch,
        compiler_params=pltpu.CompilerParams(vmem_limit_bytes=limit * MIB),
        cost_estimate=pl.CostEstimate(flops=flops, bytes_accessed=0, transcendentals=0),
    )


def like(shape, dtype):
    return jax.ShapeDtypeStruct(shape, dtype)


def with_lot(groups, lot):
    return [(group, (i, lot)) for group in groups for i in range(group.shape[0])]


def load_pieces(pieces, rows, total, sems):
    copies = []
    count = total.shape[0] // 8
    for k, (group, at) in enumerate(pieces):
        to = total.at[pl.ds(pl.multiple_of(rows[k], 32), count), :]
        copies.append(pltpu.make_async_copy(group.at[(*at, pl.ds(0, count))], to, sems.at[k]))
        copies[-1].start()
    return copies


EXTRA = 16


def load_extras(groups, spots, total, sems):
    copies = []
    for group in groups:
        for i in range(group.shape[0]):
            k = len(copies)
            source = group.at[i, 0, pl.ds(group.shape[2] - EXTRA, EXTRA), :]
            copies.append(pltpu.make_async_copy(source, total.at[spots[k]], sems.at[k]))
            copies[-1].start()
    return copies


def split_low(block):
    parts = []
    for _ in range(3):
        part = lax.reduce_precision(block, 8, 7)
        parts.append(jnp.pad(part.astype(jnp.bfloat16), ((0, EXTRA - 1), (0, 128 - block.shape[1]))))
        block = block - part
    return jnp.pad(jnp.concatenate(parts, axis=1), ((0, 0), (0, 384)))


def wait_all(copies):
    for copy in copies:
        copy.wait()


def gelu_parts(gated):
    below = 0.5 + 0.5 * lax.erf(gated * 0.7071067811865476)
    return gated * below, below


def lower_lanes(shape):
    return lax.broadcasted_iota(jnp.int32, shape, 1) < 64


def unpack_columns_of(blocks, attend, merge):
    for block, (column, merge_column) in enumerate(((0, 0), (640, 256), (1152, 384), (1792, 640))):
        attend[:, column : column + 512] = blocks[block, :, :512]
        merge[:, merge_column : merge_column + 128] = blocks[block, :, 512:640]
    for pair, (column, merge_column) in enumerate(((512, 128), (1664, 512))):
        even = blocks[2 * pair, :, 640:].astype(jnp.float32)
        odd = blocks[2 * pair + 1, :, 640:].astype(jnp.float32)
        lower = lower_lanes(even.shape)
        attend[:, column : column + 128] = jnp.where(lower, even, odd).astype(jnp.bfloat16)
        mixed_up = pltpu.roll(jnp.where(lower, odd, even), 64, 1)
        merge[:, merge_column : merge_column + 128] = mixed_up.astype(jnp.bfloat16)


def first_kernel(counts, extra, places, rows, spots, start, norms_given, positions, *refs):
    low = jnp.bfloat16
    groups = []
    for count in counts:
        groups.append(refs[:count])
        refs = refs[count:]
    attend, merge, mixed, normed, *narrow, slot_sum, slot_attended, slot_narrow, norms = refs[:10]
    blocks, attended, scores, extras, sems = refs[10:]
    copies = []
    for at, group in enumerate(groups):
        copies += load_pieces(with_lot(group, 0), rows, blocks.at[places[at]], sems.at[0, at])
        if extra:
            copies += load_extras(group, spots, extras.at[places[at]], sems.at[1, at])
    wait_all(copies)
    if extra:
        for block in range(4):
            whole = jnp.zeros((8, norms.shape[1]), jnp.float32)
            for spot in range(8):
                parts = extras[block, spot].astype(jnp.float32)[:8, :]
                value = parts[:, :128] + parts[:, 128:256] + parts[:, 256:384]
                value = jnp.concatenate([value, jnp.zeros((8, norms.shape[1] - 128), jnp.float32)], axis=1)
                whole = whole + (pltpu.roll(value, spot * (norms.shape[1] // 8), 1) if spot else value)
            norms[block : block + 1, :] = whole[:1, :]
    else:
        norms[...] = norms_given[...]
    unpack_columns_of(blocks, attend, merge)
    width = merge.shape[0]
    length = 128
    slots = 32
    scale = HEAD_DIM ** (-0.5)
    for column in range(0, 3 * width, 256):
        cut = slice(column, column + 256)
        mixed[:, cut] = dot_nn(start[...], attend[:, cut]).astype(low)
    shape = (length, length)
    apart = jnp.abs(
        lax.broadcasted_iota(jnp.int32, shape, 0) - lax.broadcasted_iota(jnp.int32, shape, 1)
    ).astype(jnp.float32)
    lower = lower_lanes(shape)

    def step(target, first, seq, carry):
        at = pl.ds(pl.multiple_of(seq * length, length), length)
        to = pl.ds(pl.multiple_of(seq * slots, slots), slots)
        for pair in range(HEADS // 2):
            column = 2 * HEAD_DIM * pair
            queries = mixed[at, column : column + 128]
            keys = mixed[at, width + column : width + column + 128]
            zero = jnp.zeros_like(queries)
            for half in range(2):
                own = jnp.where(lower, queries, zero) if half == 0 else jnp.where(lower, zero, queries)
                head = 2 * pair + half
                scores[head] = dot_nt(own, keys) * scale - apart * slopes_of(head)
        raised = scores[...]
        raised = jnp.exp(raised - jnp.max(raised, axis=-1, keepdims=True))
        scores[...] = raised / jnp.sum(raised, axis=-1, keepdims=True)
        for pair in range(HEADS // 2):
            column = 2 * HEAD_DIM * pair
            values = mixed[at, 2 * width + column : 2 * width + column + 128]
            heads = [dot_nn(scores[2 * pair + half].astype(low), values) for half in range(2)]
            attended[at, column : column + 128] = jnp.where(lower, heads[0], heads[1]).astype(low)
        total = start[at, :].astype(jnp.float32) + dot_nn(attended[at, :], merge[...])
        xhat, _ = norm_stats(total)
        rows = xhat * norms[0:1, :] + norms[1:2, :]
        normed[at, :] = rows
        target[pl.ds(pl.multiple_of((seq - first) * length, length), length), :] = rows.astype(low)
        selector = one_hot(positions[to, :], length)
        slot_sum[to, :] = select_exact(selector, total)
        slot_attended[to, :] = dot_nn(selector, attended[at, :]).astype(low)
        slot_narrow[to, :] = dot_nn(selector, rows.astype(low)).astype(low)
        return carry

    seqs = start.shape[0] // length // 2
    lax.fori_loop(0, seqs, partial(step, narrow[0], 0), 0, unroll=True)
    lax.fori_loop(seqs, 2 * seqs, partial(step, narrow[1], seqs), 0, unroll=True)


def first_part(extra, places, rows, spots, start, norms, positions, groups):
    count, width = start.shape
    slot_rows = positions.shape[0]
    low = jnp.bfloat16
    return kernel_call(
        partial(first_kernel, [len(group) for group in groups], extra),
        [
            like((width, 3 * width), low),
            like((width, width), low),
            like((count, 3 * width), low),
            like((count, width), jnp.float32),
            like((count // 2, width), low),
            like((count // 2, width), low),
            like((slot_rows, width), jnp.float32),
            like((slot_rows, width), low),
            like((slot_rows, width), low),
            like((4, width), jnp.float32),
        ],
        [IN_SMEM] * 3 + [IN_VMEM] * 3 + [ANYWHERE] * sum(map(len, groups)),
        [
            pltpu.VMEM((4, width, width), low),
            pltpu.VMEM((count, width), low),
            pltpu.VMEM((HEADS, 128, 128), jnp.float32),
            pltpu.VMEM((4, 8, EXTRA, width), low),
            pltpu.SemaphoreType.DMA((2, 4, 8)),
        ], 30)(places, rows, spots, start, norms, positions, *sum(groups, []))


def pack_columns(attend, merge, core_at):
    even = jnp.concatenate(
        [attend[:, :512], merge[:, :128], attend[:, 512:], merge[:, 128:]], axis=1
    )
    odd = jnp.concatenate([attend[:, 64:], merge[:, 64:], merge[:, :64], attend[:, :64]], axis=1)
    return jnp.where(core_at == 0, even, odd)


def unpack_columns(packed, core_at):
    even = jnp.concatenate([packed[:, :512], packed[:, 640:704]], axis=1)
    odd = jnp.concatenate([packed[:, 704:], packed[:, :512]], axis=1)
    even_merge = jnp.concatenate([packed[:, 512:640], packed[:, 704:]], axis=1)
    odd_merge = jnp.concatenate([packed[:, 640:704], packed[:, 512:640]], axis=1)
    return jnp.where(core_at == 0, even, odd), jnp.where(core_at == 0, even_merge, odd_merge)


def front_kernel(count, rows, *refs):
    sources, pieces = refs[:4], refs[4 : 4 + count]
    hidden, gates, values, sems = refs[-4:]
    copies = load_pieces(with_lot(pieces, 0), rows, gates, sems.at[0])
    copies += load_pieces(with_lot(pieces, 1), rows, values, sems.at[1])
    quarter = sources[0].shape[0]
    wait_all(copies)
    for part, source in enumerate(sources):
        at = slice(part * quarter, (part + 1) * quarter)
        block = source[...]
        for column in range(0, gates.shape[1], 256):
            cut = slice(column, column + 256)
            gated = dot_nn(block, gates[:, cut])
            valued = dot_nn(block, values[:, cut])
            hidden[at, cut] = (gelu_parts(gated)[0] * valued).astype(jnp.bfloat16)


def ffn_front(rows, sources, pieces, *earlier):
    quarter, width = sources[0].shape
    return kernel_call(
        partial(front_kernel, len(pieces)),
        [like((4 * quarter, width), jnp.bfloat16)],
        [IN_SMEM] + [IN_VMEM] * 4 + [ANYWHERE] * (len(pieces) + len(earlier)),
        [pltpu.VMEM((width, width), jnp.bfloat16)] * 2 + [pltpu.SemaphoreType.DMA((2, 8))],
        14,
        flops=2 * 4 * quarter * width * 2 * width,
    )(rows, *sources, *pieces, *earlier)[0]


def down_kernel(lots, rows, hidden_near, hidden_far, *refs):
    split, end = len(lots[0]), len(lots[0]) + len(lots[1])
    mine, other, downs, sems = refs[end:]
    copies = load_pieces(zip(refs[:split], lots[0]), rows, downs.at[0], sems.at[0])
    copies += load_pieces(zip(refs[split:end], lots[1]), rows, downs.at[1], sems.at[1])
    wait_all(copies)
    half = mine.shape[0]
    for part, target in ((1, other), (0, mine)):

        def step(tile, carry, part=part, target=target):
            at = pl.ds(pl.multiple_of(part * half + tile * 256, 256), 256)
            to = pl.ds(pl.multiple_of(tile * 256, 256), 256)
            target[to, :] = dot_nt(hidden_near[at, :], downs[0]) + dot_nt(hidden_far[at, :], downs[1])
            return carry

        lax.fori_loop(0, half // 256, step, 0)


def ffn_down(rows, hidden_near, hidden_far, near, far):
    both, width = hidden_near.shape
    return kernel_call(
        partial(down_kernel, [[lot for _, lot in group] for group in (near, far)]),
        [like((both // 2, width), jnp.float32)] * 2,
        [IN_SMEM, IN_VMEM, IN_VMEM] + [ANYWHERE] * (len(near) + len(far)),
        [pltpu.VMEM((2, width, width), jnp.bfloat16), pltpu.SemaphoreType.DMA((2, 8))], 16)(rows, hidden_near, hidden_far, *[group for group, _ in near + far])


def select_exact(selector, block):
    first = block.astype(jnp.bfloat16)
    rest = block - first.astype(jnp.float32)
    second = rest.astype(jnp.bfloat16)
    third = (rest - second.astype(jnp.float32)).astype(jnp.bfloat16)
    return dot_nn(selector, first) + dot_nn(selector, second) + dot_nn(selector, third)


def norm_back(xhat, inverse, gain_row, incoming):
    scaled = incoming * gain_row
    inner = jnp.mean(scaled * xhat, axis=-1, keepdims=True)
    back = inverse * (scaled - jnp.mean(scaled, axis=-1, keepdims=True) - xhat * inner)
    gain_back = jnp.sum(incoming * xhat, axis=0, keepdims=True)
    return back, gain_back, jnp.sum(incoming, axis=0, keepdims=True)


def one_hot(positions, length):
    shape = (positions.shape[0], length)
    return (positions == lax.broadcasted_iota(jnp.int32, shape, 1)).astype(jnp.bfloat16)


def second_kernel(
    normed, part, got, norms, positions, live, cotangent, output, pulled, back, norm_grads
):
    slots = cotangent.shape[1]
    length = normed.shape[0] // cotangent.shape[0]
    norm_grads[...] = jnp.zeros_like(norm_grads)

    def step(seq, carry):
        at = pl.ds(pl.multiple_of(seq * length, length), length)
        to = pl.ds(pl.multiple_of(seq * slots, slots), slots)
        total = normed[at, :] + part[at, :] + got[at, :]
        xhat, _ = norm_stats(total)
        output[at, :] = (xhat * norms[2:3, :] + norms[3:4, :]).astype(jnp.bfloat16)
        selector = one_hot(positions[to, :], length)
        xhat, inverse = norm_stats(select_exact(selector, total))
        incoming = jnp.where(live[to, :] > 0, cotangent[seq].astype(jnp.float32), 0.0)
        slot_back, gain_back, shift_back = norm_back(xhat, inverse, norms[2:3, :], incoming)
        back[to, :] = slot_back
        pulled[to, :] = slot_back.astype(jnp.bfloat16)
        norm_grads[0:1, :] += gain_back
        norm_grads[1:2, :] += shift_back
        return carry

    lax.fori_loop(0, cotangent.shape[0], step, 0, unroll=True)


def second_norm(normed, part, got, norms, positions, live, cotangent):
    count, width = normed.shape
    slot_rows = positions.shape[0]
    return kernel_call(
        second_kernel,
        [
            like((count, width), jnp.bfloat16),
            like((slot_rows, width), jnp.bfloat16),
            like((slot_rows, width), jnp.float32),
            like((2, width), jnp.float32),
        ],
        [IN_VMEM] * 7,
        [], 14)(normed, part, got, norms, positions, live, cotangent)


def back_kernel(count, lots, rows, *refs):
    pulls, narrows = refs[0:4], refs[4:8]
    wide, deep = refs[8 : 8 + count[0]], refs[8 + count[0] : 8 + count[0] + count[1]]
    keep, send, pull_rows, work_rows, gate_back, value_back, hidden = refs[
        8 + count[0] + count[1] : -4
    ]
    gates, values, downs, sems = refs[-4:]
    copies = load_pieces(with_lot(wide, 0), rows, gates, sems.at[0])
    copies += load_pieces(with_lot(wide, 1), rows, values, sems.at[1])
    copies += load_pieces(zip(deep, lots), rows, downs, sems.at[2])
    size = pulls[0].shape[0]
    for k in range(4):
        pull_rows[k * size : (k + 1) * size, :] = pulls[k][...]
        work_rows[k * size : (k + 1) * size, :] = narrows[k][...]
    wait_all(copies)
    for column in range(0, gates.shape[1], 256):
        cut = slice(column, column + 256)
        gated = dot_nn(work_rows[...], gates[:, cut])
        valued = dot_nn(work_rows[...], values[:, cut])
        hidden_back = dot_nn(pull_rows[...], downs[:, cut])
        gelu, below = gelu_parts(gated)
        slope = below + gated * (0.3989422804014327 * jnp.exp(-0.5 * gated * gated))
        hidden[:, cut] = (gelu * valued).astype(jnp.bfloat16)
        gate_back[:, cut] = (hidden_back * valued * slope).astype(jnp.bfloat16)
        value_back[:, cut] = (hidden_back * gelu).astype(jnp.bfloat16)
    for column in range(0, gates.shape[0], 256):
        cut = slice(column, column + 256)
        total = dot_nt(gate_back[...], gates[cut, :]) + dot_nt(value_back[...], values[cut, :])
        for k, target in enumerate((keep, keep, send, send)):
            target[k % 2, :, cut] = total[k * size : (k + 1) * size]


def ffn_back(rows, pulls, narrows, wide, deep):
    size, width = pulls[0].shape
    low = jnp.bfloat16
    return kernel_call(
        partial(back_kernel, (len(wide), len(deep)), [lot for _, lot in deep]),
        [like((2, size, width), jnp.float32)] * 2 + [like((4 * size, width), low)] * 5,
        [IN_SMEM] + [IN_VMEM] * 8 + [ANYWHERE] * (len(wide) + len(deep)),
        [pltpu.VMEM((width, width), low)] * 3 + [pltpu.SemaphoreType.DMA((3, 8))], 22)(rows, *pulls, *narrows, *wide, *[group for group, _ in deep])


def store_pieces(total, rows, mine, other):
    count = total.shape[0] // 8
    for k in range(8):
        at = pl.ds(pl.multiple_of(rows[k], 32), count)
        to = mine if k < 4 else other
        to[k % 4, :count, :] = total[at, :]


def grads_kernel(lots, rows, *refs):
    factors, refs = refs[: 2 * lots], refs[-3 - lots :]
    mine, other, total, turned = refs[0], refs[1], refs[2], refs[3:]
    for lot in range(lots):
        turned[lot][...] = factors[2 * lot][...].T
    for lot in range(lots):
        for column in range(0, total.shape[1], 256):
            cut = slice(column, column + 256)
            product = dot_nn(turned[lot][...], factors[2 * lot + 1][:, cut])
            total[:, cut] = product.astype(jnp.bfloat16)
        store_pieces(total, rows, mine.at[:, lot], other.at[:, lot])


def ffn_grads(rows, factors, *earlier):
    size, width = factors[0].shape
    lots = len(factors) // 2
    low = jnp.bfloat16
    return kernel_call(
        partial(grads_kernel, lots),
        [like((4, lots, width // 8, width), low)] * 2,
        [IN_SMEM] + [IN_VMEM] * len(factors) + [ANYWHERE] * len(earlier),
        [pltpu.VMEM((width, width), low)] + [pltpu.VMEM((width, size), low)] * lots, 16)(rows, *factors, *earlier)


def split_kernel(from_y, from_x, *refs):
    first, second, sems = refs[-3:]
    half = first.shape[0]
    copies = [
        pltpu.make_async_copy(from_y.at[pl.ds(0, half)], first, sems.at[0]),
        pltpu.make_async_copy(from_x.at[pl.ds(half, half)], second, sems.at[1]),
    ]
    for copy in copies:
        copy.start()
    wait_all(copies)


def split_halves(from_y, from_x, *earlier):
    half = like((from_y.shape[0] // 2,) + from_y.shape[1:], from_y.dtype)
    return kernel_call(
        split_kernel,
        [half, half],
        [ANYWHERE] * (2 + len(earlier)),
        [pltpu.SemaphoreType.DMA((2,))], 6)(from_y, from_x, *earlier)


def cast_kernel(first, second, _, both):
    both[0] = first[...].astype(jnp.bfloat16)
    both[1] = second[...].astype(jnp.bfloat16)


def cast_wide(first, second, earlier):
    return kernel_call(
        cast_kernel,
        [like((2,) + first.shape, jnp.bfloat16)],
        [IN_VMEM] * 2 + [ANYWHERE],
        [], 4)(first, second, earlier)[0]


def wide_sum(*blocks):
    return sum(block.astype(jnp.float32) for block in blocks)


def total_of(*blocks):
    return wide_sum(*blocks)


def corner_kernel(near, got, *refs):
    first, second = refs[-2:]
    for k in range(4):
        target = first if k < 2 else second
        target[k % 2] = wide_sum(near[k], got[k]).astype(jnp.bfloat16)


def corner_sum(near, got, *earlier):
    half = like((2,) + near.shape[1:], near.dtype)
    return kernel_call(
        corner_kernel, [half, half], [IN_VMEM] * 2 + [ANYWHERE] * len(earlier), [], 6)(near, got, *earlier)


def sides_kernel(near_y, got_y, near_x, got_x, corner_x, corner_y, _, to_x, to_y):
    for k in range(4):
        corner = [corner_x[k]] if k < 2 else []
        to_y[k] = wide_sum(near_y[k], got_y[k], *corner).astype(jnp.bfloat16)
        corner = [corner_y[k - 2]] if k >= 2 else []
        to_x[k] = wide_sum(near_x[k], got_x[k], *corner).astype(jnp.bfloat16)


def sides_sum(near, got, corner_x, corner_y, earlier):
    side = like(near[1].shape, near[1].dtype)
    return kernel_call(sides_kernel, [side, side], [IN_VMEM] * 6 + [ANYWHERE], [], 10)(
        near[1], got[1], near[2], got[2], corner_x, corner_y, earlier
    )


def chip_kernel(near, got, got_x, got_y, _, mine, far, side, last):
    for k, target in enumerate((mine, far, side, last)):
        total = wide_sum(near[k], got[k], got_x[k], got_y[k])
        target[...] = total.astype(target.dtype)


def chip_sum(near, got, got_x, got_y, earlier):
    piece = near.shape[1:]
    mine, far, side, last = kernel_call(
        chip_kernel,
        [like(piece, jnp.float32)] + [like(piece, near.dtype)] * 3,
        [IN_VMEM] * 4 + [ANYWHERE],
        [], 8)(near, got, got_x, got_y, earlier)
    return mine, side, far, last


def halves_kernel(mine, got, *refs):
    keep, send = refs[-2:]
    half = keep.shape[0]
    for k in range(half):
        keep[k] = wide_sum(mine[k], got[k]).astype(keep.dtype)
        send[k] = wide_sum(mine[half + k], got[half + k]).astype(send.dtype)


def halves_sum(mine, got, *earlier):
    half = like((mine.shape[0] // 2,) + mine.shape[1:], mine.dtype)
    return kernel_call(
        halves_kernel, [half, half], [IN_VMEM] * 2 + [ANYWHERE] * len(earlier), [], 8)(mine, got, *earlier)


def row_gradient_kernel(placed, mixed_back, attend, _, output):
    for column in range(0, placed.shape[1], 256):
        cut = slice(column, column + 256)
        output[:, cut] = placed[:, cut] + dot_nt(mixed_back[...], attend[cut, :])


def row_gradient(placed, mixed_back, attend, earlier):
    count, width = placed.shape
    return kernel_call(
        row_gradient_kernel,
        [like(placed.shape, placed.dtype)],
        [IN_VMEM] * 3 + [ANYWHERE],
        [], 14)(placed, mixed_back, attend, earlier)[0]


def slopes_of(head):
    return 2.0 ** (-8.0 * (head + 1) / HEADS)


def attend_kernel(
    extra,
    rows,
    columns,
    spots,
    second_grads,
    keep,
    got,
    second_back,
    slot_sum,
    norms,
    merge,
    mixed,
    slot_attended,
    start,
    positions,
    _,
    placed,
    mixed_back,
    norm_grads,
    *refs,
):
    near, far = refs[0:4], refs[4:8]
    merge_grad, total, branch, attended_back, first_back, turned, extras = refs[8:]
    width = norms.shape[1]
    slots = 32
    length = 128
    low = jnp.bfloat16
    scale = HEAD_DIM ** (-0.5)
    xhat, inverse = norm_stats(slot_sum[...])
    incoming = keep[...] + got[...].astype(jnp.float32) + second_back[...]
    slot_back, gain_back, shift_back = norm_back(xhat, inverse, norms[0:1, :], incoming)
    norm_grads[0:1, :] = gain_back
    norm_grads[1:2, :] = shift_back
    if extra:
        both = [gain_back, shift_back, second_grads[0:1, :], second_grads[1:2, :]]
        zero_rows = jnp.zeros((EXTRA - 1, width), jnp.float32)
        for block in range(4):
            whole = jnp.concatenate([both[block], zero_rows], axis=0)
            for spot in range(8):
                turn = (8 - spot) % 8 * (width // 8)
                extras[block, spot] = (pltpu.roll(whole, turn, 1) if turn else whole).astype(low)
    first_back[...] = slot_back
    branch[...] = slot_back.astype(low)
    attended_back[...] = dot_nt(branch[...], merge[...]).astype(low)
    merge_grad[...] = dot_tn(slot_attended[...], branch[...])
    lane_head = lax.broadcasted_iota(jnp.int32, (slots, width), 1) // HEAD_DIM

    def apart_heads(block):
        zero = jnp.zeros_like(block)
        return jnp.concatenate(
            [jnp.where(lane_head == head, block, zero) for head in range(HEADS)], axis=0
        )

    def join_heads(block):
        total = jnp.zeros((slots, width), jnp.float32)
        for head in range(HEADS):
            total = jnp.where(lane_head == head, block[head * slots : (head + 1) * slots], total)
        return total

    def step(seq, carry):
        at = pl.ds(pl.multiple_of(seq * length, length), length)
        to = pl.ds(pl.multiple_of(seq * slots, slots), slots)
        spots = positions[to, :]
        selector = one_hot(spots, length)
        apart = jnp.abs(
            spots - lax.broadcasted_iota(jnp.int32, (slots, length), 1)
        ).astype(jnp.float32)
        keys = mixed[at, width : 2 * width]
        values = mixed[at, 2 * width :]
        queries = apart_heads(dot_nn(selector, mixed[at, :width])).astype(low)
        heads_back = apart_heads(attended_back[to, :].astype(jnp.float32)).astype(low)
        bias = jnp.concatenate([apart * slopes_of(head) for head in range(HEADS)], axis=0)
        scores = dot_nt(queries, keys) * scale - bias
        exp_scores = jnp.exp(scores - jnp.max(scores, axis=-1, keepdims=True))
        probs = exp_scores / jnp.sum(exp_scores, axis=-1, keepdims=True)
        probs_back = dot_nt(heads_back, values)
        inner = jnp.sum(probs * probs_back, axis=-1, keepdims=True)
        scores_back = (probs * (probs_back - inner)).astype(low)
        queries_back = (join_heads(dot_nn(scores_back, keys)) * scale).astype(low)
        mixed_back[at, :width] = dot_tn(selector, queries_back).astype(low)
        mixed_back[at, width : 2 * width] = (dot_tn(scores_back, queries) * scale).astype(low)
        mixed_back[at, 2 * width :] = dot_tn(probs.astype(low), heads_back).astype(low)
        spread = (spots == lax.broadcasted_iota(jnp.int32, (slots, length), 1)).astype(jnp.float32)
        placed[at, :] = select_exact(jnp.transpose(spread).astype(low), first_back[to, :])
        return carry

    lax.fori_loop(0, mixed.shape[0] // length, step, 0, unroll=True)
    turned[...] = start[...].T
    for core, target in ((1, far), (0, near)):
        for k in range(2):
            base = 6 * (2 * core + k)
            for part in range(2):
                column = pl.ds(pl.multiple_of(columns[base] + 256 * part, 128), 256)
                product = dot_nn(turned[...], mixed_back[:, column])
                total[:, 256 * part : 256 * part + 256] = product.astype(low)
            column = pl.ds(pl.multiple_of(columns[base + 1], 128), 128)
            total[:, 512:640] = merge_grad[:, column].astype(low)
            column = pl.ds(pl.multiple_of(columns[base + 2], 128), 128)
            single = dot_nn(turned[...], mixed_back[:, column])
            column = pl.ds(pl.multiple_of(columns[base + 3], 128), 128)
            merged = pltpu.roll(merge_grad[:, column], 64, 1)
            attend_lane = lower_lanes(single.shape) == (columns[base + 4] == 0)
            total[:, 640:] = jnp.where(attend_lane, single, merged).astype(low)
            sides = target[2 * k : 2 * k + 2]
            store_pieces(total, rows, *sides)
            if extra:
                for j in range(8):
                    sides[j // 4][j % 4, width // 8 :, :] = extras[columns[base + 5], spots[j]]


def attend_back(extra, rows, columns, spots, second_grads, *blocks):
    start, mixed = blocks[8], blocks[6]
    count, width = start.shape
    slot_rows = blocks[0].shape[0]
    low = jnp.bfloat16
    return kernel_call(
        partial(attend_kernel, extra),
        [
            like((count, width), jnp.float32),
            like(mixed.shape, low),
            like((2, width), jnp.float32),
        ]
        + [like((4, width // 8 + (EXTRA if extra else 0), width), low)] * 8,
        [IN_SMEM] * 3 + [IN_VMEM] * 11 + [ANYWHERE],
        [
            pltpu.VMEM((width, width), jnp.float32),
            pltpu.VMEM((width, width), low),
            pltpu.VMEM((slot_rows, width), low),
            pltpu.VMEM((slot_rows, width), low),
            pltpu.VMEM((slot_rows, width), jnp.float32),
            pltpu.VMEM((width, count), low),
            pltpu.VMEM((4, 8, EXTRA, width), low),
        ], 32)(rows, columns, spots, second_grads, *blocks)


def adamw_step(master, first, second, gradient, step_value, decay):
    step_rate = peak_rate * jnp.minimum(
        step_value / warm_steps, (total_steps - step_value) / (total_steps - warm_steps)
    )
    fix_one = 1.0 - jnp.power(jnp.float32(beta_one), step_value)
    fix_two = 1.0 - jnp.power(jnp.float32(beta_two), step_value)
    moment = beta_one * first + (1.0 - beta_one) * gradient
    squares = beta_two * second + (1.0 - beta_two) * gradient * gradient
    updated = master - step_rate * (
        moment / fix_one / (jnp.sqrt(squares / fix_two) + adam_eps) + decay * master
    )
    return (moment, squares, updated)


def shards(
    hidden_rows,
    token_table,
    masked_positions,
    masked_counts,
    replace_rows,
    masked_cotangent,
    step_number,
    attend_master,
    merge_master,
    norms_master,
    gate_master,
    value_master,
    down_master,
    first_attend,
    first_merge,
    first_norms,
    first_gate,
    first_value,
    first_down,
    second_attend,
    second_merge,
    second_norms,
    second_gate,
    second_value,
    second_down,
):
    local_seqs, slot_count = masked_positions.shape
    local_rows, model_width = hidden_rows.shape
    length = local_rows // local_seqs
    slot_rows = local_seqs * slot_count
    dp_size = lax.axis_size("dp")
    core_at = lax.axis_index("mp") & 1
    x_at = lax.axis_index("mp") >> 1
    low = jnp.bfloat16
    rows = piece_rows(model_width)

    packed = pack_columns(attend_master.astype(low), merge_master.astype(low), core_at)[None]
    small = is_small()
    deep = down_master.astype(low).T[None]

    order = [(core, k) for core in range(2) for k in range(2)]
    places = [2 * (x_at ^ k) + (core_at ^ core) for core, k in order]
    table = jnp.array(
        [
            [0, 0, 512, 128, 0, 0],
            [640, 256, 512, 128, 1, 1],
            [1152, 384, 1664, 512, 0, 2],
            [1792, 640, 1664, 512, 1, 3],
        ],
        jnp.int32,
    )
    columns = jnp.concatenate([table[place] for place in places])
    places = jnp.stack(places).astype(jnp.int32)
    spots = piece_rows(8)
    if small:
        packed = jnp.concatenate([packed, split_low(norms_master)[None]], axis=1)
        packed_z = [packed] + [flip(packed, "dp", 2 * k) for k in (2, 1, 3)]
        wide = cast_wide(gate_master, value_master, packed_z[2])

        deep = after(deep, packed_z[2])
        deep_y, deep_x = flip_y(deep), flip_x(deep)
        replace_rows = after(replace_rows, deep_y)

    live_slots = jnp.arange(slot_count, dtype=jnp.int32)[None, :] < masked_counts[:, None]
    at_slot = masked_positions[:, :, None] == jnp.arange(length, dtype=jnp.int32)[None, None, :]
    place_bool = at_slot & live_slots[:, :, None]
    chosen = jnp.take(token_table, replace_rows.reshape(-1), axis=0).reshape(
        local_seqs, slot_count, model_width
    )
    swapped = jnp.einsum(
        "sjt,sjd->std", place_bool.astype(low), chosen, preferred_element_type=jnp.float32
    ).astype(low)
    replaced = jnp.any(place_bool, axis=1)[:, :, None]
    start_rows = jnp.where(
        replaced, swapped, hidden_rows.reshape(local_seqs, length, model_width)
    ).reshape(local_rows, model_width)
    positions = masked_positions.reshape(slot_rows, 1)
    live = live_slots.astype(jnp.float32).reshape(slot_rows, 1)
    indices = [rows, places, columns, spots, positions, live]
    if small:
        deep_parts = jnp.concatenate([deep, deep_y, deep_x, flip_x(deep_y)])
        packed_z[0] = after(packed_z[0], wide, deep_parts, *indices)
        wide_z = gather_z(after(wide, packed_z[1], packed_z[3]))
        packed_z = jnp.stack(packed_z)
        packed_y, packed_x = flip_y(packed_z), flip_x(packed_z)
        first_half, second_half = split_halves(packed_y, packed_x, wide_z[1], wide_z[2], start_rows)
        packed_near = [packed_z, packed_y]
        packed_far = [packed_x, flip_x(first_half), flip_y(second_half)]
        wide_z[0] = after(wide_z[0], *packed_far[1:])
        deep_z = gather_z(after(deep_parts, *wide_z[1:])[None])
        wide_z = jnp.stack(wide_z)
        wide_y, wide_x = flip_y(wide_z), flip_x(wide_z)
        norms = jnp.zeros((4, model_width), jnp.float32)
    else:
        packed_near, packed_far = gather_whole(packed)
        norms = lax.all_gather(norms_master, "dp", axis=1, tiled=True)
        norms = lax.all_gather(norms, "mp", axis=0, tiled=True)

    packed_groups = [packed_near, packed_far]
    packed_groups += [[flip_core(part) for part in group] for group in packed_groups]
    (
        attend_full,
        merge_full,
        mixed,
        normed,
        narrow,
        narrow_end,
        slot_sum,
        slot_attended,
        slot_narrow,
        norms,
    ) = first_part(
        small,
        places,
        rows,
        spots,
        start_rows,
        norms,
        positions,
        packed_groups,
    )
    if small:
        first_half, second_half = split_halves(wide_y, wide_x, narrow, deep_z[2])
        wide_near = [wide_z, wide_y]
        wide_far = [wide_x, flip_x(first_half), flip_y(second_half)]
        deep_near = [(part, (0, side)) for side in (0, 1) for part in deep_z]
        deep_far = [(part, (0, side)) for side in (2, 3) for part in deep_z]
    else:
        wide_near, wide_far = gather_whole(
            jnp.stack([gate_master.astype(low), value_master.astype(low)])
        )
        deep_near, deep_far = (with_lot(group, 0) for group in gather_whole(deep))

    def over_group(block):
        other_x = flip_x(block)
        return [block, other_x, flip_core(block), flip_core(other_x)]


    chip_rows = (narrow, narrow_end, flip_core(narrow), flip_core(narrow_end))
    hidden_near = ffn_front(rows, chip_rows, wide_near)
    hidden_far = ffn_front(rows, chip_rows, wide_far, hidden_near, deep_z[1] if small else rows)
    narrows = over_group(after(slot_narrow, hidden_far))
    ffn_mine, ffn_other = ffn_down(rows, hidden_near, hidden_far, deep_near, deep_far)
    layer_output, pulled, second_back, second_grads = second_norm(
        normed, ffn_mine, flip_core(ffn_other), norms, positions, live, masked_cotangent
    )

    keep, send, *factors = ffn_back(rows, over_group(pulled), narrows, wide_near, deep_near)
    pull_rows, work_rows, gate_back, value_back, slot_hidden = factors
    chip_back = keep + flip_core(send)
    pair_own, pair_far = ffn_grads(rows, (pull_rows, slot_hidden, work_rows, gate_back))
    value_own, value_far = ffn_grads(rows, (work_rows, value_back), pair_own)
    if small:
        pair_got = flip_y(pair_far)
    placed, mixed_back, first_grads, *parts = attend_back(
        small,
        rows,
        columns,
        spots,
        second_grads,
        chip_back[0],
        flip_x(chip_back[1].astype(low)),
        second_back,
        slot_sum,
        norms,
        merge_full,
        mixed,
        slot_attended,
        start_rows,
        positions,
        value_far,
    )
    near, far = parts[:4], parts[4:]
    got = [flip_core(part) for part in far]
    if small:
        value_got = flip_y(value_far)
        corner_a, corner_b = corner_sum(near[3], got[3], *got[:3])
        corner_x, corner_y = flip_x(corner_a), flip_y(corner_b)
        pair_keep, pair_send = halves_sum(pair_own, pair_got, corner_a)
        pair_back = flip(pair_send, "dp", 2)
        to_x, to_y = sides_sum(near, got, corner_x, corner_y, value_got)
        got_x, got_y = flip_x(to_x), flip_y(to_y)
        value_keep, value_send = halves_sum(value_own, value_got, to_x)
        value_back = flip(value_send, "dp", 2)
        pair_keep, pair_send = halves_sum(pair_keep, pair_back, value_send)
        pair_last = flip(pair_send[0], "dp", 4)
        input_gradient = row_gradient(placed, mixed_back, attend_full, pair_send)
        value_keep, value_send = halves_sum(value_keep, value_back, input_gradient)
        value_last = flip(value_send[0], "dp", 4)
        mine, *sent = chip_sum(near[0], got[0], got_x, got_y, input_gradient)
        pair_grad = total_of(pair_keep[0], after(pair_last, mine))
        gradient_value = total_of(value_keep[0], after(value_last, mine))[0]
        packed_grad = total_of(mine, *[flip(sent[k - 1], "dp", 2 * k) for k in (1, 2, 3)])
        gradient_down, gradient_gate = pair_grad[0].T, pair_grad[1]
    else:
        here, across_y, across_x, corner = (add_low(near[k], got[k]) for k in range(4))
        input_gradient = row_gradient(placed, mixed_back, attend_full, placed)
        gradient_down = from_pieces(pair_own[:, 0], pair_far[:, 0]).T
        gradient_gate = from_pieces(pair_own[:, 1], pair_far[:, 1])
        gradient_value = from_pieces(value_own[:, 0], value_far[:, 0])
        packed_grad = from_pieces(
            add_low(here, flip_x(across_x)), add_low(across_y, flip_x(corner))
        )
    own_rows = attend_master.shape[0]
    gradient_attend, gradient_merge = unpack_columns(packed_grad[:own_rows], core_at)
    if small:
        gradient_norms = packed_grad[own_rows : own_rows + 1, :own_rows]
    else:
        norm_parts = jnp.concatenate([first_grads, second_grads], axis=0)
        gradient_norms = lax.psum_scatter(norm_parts, "mp", scatter_dimension=0, tiled=True)
        gradient_norms = lax.psum_scatter(gradient_norms, "dp", scatter_dimension=1, tiled=True)

    step_value = step_number[0].astype(jnp.float32)
    moment_attend, squares_attend, updated_attend = adamw_step(
        attend_master, first_attend, second_attend, gradient_attend, step_value, decay_rate
    )
    moment_merge, squares_merge, updated_merge = adamw_step(
        merge_master, first_merge, second_merge, gradient_merge, step_value, decay_rate
    )
    moment_norms, squares_norms, updated_norms = adamw_step(
        norms_master, first_norms, second_norms, gradient_norms, step_value, 0.0
    )
    moment_gate, squares_gate, updated_gate = adamw_step(
        gate_master, first_gate, second_gate, gradient_gate, step_value, decay_rate
    )
    moment_value, squares_value, updated_value = adamw_step(
        value_master, first_value, second_value, gradient_value, step_value, decay_rate
    )
    moment_down, squares_down, updated_down = adamw_step(
        down_master, first_down, second_down, gradient_down, step_value, decay_rate
    )
    return (
        layer_output,
        input_gradient,
        gradient_attend,
        gradient_merge,
        gradient_norms,
        gradient_gate,
        gradient_value,
        gradient_down,
        moment_attend,
        moment_merge,
        moment_norms,
        moment_gate,
        moment_value,
        moment_down,
        squares_attend,
        squares_merge,
        squares_norms,
        squares_gate,
        squares_value,
        squares_down,
        updated_attend,
        updated_merge,
        updated_norms,
        updated_gate,
        updated_value,
        updated_down,
    )


def solution(mesh):
    return jax.shard_map(
        shards,
        mesh=mesh,
        in_specs=(
            P(("dp", "mp"), None),
            P(),
            P(("dp", "mp"), None),
            P(("dp", "mp")),
            P(("dp", "mp"), None),
            P(("dp", "mp"), None, None),
            P(),
            P("dp", "mp"),
            P("dp", "mp"),
            P("mp", "dp"),
            P("dp", "mp"),
            P("dp", "mp"),
            P("mp", "dp"),
            P("dp", "mp"),
            P("dp", "mp"),
            P("mp", "dp"),
            P("dp", "mp"),
            P("dp", "mp"),
            P("mp", "dp"),
            P("dp", "mp"),
            P("dp", "mp"),
            P("mp", "dp"),
            P("dp", "mp"),
            P("dp", "mp"),
            P("mp", "dp"),
        ),
        out_specs=(
            P(("dp", "mp"), None),
            P(("dp", "mp"), None),
            P("dp", "mp"),
            P("dp", "mp"),
            P("mp", "dp"),
            P("dp", "mp"),
            P("dp", "mp"),
            P("mp", "dp"),
            P("dp", "mp"),
            P("dp", "mp"),
            P("mp", "dp"),
            P("dp", "mp"),
            P("dp", "mp"),
            P("mp", "dp"),
            P("dp", "mp"),
            P("dp", "mp"),
            P("mp", "dp"),
            P("dp", "mp"),
            P("dp", "mp"),
            P("mp", "dp"),
            P("dp", "mp"),
            P("dp", "mp"),
            P("mp", "dp"),
            P("dp", "mp"),
            P("dp", "mp"),
            P("mp", "dp"),
        ),
        check_vma=False,
    )
```
